32 devices in a mesh: stream: 8 (over z, x), tm: 4 (over y, core).
Axes of the slice: x: 2, y: 2, z: 4, core: 2. Of those that a mesh axis runs over, the one named last changes fastest.
Arguments:
- hidden: bfloat16 [16, 512, 1024], P('stream', 'tm'), may hold values from -6 to 6
- memory: bfloat16 [16, 512, 1024], P('stream', 'tm'), may hold values from -6 to 6
- compressed: bfloat16 [16, 512, 1024], P('stream', 'tm'), may hold values from -6 to 6
- reset_flag: int32 [16], P('stream'), may hold values from 0 to 1, as said below
- boundary: int32 [16, 512], P('stream'), may hold values from 0 to 1
- query_weight: bfloat16 [1024, 1024], P('stream'), may hold values from -0.1875 to 0.1875
- key_weight: bfloat16 [1024, 1024], P('stream'), may hold values from -0.1875 to 0.1875
- value_weight: bfloat16 [1024, 1024], P('stream'), may hold values from -0.1875 to 0.1875
- output_weight: bfloat16 [1024, 1024], P('stream'), may hold values from -3 to 3
- up_weight: bfloat16 [1024, 4096], P('stream'), may hold values from -0.1875 to 0.1875
- down_weight: bfloat16 [4096, 1024], P('stream'), may hold values from -0.09375 to 0.09375
- conv_weight: bfloat16 [4, 1024, 1024], P(None, 'stream'), may hold values from -0.09375 to 0.09375
- attn_gain: bfloat16 [1024], P('stream'), may hold values from 0.099609375 to 1.8984375
- ffn_gain: bfloat16 [1024], P('stream'), may hold values from 0.099609375 to 1.8984375
- grad_out: bfloat16 [16, 512, 1024], P('stream', 'tm'), may hold values from -6 to 6
- grad_fresh: bfloat16 [16, 256, 1024], P('stream', 'tm'), may hold values from -6 to 6
Outputs:
- layer_out: bfloat16 [16, 512, 1024], P('stream', 'tm')
- fresh_memory: bfloat16 [16, 256, 1024], P('stream', 'tm')
- grad_input: float32 [16, 512, 1024], P('stream', 'tm')
- query_grad: float32 [1024, 1024], P('stream')
- key_grad: float32 [1024, 1024], P('stream')
- value_grad: float32 [1024, 1024], P('stream')
- output_grad: float32 [1024, 1024], P('stream')
- up_grad: float32 [1024, 4096], P('stream')
- down_grad: float32 [4096, 1024], P('stream')
- conv_grad: float32 [4, 1024, 1024], P(None, 'stream')
- attn_gain_grad: float32 [1024], P('stream')
- ffn_gain_grad: float32 [1024], P('stream')
The draws below stay inside these ranges and needn't reach their ends.
Inputs may be any that keep to these rules, and one draw needn't show every extreme that they name: In every aligned group of 2 streams at least one stream has reset_flag 0 and no boundary.
All inputs are finite; a program needn't handle non-finite values.
Results may differ from the reference program's by a relative error of at most 0.013.
Values may be sent and summed in bfloat16 or wider, within the bound.
A program may use at most 256 MiB of HBM per device.

```python
import jax
import jax.numpy as jnp
from jax import lax

D = 1024
HEADS = 8
HEAD_DIM = 128
FF = 4096
SEG = 512
MEM = 512
CMEM = 512
STR_DEV = 2
STREAMS = 16


def stream_plan(key):
    pick_key, having_key, marks_key, reset_key = jax.random.split(key, 4)
    groups = STREAMS // STR_DEV
    chosen = jax.random.randint(pick_key, (groups,), 0, STR_DEV)
    member = jnp.arange(STREAMS) % STR_DEV
    spared = member == jnp.repeat(chosen, STR_DEV, total_repeat_length=STREAMS)
    having = jax.random.randint(having_key, (STREAMS, 1), 0, 2)
    marks = (jax.random.randint(marks_key, (STREAMS, SEG), 0, SEG) == 0).astype(jnp.int32) * having
    resets = (jax.random.randint(reset_key, (STREAMS,), 0, 3) == 0).astype(jnp.int32)
    marks = jnp.where(spared[:, None], 0, marks).astype(jnp.int32)
    resets = jnp.where(spared, 0, resets).astype(jnp.int32)
    return (resets, marks)


def draw_reset_flag(key, part):
    planned = stream_plan(key)
    return planned[0]


def draw_boundary(key, part):
    planned = stream_plan(key)
    return planned[1]


def shard_levels(stream_key, extent, cuts, low, top_value):
    level = 1.0
    for position, shards_of in cuts:
        steps = jax.random.uniform(jax.random.fold_in(jax.random.fold_in(stream_key, 6), position), (shards_of,), jnp.float32, low / len(cuts), top_value / len(cuts))
        level = level * jnp.repeat(jnp.exp(steps), extent[position] // shards_of).reshape((-1,) + (1,) * (len(extent) - 1 - position))
    return level


def normal_values(own_key, dims, scale, most, cuts=(), dtype=jnp.bfloat16):
    loudness = shard_levels(own_key, dims, cuts, -0.22, 0.18) if cuts else 1.0
    entries = jax.random.normal(own_key, dims, jnp.float32) * scale * loudness
    return jnp.minimum(jnp.maximum(entries, -most), most).astype(dtype)


def setup_inputs(seed: int = 0) -> dict:
    keys = jax.random.split(jax.random.key(seed), 17)
    return {
        "hidden": normal_values(keys[0], (STREAMS, SEG, D), 1.0, 6.0, ((0, 8), (1, 4))),
        "memory": normal_values(keys[1], (STREAMS, MEM, D), 1.0, 6.0, ((0, 8), (1, 4))),
        "compressed": normal_values(keys[2], (STREAMS, CMEM, D), 1.0, 6.0, ((0, 8), (1, 4))),
        "reset_flag": draw_reset_flag(jax.random.fold_in(keys[16], 71), 0),
        "boundary": draw_boundary(jax.random.fold_in(keys[16], 71), 0),
        "query_weight": normal_values(keys[5], (D, D), D ** -0.5, 0.1875, ((0, 8),)),
        "key_weight": normal_values(keys[6], (D, D), D ** -0.5, 0.1875, ((0, 8),)),
        "value_weight": normal_values(keys[7], (D, D), D ** -0.5, 0.1875, ((0, 8),)),
        "output_weight": normal_values(keys[8], (D, D), (max(1, D // 256)) ** -0.5, 3.0, ((0, 8),)),
        "up_weight": normal_values(keys[9], (D, FF), D ** -0.5, 0.1875, ((0, 8),)),
        "down_weight": normal_values(keys[10], (FF, D), FF ** -0.5, 0.09375, ((0, 8),)),
        "conv_weight": normal_values(keys[11], (4, D, D), (4 * D) ** -0.5, 0.09375, ((1, 8),)),
        "attn_gain": jnp.clip(1.0 + 0.18 * jax.random.normal(keys[12], (D,), jnp.float32), 0.099609375, 1.8984375).astype(jnp.bfloat16),
        "ffn_gain": jnp.clip(1.0 + 0.18 * jax.random.normal(keys[13], (D,), jnp.float32), 0.099609375, 1.8984375).astype(jnp.bfloat16),
        "grad_out": normal_values(keys[14], (STREAMS, SEG, D), 1.0, 6.0, ((0, 8), (1, 4))),
        "grad_fresh": normal_values(keys[15], (STREAMS, MEM // 2, D), 1.0, 6.0, ((0, 8), (1, 4))),
    }


@jax.custom_vjp
def low(v):
    return lax.optimization_barrier(v.astype(jnp.bfloat16)).astype(jnp.float32)

@jax.custom_vjp
def low_back(v):
    return v

def low_keep(v):
    return (low(v), None)

def low_pass(kept, grad):
    return (grad,)

def back_keep(v):
    return (v, None)

def back_low(kept, grad):
    return (low(grad),)
low.defvjp(low_keep, low_pass)
low_back.defvjp(back_keep, back_low)

def matmul(left_side, right_side):
    return jnp.dot(left_side, right_side, precision=lax.Precision.HIGHEST)

def normalize(matrix, scaling):
    center = matrix - lax.optimization_barrier(jnp.mean(matrix, axis=-1, keepdims=True))
    spread = lax.optimization_barrier(jnp.mean(center * center, axis=-1, keepdims=True))
    return center * lax.rsqrt(spread + 1e-05) * scaling

def rotate(tensor, places):
    half_dim = tensor.shape[-1] // 2
    frequency = 10000.0 ** (-jnp.arange(half_dim).astype(jnp.float32) * 2.0 / tensor.shape[-1])
    angles = places[:, None] * frequency[None, :]
    cosine = jnp.cos(angles)[:, None, :]
    sines = jnp.sin(angles)[:, None, :]
    first_half = tensor[..., :half_dim]
    second = tensor[..., half_dim:]
    return jnp.concatenate([first_half * cosine - second * sines, first_half * sines + second * cosine], axis=-1)

def visibility(reset_one, bound_one):
    documents = jnp.cumsum(bound_one).astype(jnp.int32)
    memory_ok = (reset_one == 0) & (documents == 0)
    positions = jnp.arange(SEG).astype(jnp.int32)
    local_ok = (positions[None, :] <= positions[:, None]) & (documents[None, :] == documents[:, None])
    spread_ok = jnp.broadcast_to(memory_ok[:, None], (SEG, CMEM + MEM))
    return jnp.concatenate([spread_ok, local_ok], axis=1)

def stream_forward(hidden, memory, compressed, visible, weights):
    query_weight, key_weight, value_weight, output_weight, up_weight, down_weight, conv_weight, attn_gain, ffn_gain = weights
    key_count = CMEM + MEM + SEG
    context = jnp.concatenate([compressed, memory, hidden], axis=0)
    normed = low(normalize(context, attn_gain))
    places = jnp.arange(key_count).astype(jnp.float32)
    query_raw = low_back(matmul(normed[CMEM + MEM:], query_weight))
    key_raw = low_back(matmul(normed, key_weight))
    value_rows = low(low_back(matmul(normed, value_weight)))
    queries = low(rotate(query_raw.reshape(SEG, HEADS, HEAD_DIM), places[CMEM + MEM:]) * HEAD_DIM ** (-0.5))
    key_rows = low(rotate(key_raw.reshape(key_count, HEADS, HEAD_DIM), places))
    scores = low_back(jnp.einsum('qhd,khd->hqk', queries, key_rows, precision=lax.Precision.HIGHEST))
    scores = jnp.where(visible[None], scores, -1e+30)
    row_max = lax.optimization_barrier(jnp.max(scores, axis=-1, keepdims=True))
    shifted = jnp.exp(scores - row_max)
    attention = low(shifted / lax.optimization_barrier(jnp.sum(shifted, axis=-1, keepdims=True)))
    attended = jnp.einsum('hqk,khd->qhd', attention, value_rows.reshape(key_count, HEADS, HEAD_DIM), precision=lax.Precision.HIGHEST)
    attended = low(low_back(attended.reshape(SEG, D)))
    middle = hidden + low_back(matmul(attended, output_weight))
    normed_ffn = low(normalize(middle, ffn_gain))
    preact = low_back(matmul(normed_ffn, up_weight))
    activated = low(jax.nn.gelu(preact, approximate=False))
    layer_out = middle + low_back(matmul(activated, down_weight))
    padded = jnp.pad(memory, ((1, 1), (0, 0)))
    stacked = jnp.concatenate([padded[offset:offset + MEM:2] for offset in range(4)], axis=1)
    fresh_rows = matmul(stacked, conv_weight.reshape(4 * D, D))
    return (layer_out, fresh_rows)

def reference(hidden, memory, compressed, reset_flag, boundary, query_weight, key_weight, value_weight, output_weight, up_weight, down_weight, conv_weight, attn_gain, ffn_gain, grad_out, grad_fresh):
    weights = (query_weight.astype(jnp.float32), key_weight.astype(jnp.float32), value_weight.astype(jnp.float32), output_weight.astype(jnp.float32), up_weight.astype(jnp.float32), down_weight.astype(jnp.float32), conv_weight.astype(jnp.float32), attn_gain.astype(jnp.float32), ffn_gain.astype(jnp.float32))

    def one_stream(totals, sliced):
        hidden_one, memory_one, compressed_one, reset_one, bound_one, cot_out, cot_fresh = sliced
        visible = visibility(reset_one, bound_one)
        memory_f = memory_one.astype(jnp.float32)
        compressed_f = compressed_one.astype(jnp.float32)

        def forward(hidden_f, params):
            return stream_forward(hidden_f, memory_f, compressed_f, visible, params)
        results, pullback = jax.vjp(forward, hidden_one.astype(jnp.float32), weights)
        grad_hidden, grad_weights = pullback((cot_out.astype(jnp.float32), cot_fresh.astype(jnp.float32)))
        totals = jax.tree.map(lambda left_side, right_side: left_side + right_side, totals, grad_weights)
        return (totals, (results[0].astype(jnp.bfloat16), results[1].astype(jnp.bfloat16), grad_hidden))
    zeros_start = jax.tree.map(jnp.zeros_like, weights)
    totals, stacked_out = lax.scan(one_stream, zeros_start, (hidden, memory, compressed, reset_flag, boundary, grad_out, grad_fresh))
    return (stacked_out[0], stacked_out[1], stacked_out[2], totals[0], totals[1], totals[2], totals[3], totals[4], totals[5], totals[6], totals[7], totals[8])
```

```python
import jax
import jax.numpy as jnp
from jax import lax
from jax.sharding import PartitionSpec as P

HEAD_DIM = 128
BF = jnp.bfloat16
F32 = jnp.float32


def layer_norm(rows):
    center = rows - jnp.mean(rows, axis=-1, keepdims=True)
    spread = jnp.mean(center * center, axis=-1, keepdims=True)
    inv = lax.rsqrt(spread + 1e-05)
    return center * inv, inv


def norm_back(grad, unit, inv, gain):
    c = grad * gain
    return inv * (
        c
        - jnp.mean(c, axis=-1, keepdims=True)
        - unit * jnp.mean(c * unit, axis=-1, keepdims=True)
    )


def rotate(tensor, places, sign):
    half = HEAD_DIM // 2
    frequency = 10000.0 ** (-jnp.arange(half).astype(F32) * 2.0 / HEAD_DIM)
    angles = places[:, None] * frequency[None, :]
    cosine = jnp.cos(angles)[:, None, :]
    sines = sign * jnp.sin(angles)[:, None, :]
    a = tensor[..., :half]
    b = tensor[..., half:]
    return jnp.concatenate([a * cosine - b * sines, a * sines + b * cosine], axis=-1)


def mm(a, b):
    return jnp.dot(a, b, preferred_element_type=F32)


def mmt(a, b):
    return lax.dot_general(a, b, (((a.ndim - 1,), (1,)), ((), ())), preferred_element_type=F32)


def tmm(a, b):
    dims = tuple(range(a.ndim - 1))
    return lax.dot_general(a, b, ((dims, dims), ((), ())), preferred_element_type=F32)


def per_device(
    hidden,
    memory,
    compressed,
    reset_flag,
    boundary,
    query_weight,
    key_weight,
    value_weight,
    output_weight,
    up_weight,
    down_weight,
    conv_weight,
    attn_gain,
    ffn_gain,
    grad_out,
    grad_fresh,
):
    groups = lax.axis_size("stream")
    parts = lax.axis_size("tm")
    rank = lax.axis_index("tm")
    streams, seg_rows, width = hidden.shape
    own = query_weight.shape[0]
    cols = width // parts
    heads = cols // HEAD_DIM
    ff_rows = down_weight.shape[0] // parts
    seg = seg_rows * parts
    cmem = compressed.shape[1] * parts
    mem = memory.shape[1] * parts
    front = cmem + mem

    def col(w):
        return lax.dynamic_slice_in_dim(w, rank * cols, cols, axis=w.ndim - 1)

    gains = lax.all_gather(jnp.stack([attn_gain, ffn_gain]), "stream", axis=1, tiled=True)
    gain_a = gains[0].astype(F32)
    gain_f = gains[1].astype(F32)
    near = jnp.concatenate(
        [col(query_weight), col(key_weight), col(value_weight), output_weight], axis=1
    )
    up_own = lax.dynamic_index_in_dim(
        up_weight.reshape(own, groups, parts, ff_rows), rank, 2, keepdims=False
    ).reshape(own, groups * ff_rows)
    down_own = lax.dynamic_slice_in_dim(down_weight, rank * ff_rows, ff_rows, 0)
    conv_own = col(conv_weight)
    taps = conv_own.shape[0]
    near_full = lax.all_gather(near, "stream", axis=0, tiled=True)
    wq = near_full[:, :cols]
    wk = near_full[:, cols : 2 * cols]
    wv = near_full[:, 2 * cols : 3 * cols]
    wo = near_full[:, 3 * cols :]
    up = lax.all_gather(up_own, "stream", axis=0, tiled=True)
    down = lax.all_gather(down_own, "stream", axis=0, tiled=True)
    conv = lax.all_gather(conv_own, "stream", axis=1, tiled=True)

    context = jnp.concatenate(
        [
            lax.all_gather(compressed, "tm", axis=1, tiled=True),
            lax.all_gather(memory, "tm", axis=1, tiled=True),
            lax.all_gather(hidden, "tm", axis=1, tiled=True),
        ],
        axis=1,
    )
    unit, _ = layer_norm(context.astype(F32))
    normed = (unit * gain_a).astype(BF)
    keys_n = front + seg
    places = jnp.arange(keys_n).astype(F32)
    scale = HEAD_DIM ** (-0.5)
    q = (
        rotate(mm(normed[:, front:], wq).reshape(streams, seg, heads, HEAD_DIM), places[front:], 1.0)
        * scale
    ).astype(BF)
    k = rotate(mm(normed, wk).reshape(streams, keys_n, heads, HEAD_DIM), places, 1.0).astype(BF)
    v = mm(normed, wv).astype(BF).reshape(streams, keys_n, heads, HEAD_DIM)
    documents = jnp.cumsum(boundary, axis=1)
    memory_ok = (reset_flag[:, None] == 0) & (documents == 0)
    spots = jnp.arange(seg)
    local_ok = (spots[None, None, :] <= spots[None, :, None]) & (
        documents[:, None, :] == documents[:, :, None]
    )
    visible = jnp.concatenate(
        [jnp.broadcast_to(memory_ok[:, :, None], (streams, seg, front)), local_ok], axis=2
    )
    scores = jnp.einsum("sqhd,skhd->shqk", q, k, preferred_element_type=F32)
    scores = jnp.where(visible[:, None], scores, -1e30)
    row_max = jnp.max(scores, axis=-1, keepdims=True)
    shifted = jnp.exp(scores - row_max)
    probs = shifted / jnp.sum(shifted, axis=-1, keepdims=True)
    probs_low = probs.astype(BF)
    attended = jnp.einsum("shqk,skhd->sqhd", probs_low, v, preferred_element_type=F32)
    attended = attended.reshape(streams, seg, cols).astype(BF)
    attended_rows = lax.all_to_all(attended, "tm", split_axis=1, concat_axis=2, tiled=True)
    middle = hidden.astype(F32) + mm(attended_rows, wo)
    unit_f, inv_f = layer_norm(middle)
    nf_rows = (unit_f * gain_f).astype(BF)
    nf = lax.all_gather(nf_rows, "tm", axis=1, tiled=True)
    preact = mm(nf, up)
    activated, gelu_back = jax.vjp(lambda t: jax.nn.gelu(t, approximate=False), preact)
    act = activated.astype(BF)
    down_part = mm(act, down).astype(BF)
    layer_out = (
        middle + lax.psum_scatter(down_part, "tm", scatter_dimension=1, tiled=True).astype(F32)
    ).astype(BF)

    memory_full = context[:, cmem:front]
    padded = jnp.pad(memory_full, ((0, 0), (1, 1), (0, 0)))
    stacked = jnp.concatenate([padded[:, o : o + mem : 2] for o in range(taps)], axis=2)
    fresh = mm(stacked, conv.reshape(taps * width, cols)).astype(BF)
    fresh_memory = lax.all_to_all(fresh, "tm", split_axis=1, concat_axis=2, tiled=True)
    grad_fresh_c = lax.all_to_all(grad_fresh, "tm", split_axis=2, concat_axis=1, tiled=True)
    conv_grad = (
        tmm(stacked, grad_fresh_c)
        .astype(BF)
        .reshape(taps, width, cols)
        .transpose(1, 0, 2)
        .reshape(width, taps * cols)
    )

    go = lax.all_gather(grad_out, "tm", axis=1, tiled=True)
    grad_act = mmt(go, down)
    down_grad = tmm(act, go).astype(BF)
    grad_pre = gelu_back(grad_act)[0].astype(BF)
    up_grad = tmm(nf, grad_pre).astype(BF)
    gnf_part = mmt(grad_pre, up).astype(BF)
    gnf = lax.psum_scatter(gnf_part, "tm", scatter_dimension=1, tiled=True).astype(F32)
    grad_middle = grad_out.astype(F32) + norm_back(gnf, unit_f, inv_f, gain_f)
    gm_low = grad_middle.astype(BF)
    output_part = tmm(attended_rows, gm_low).astype(BF)
    output_grad = lax.psum_scatter(output_part, "tm", scatter_dimension=1, tiled=True)
    ga_rows = mmt(gm_low, wo).astype(BF)
    ga = lax.all_to_all(ga_rows, "tm", split_axis=2, concat_axis=1, tiled=True)
    ga = ga.reshape(streams, seg, heads, HEAD_DIM)
    far = lax.psum_scatter(
        jnp.concatenate([up_grad, down_grad, conv_grad], axis=1),
        "stream",
        scatter_dimension=0,
        tiled=True,
    )

    grad_probs = jnp.einsum("sqhd,skhd->shqk", ga, v, preferred_element_type=F32)
    inner = jnp.sum(probs * grad_probs, axis=-1, keepdims=True)
    gs = (probs * (grad_probs - inner)).astype(BF)
    gq = jnp.einsum("shqk,skhd->sqhd", gs, k, preferred_element_type=F32)
    gk = jnp.einsum("shqk,sqhd->skhd", gs, q, preferred_element_type=F32)
    gv = jnp.einsum("shqk,sqhd->skhd", probs_low, ga, preferred_element_type=F32)
    gq = (rotate(gq, places[front:], -1.0) * scale).astype(BF).reshape(streams, seg, cols)
    gk = rotate(gk, places, -1.0).astype(BF).reshape(streams, keys_n, cols)
    gv = gv.astype(BF).reshape(streams, keys_n, cols)
    query_grad = tmm(normed[:, front:], gq).astype(BF)
    key_grad = tmm(normed, gk).astype(BF)
    value_grad = tmm(normed, gv).astype(BF)
    gn_part = (mmt(gq, wq) + mmt(gk[:, front:], wk) + mmt(gv[:, front:], wv)).astype(BF)
    gn = lax.psum_scatter(gn_part, "tm", scatter_dimension=1, tiled=True).astype(F32)
    unit_h, inv_h = layer_norm(hidden.astype(F32))
    grad_input = grad_middle + norm_back(gn, unit_h, inv_h, gain_a)
    close = lax.psum_scatter(
        jnp.concatenate([query_grad, key_grad, value_grad, output_grad], axis=1),
        "stream",
        scatter_dimension=0,
        tiled=True,
    )
    far_all = lax.all_gather(far, "tm", axis=0).astype(F32)
    close_all = lax.all_gather(close, "tm", axis=0).astype(F32)

    def spread_cols(t):
        return t.transpose(1, 0, 2).reshape(own, width)

    query_grad = spread_cols(close_all[:, :, :cols])
    key_grad = spread_cols(close_all[:, :, cols : 2 * cols])
    value_grad = spread_cols(close_all[:, :, 2 * cols : 3 * cols])
    output_grad = spread_cols(close_all[:, :, 3 * cols :])
    ff = groups * ff_rows
    up_grad = (
        far_all[:, :, :ff]
        .reshape(parts, own, groups, ff_rows)
        .transpose(1, 2, 0, 3)
        .reshape(own, ff * parts)
    )
    down_grad = far_all[:, :, ff : ff + width].reshape(parts * ff_rows, width)
    conv_grad = (
        far_all[:, :, ff + width :]
        .reshape(parts, own, taps, cols)
        .transpose(2, 1, 0, 3)
        .reshape(taps, own, width)
    )
    wide = lambda w: w.astype(F32)
    attn_gain_grad = jnp.sum(
        wide(query_weight) * query_grad
        + wide(key_weight) * key_grad
        + wide(value_weight) * value_grad,
        axis=1,
    ) / wide(attn_gain)
    ffn_gain_grad = jnp.sum(wide(up_weight) * up_grad, axis=1) / wide(ffn_gain)
    return (
        layer_out,
        fresh_memory,
        grad_input,
        query_grad,
        key_grad,
        value_grad,
        output_grad,
        up_grad,
        down_grad,
        conv_grad,
        attn_gain_grad,
        ffn_gain_grad,
    )


def solution(mesh):
    act = P("stream", "tm", None)
    row = P("stream", None)
    in_specs = (act, act, act, P("stream"), row) + (row,) * 6 + (
        P(None, "stream", None),
        P("stream"),
        P("stream"),
        act,
        act,
    )
    out_specs = (act, act, act) + (row,) * 6 + (
        P(None, "stream", None),
        P("stream"),
        P("stream"),
    )
    return jax.shard_map(
        per_device, mesh=mesh, in_specs=in_specs, out_specs=out_specs, check_vma=False
    )
```

```python
import functools

import jax
import jax.numpy as jnp
from jax import lax
from jax.experimental import pallas as pl
from jax.experimental.pallas import tpu as pltpu
from jax.sharding import PartitionSpec as P

HEAD_DIM = 128
PARTS = 4
BF = jnp.bfloat16
F32 = jnp.float32
MESH = pl.DeviceIdType.MESH

QKV, WO, UP, DOWN, CONV = range(5)
(T_CTX0, T_CTX1, T_CTX2, T_GO, T_GF, T_WO, T_ATT0, T_ATT1, T_NF0, T_NF1, T_GNF0, T_GNF1) = range(12)
(T_OUT0, T_OUT1, T_GA, T_OP, T_GN0, T_GN1, T_FR) = range(12, 19)
T_COUNT = 19


def dot(a, b, ca=1, cb=0):
    return lax.dot_general(a, b, (((ca,), (cb,)), ((), ())), preferred_element_type=F32)


def loop(n, body):
    def step(i, carry):
        body(i)
        return carry

    lax.fori_loop(0, n, step, 0)


def ds(start, size):
    return pl.ds(pl.multiple_of(start, size), size)


def mean(x):
    return jnp.sum(x, axis=-1, keepdims=True) * (1.0 / x.shape[-1])


def layer_norm(rows):
    center = rows - mean(rows)
    inv = lax.rsqrt(mean(center * center) + 1e-05)
    return center * inv, inv


def norm_back(c, unit, inv):
    return inv * (c - mean(c) - unit * mean(c * unit))


def kernel(
    n_z,
    own,
    hidden,
    memory,
    compressed,
    query_weight,
    key_weight,
    value_weight,
    output_weight,
    up_own,
    down_weight,
    conv_weight,
    grad_out,
    grad_fresh,
    gain_a,
    gain_f,
    cosines,
    sines,
    row_info,
    doc_k,
    layer_out,
    fresh_out,
    grad_input,
    out_q,
    out_k,
    out_v,
    out_o,
    out_up,
    out_down,
    out_conv,
    conv_all,
    unit,
    memraw,
    wqkv,
    wo,
    up,
    down,
    qs,
    kv,
    probs,
    att_own,
    att_rows,
    middle,
    nf,
    go,
    gf,
    act,
    gpre,
    ga,
    gm,
    gm_low,
    gnp,
    d_a,
    y_a,
    d_b,
    y_b,
    d_o,
    y_o,
    l_o,
    l_conv,
    x_qkv,
    x_o,
    x_up,
    x_down,
    x_conv,
    z_qkv,
    z_o,
    z_up,
    z_down,
    z_conv,
    t_v,
    t_q,
    loc,
    tm_s,
    tm_r,
    ag_s,
    ag_r,
    rx_s,
    rx_r,
    rz_s,
    rz_r,
    fin_s,
    fin_r,
):
    st = lax.axis_index("stream")
    r = lax.axis_index("tm")
    z = lax.div(st, 2)
    x = lax.rem(st, 2)
    core = lax.rem(r, 2)
    r1 = r + 1 - 2 * core
    r2 = lax.rem(r + 2, 4)
    r3 = lax.rem(r1 + 2, 4)
    xn = z * 2 + 1 - x
    seg = 512
    col = 256

    def zpeer(dz):
        return lax.rem(z + dz, n_z)

    def zfrom(dz):
        return lax.rem(z + n_z - dz, n_z)

    def load(src, dst, i):
        d = pltpu.make_async_copy(src, dst, loc.at[i])
        d.start()
        return d

    own_rows = ds(st * own, own)
    rcol = ds(r * col, col)
    ld_q = load(query_weight.at[:, rcol], wqkv.at[own_rows, pl.ds(0, col)], 0)
    ld_k = load(key_weight.at[:, rcol], wqkv.at[own_rows, pl.ds(col, col)], 1)
    ld_v = load(value_weight.at[:, rcol], wqkv.at[own_rows, pl.ds(2 * col, col)], 2)
    ld_o = load(output_weight.at[:, rcol], wo.at[own_rows, rcol], 3)
    ld_up = load(up_own, up.at[own_rows], 4)
    ld_dn = load(down_weight.at[ds(r * own, own)], down.at[own_rows], 5)
    ld_cv = [
        load(conv_weight.at[k, :, rcol], conv_all.at[own_rows, pl.ds(k * col, col)], 6 + k)
        for k in range(4)
    ]
    tslot = ds(r * 128, 128)
    ld_c = [
        load(compressed, unit.at[0, :, tslot], 10),
        load(memory, memraw.at[:, :, ds(r * 64, 64)], 11),
        load(hidden, unit.at[2, :, tslot], 12),
        load(hidden, gm_low, 13),
    ]
    ld_go = load(grad_out, go.at[:, tslot], 14)
    ld_gf = load(grad_fresh.at[:, :, rcol], gf.at[:, ds(r * 64, 64)], 15)

    barrier = pltpu.get_barrier_semaphore()
    for peer in (r1, r2, r3):
        pl.semaphore_signal(barrier, 1, device_id=(st, peer), device_id_type=MESH)
    pl.semaphore_signal(barrier, 1, device_id=(xn, r), device_id_type=MESH)

    def greet(i):
        pl.semaphore_signal(
            barrier, 1, device_id=(zpeer(i + 1) * 2 + x, r), device_id_type=MESH
        )

    loop(n_z - 1, greet)
    pl.semaphore_wait(barrier, 4 + n_z - 1)

    def tm_copy(src, dst, op, i, peer):
        return pltpu.make_async_remote_copy(
            src, dst, tm_s.at[op, i], tm_r.at[op, i], device_id=(st, peer), device_id_type=MESH
        )

    def gather_start(op, src, slot):
        tm_copy(src, slot(r), op, 1, r2).start()
        tm_copy(src, slot(r), op, 0, r1).start()

    def gather_forward(op, slot):
        tm_copy(slot(r2), slot(r2), op, 1, r2).wait_recv()
        tm_copy(slot(r2), slot(r2), op, 2, r1).start()

    def gather_finish(op, slot):
        tm_copy(slot(r1), slot(r1), op, 0, r1).wait_recv()
        tm_copy(slot(r3), slot(r3), op, 2, r1).wait_recv()

    def gather_drain(op, slot):
        tm_copy(slot(r), slot(r), op, 0, r1).wait_send()
        tm_copy(slot(r), slot(r), op, 1, r2).wait_send()
        tm_copy(slot(r2), slot(r2), op, 2, r1).wait_send()

    peers = ((0, r1), (1, r2), (2, r3))

    def swap_start(op, src, dst):
        for i, p in peers[::-1]:
            tm_copy(src(p), dst(r), op, i, p).start()

    def swap_finish(op, dst):
        for i, p in peers:
            tm_copy(dst(p), dst(p), op, i, p).wait_recv()

    def swap_drain(op, src):
        for i, p in peers:
            tm_copy(src(p), src(p), op, i, p).wait_send()

    def reduce_start(op, part, far, near):
        tm_copy(part(r3), far, op, 0, r1).start()
        tm_copy(part(r1), near, op, 1, r1).start()

    def reduce_mid(op, part, far, land):
        tm_copy(far, far, op, 0, r1).wait_recv()
        far[...] = (far[...].astype(F32) + part(r2)[...].astype(F32)).astype(BF)
        tm_copy(far, land, op, 2, r2).start()

    def reduce_end(op, part, near, land):
        tm_copy(near, near, op, 1, r1).wait_recv()
        tm_copy(land, land, op, 2, r2).wait_recv()
        return part(r)[...].astype(F32) + near[...].astype(F32) + land[...].astype(F32)

    def reduce_drain(op, part, far):
        tm_copy(part(r3), far, op, 0, r1).wait_send()
        tm_copy(part(r1), far, op, 1, r1).wait_send()
        tm_copy(far, far, op, 2, r2).wait_send()

    held = {
        QKV: wqkv,
        WO: wo.at[:, rcol],
        UP: up,
        DOWN: down,
        CONV: conv_all,
    }

    def wslot(g, s):
        return held[g].at[ds(s * own, own)]

    def w_copy(g, s, i, dev):
        return pltpu.make_async_remote_copy(
            wslot(g, s), wslot(g, s), ag_s.at[g, i], ag_r.at[g, i], device_id=(dev, r), device_id_type=MESH
        )

    def w_send(g):
        w_copy(g, st, 0, xn).start()
        loop(n_z - 1, lambda i: w_copy(g, st, i + 1, zpeer(i + 1) * 2 + x).start())

    def w_forward(g):
        def one(i):
            s = zfrom(i + 1) * 2 + x
            w_copy(g, s, i + 1, st).wait_recv()
            w_copy(g, s, n_z + i, xn).start()

        loop(n_z - 1, one)

    def w_finish(g):
        w_copy(g, xn, 0, xn).wait_recv()
        loop(n_z - 1, lambda i: w_copy(g, zfrom(i + 1) * 2 + 1 - x, n_z + i, xn).wait_recv())

    def w_drain(g):
        loop(2 * n_z - 1, lambda i: w_copy(g, st, i, xn).wait_send())

    x_buf = {QKV: x_qkv, WO: x_o, UP: x_up, DOWN: x_down, CONV: x_conv}
    z_buf = {QKV: z_qkv, WO: z_o, UP: z_up, DOWN: z_down, CONV: z_conv}
    grads = {QKV: act.at[:, pl.ds(0, 3 * col)], WO: l_o, UP: up, DOWN: down, CONV: l_conv}

    def gx_copy(g, zz):
        return pltpu.make_async_remote_copy(
            grads[g].at[ds((zz * 2 + 1 - x) * own, own)],
            x_buf[g].at[ds(zz * own, own)],
            rx_s.at[g, zz],
            rx_r.at[g, zz],
            device_id=(xn, r),
            device_id_type=MESH,
        )

    def gx_start(g):
        loop(n_z, lambda i: gx_copy(g, zpeer(i + 1)).start())

    def gz_copy(g, dz, zz):
        return pltpu.make_async_remote_copy(
            x_buf[g].at[ds(zz * own, own)],
            z_buf[g].at[ds((dz - 1) * own, own)],
            rz_s.at[g, dz],
            rz_r.at[g, dz],
            device_id=(zz * 2 + x, r),
            device_id_type=MESH,
        )

    def gz_start(g):
        def one(i):
            zz = zpeer(i + 1)
            gx_copy(g, zz).wait_recv()
            rows = ds(zz * own, own)
            x_buf[g][rows] = (
                x_buf[g][rows].astype(F32) + grads[g][ds((zz * 2 + x) * own, own)].astype(F32)
            ).astype(BF)
            gz_copy(g, i + 1, zz).start()

        loop(n_z - 1, one)

    outs = {
        WO: (((0, col), lambda p: out_o.at[:, ds(p * col, col)]),),
        QKV: (
            ((0, col), lambda p: out_q.at[:, ds(p * col, col)]),
            ((col, col), lambda p: out_k.at[:, ds(p * col, col)]),
            ((2 * col, col), lambda p: out_v.at[:, ds(p * col, col)]),
        ),
        UP: (((0, 1024), lambda p: out_up.at[p]),),
        DOWN: (((0, 1024), lambda p: out_down.at[ds(p * own, own)]),),
        CONV: tuple(
            ((k * col, col), (lambda k: lambda p: out_conv.at[k, :, ds(p * col, col)])(k))
            for k in range(4)
        ),
    }
    fin_base = {QKV: 0, WO: 3, UP: 4, DOWN: 5, CONV: 6}

    def fin_copy(g, j, i, p, slot_rank):
        (lane, size), slot = outs[g][j]
        n = fin_base[g] + j
        return pltpu.make_async_remote_copy(
            x_buf[g].at[ds(z * own, own), pl.ds(lane, size)],
            slot(slot_rank),
            fin_s.at[n, i],
            fin_r.at[n, i],
            device_id=(st, p),
            device_id_type=MESH,
        )

    def g_final(g, gain):
        gx_copy(g, z).wait_recv()
        rows = ds(z * own, own)
        total = x_buf[g][rows].astype(F32) + grads[g][ds((z * 2 + x) * own, own)].astype(F32)
        for dz in range(1, n_z):
            gz_copy(g, dz, zpeer(dz)).wait_recv()
            total = total + z_buf[g][pl.ds((dz - 1) * own, own)].astype(F32)
        if gain is not None:
            total = total * gain[...]
        x_buf[g][rows] = total.astype(BF)
        for j in range(len(outs[g])):
            for i, p in peers[::-1]:
                fin_copy(g, j, i, p, r).start()
            (lane, size), slot = outs[g][j]
            pltpu.make_async_copy(
                x_buf[g].at[rows, pl.ds(lane, size)], slot(r), loc.at[fin_base[g] + j]
            ).start()

    def g_drain(g):
        loop(n_z, lambda i: gx_copy(g, i).wait_send())
        loop(n_z - 1, lambda i: gz_copy(g, i + 1, zpeer(i + 1)).wait_send())
        for j in range(len(outs[g])):
            for i, p in peers:
                d = fin_copy(g, j, i, p, p)
                d.wait_recv()
                d.wait_send()
            (lane, size), slot = outs[g][j]
            pltpu.make_async_copy(
                x_buf[g].at[ds(z * own, own), pl.ds(lane, size)], slot(r), loc.at[fin_base[g] + j]
            ).wait()

    ctx_slot = (
        lambda p: unit.at[0, :, ds(p * 128, 128)],
        lambda p: memraw.at[:, :, ds(p * 64, 64)],
        lambda p: unit.at[2, :, ds(p * 128, 128)],
    )
    ctx_src = (compressed, memory, hidden)
    for p in range(3):
        gather_start(T_CTX0 + p, ctx_src[p], ctx_slot[p])

    for d in (ld_q, ld_k, ld_v):
        d.wait()
    wqkv[own_rows] = (wqkv[own_rows].astype(F32) * gain_a[...]).astype(BF)
    w_send(QKV)
    ld_o.wait()
    w_send(WO)
    ld_up.wait()
    up[own_rows] = (up[own_rows].astype(F32) * gain_f[...]).astype(BF)
    w_send(UP)
    ld_dn.wait()
    w_send(DOWN)
    for d in ld_cv:
        d.wait()
    w_send(CONV)
    for d in ld_c:
        d.wait()
    ld_go.wait()
    ld_gf.wait()

    def norm_block(p, rank):
        def one(s):
            if p == 1:
                for half in range(2):
                    raw = memraw[s, half, ds(rank * 64, 64), :]
                    unit[p, s, ds(half * 256 + rank * 64, 64), :] = layer_norm(raw.astype(F32))[
                        0
                    ].astype(BF)
            else:
                rows = ds(rank * 128, 128)
                unit[p, s, rows, :] = layer_norm(unit[p, s, rows, :].astype(F32))[0].astype(BF)

        loop(2, one)

    def context(p):
        op, slot = T_CTX0 + p, ctx_slot[p]
        norm_block(p, r)
        gather_forward(op, slot)
        tm_copy(slot(r1), slot(r1), op, 0, r1).wait_recv()
        norm_block(p, r1)
        tm_copy(slot(r3), slot(r3), op, 2, r1).wait_recv()
        norm_block(p, r3)
        tm_copy(slot(r2), slot(r2), op, 2, r1).wait_send()
        norm_block(p, r2)

    def project(p):
        def one(i):
            s = lax.div(i, 2)
            at = lax.rem(i, 2) * 256
            rows = ds(at, 256)
            place = pl.ds(pl.multiple_of(p * seg + at, 256), 256)
            a = unit[p, s, rows, :]
            cs = cosines[place, :]
            sn = sines[place, :]

            def rot(t):
                return t * cs + pltpu.roll(t, 64, 1) * sn

            both = dot(a, wqkv[:, pl.ds(col, 2 * col)])
            for h in range(2):
                kv[s, place, pl.ds(h * 128, 128)] = rot(both[:, h * 128 : h * 128 + 128]).astype(BF)
            kv[s, place, pl.ds(col, col)] = both[:, col:].astype(BF)
            if p == 2:
                q = dot(a, wqkv[:, pl.ds(0, col)])
                for h in range(2):
                    qs[s, rows, pl.ds(h * 128, 128)] = (
                        rot(q[:, h * 128 : h * 128 + 128]) * HEAD_DIM ** (-0.5)
                    ).astype(BF)

        loop(4, one)

    context(0)
    w_forward(QKV)
    context(1)
    w_forward(WO)
    w_finish(QKV)
    project(0)
    project(1)
    context(2)
    go_slot = lambda p: go.at[:, ds(p * 128, 128)]
    gather_start(T_GO, grad_out, go_slot)
    gf_src = lambda p: grad_fresh.at[:, :, ds(p * col, col)]
    gf_dst = lambda p: gf.at[:, ds(p * 64, 64)]
    swap_start(T_GF, gf_src, gf_dst)
    project(2)
    w_finish(WO)
    wo_slot = lambda p: wo.at[:, ds(p * col, col)]
    gather_start(T_WO, wo_slot(r), wo_slot)

    def attend(s):
        def one(qt):
            rows = ds(qt * 128, 128)
            shape = (128, seg)
            below = lax.broadcasted_iota(jnp.int32, shape, 1) <= (
                lax.broadcasted_iota(jnp.int32, shape, 0) + qt * 128
            )
            info = row_info[s, rows, :]
            same = doc_k[s] == info[:, 0:1]
            seen = below & same
            bias = info[:, 1:2]
            for h in range(2):
                lanes = pl.ds(h * 128, 128)
                q = qs[s, rows, lanes]
                far = dot(q, kv[s, pl.ds(0, 1024), lanes], 1, 1) + bias
                near = jnp.where(seen, dot(q, kv[s, pl.ds(1024, seg), lanes], 1, 1), -1e30)
                top = jnp.maximum(
                    jnp.max(far, axis=-1, keepdims=True), jnp.max(near, axis=-1, keepdims=True)
                )
                far = jnp.exp(far - top)
                near = jnp.exp(near - top)
                inv = 1.0 / (
                    jnp.sum(far, axis=-1, keepdims=True) + jnp.sum(near, axis=-1, keepdims=True)
                )
                far = (far * inv).astype(BF)
                near = (near * inv).astype(BF)
                probs[s, h, rows, pl.ds(0, 1024)] = far
                probs[s, h, rows, pl.ds(1024, seg)] = near
                vl = pl.ds(col + h * 128, 128)
                o = dot(far, kv[s, pl.ds(0, 1024), vl]) + dot(near, kv[s, pl.ds(1024, seg), vl])
                att_own[s, rows, lanes] = o.astype(BF)

        loop(4, one)

    att_src = lambda s: lambda p: att_own.at[s, ds(p * 128, 128)]
    att_dst = lambda s: lambda p: att_rows.at[s, :, ds(p * col, col)]

    def attend_send(s):
        swap_start(T_ATT0 + s, att_src(s), att_dst(s))
        att_rows[s, :, rcol] = att_own[s, tslot, :]

    attend(0)
    attend_send(0)
    gather_forward(T_GO, go_slot)
    w_forward(UP)
    gather_forward(T_WO, wo_slot)
    attend(1)
    attend_send(1)
    w_finish(UP)

    swap_finish(T_GF, gf_dst)

    def conv_grads(i):
        c = ds(i * 256, 256)
        even_acc = jnp.zeros((256, 512), F32)
        odd_acc = jnp.zeros((256, 512), F32)
        for s in range(2):
            g = gf[s].astype(F32)
            at = lax.broadcasted_iota(jnp.int32, g.shape, 0)
            ahead = jnp.where(at == 255, 0.0, pltpu.roll(g, 255, 0))
            behind = jnp.where(at == 0, 0.0, pltpu.roll(g, 1, 0))
            low = gf[s]
            odd_acc += dot(memraw[s, 1, :, c], jnp.concatenate([ahead.astype(BF), low], 1), 0, 0)
            even_acc += dot(memraw[s, 0, :, c], jnp.concatenate([low, behind.astype(BF)], 1), 0, 0)
        l_conv[c, pl.ds(0, col)] = odd_acc[:, :col].astype(BF)
        l_conv[c, pl.ds(col, col)] = even_acc[:, :col].astype(BF)
        l_conv[c, pl.ds(2 * col, col)] = odd_acc[:, col:].astype(BF)
        l_conv[c, pl.ds(3 * col, col)] = even_acc[:, col:].astype(BF)

    loop(4, conv_grads)
    gx_start(CONV)

    swap_finish(T_ATT0, att_dst(0))
    swap_finish(T_ATT1, att_dst(1))
    gather_finish(T_WO, wo_slot)
    gather_finish(T_GO, go_slot)

    def project_out(i):
        c = ds(i * 256, 256)
        mid = dot(att_rows[...].reshape(256, 1024), wo[:, c]).reshape(2, 128, 256)
        middle[:, :, c] = gm_low[:, :, c].astype(F32) + mid

    loop(4, project_out)
    nf_slot = lambda s: lambda p: nf.at[s, ds(p * 128, 128)]
    for s in range(2):
        nf[s, tslot, :] = layer_norm(middle[s])[0].astype(BF)
        gather_start(T_NF0 + s, nf_slot(s)(r), nf_slot(s))
    w_forward(DOWN)
    for s in range(2):
        gather_forward(T_NF0 + s, nf_slot(s))
    w_finish(DOWN)

    def ffn(s):
        def one(i):
            c = ds(i * 256, 256)
            pre = dot(nf[s], up[:, c])
            g_act = dot(go[s], down[c, :], 1, 1)
            phi = 0.5 + 0.5 * lax.erf(pre * 0.7071067811865476)
            act[pl.ds(s * seg, seg), c] = (pre * phi).astype(BF)
            slope = phi + pre * (jnp.exp(pre * pre * -0.5) * 0.3989422804014327)
            gpre[pl.ds(s * seg, seg), c] = (g_act * slope).astype(BF)

        loop(4, one)

        def back(i):
            c = ds(i * 256, 256)
            gnp[pl.ds(s * seg, seg), c] = dot(
                gpre[pl.ds(s * seg, seg), :], up[c, :], 1, 1
            ).astype(BF)

        loop(4, back)

    def rows_of(buf, s):
        return lambda p: buf.at[pl.ds(pl.multiple_of(s * seg + p * 128, 128), 128)]

    for s in range(2):
        gather_finish(T_NF0 + s, nf_slot(s))
        ffn(s)
        reduce_start(T_GNF0 + s, rows_of(gnp, s), d_b.at[s, 1], d_b.at[s, 0])
    for s in range(2):
        reduce_mid(T_GNF0 + s, rows_of(gnp, s), d_b.at[s, 1], y_b.at[s])
    w_forward(CONV)

    w_drain(UP)
    nf2 = nf

    def up_grads(i):
        c = ds(i * 256, 256)
        up[c, :] = (
            dot(nf2[0, :, c], gpre[pl.ds(0, seg), :], 0, 0)
            + dot(nf2[1, :, c], gpre[pl.ds(seg, seg), :], 0, 0)
        ).astype(BF)

    loop(4, up_grads)
    gx_start(UP)

    for s in range(2):
        c = reduce_end(T_GNF0 + s, rows_of(gnp, s), d_b.at[s, 0], y_b.at[s])
        u, inv = layer_norm(middle[s])
        g = go[s, tslot, :].astype(F32) + norm_back(c, u, inv)
        gm[s] = g
        gm_low[s] = g.astype(BF)
        reduce_drain(T_GNF0 + s, rows_of(gnp, s), d_b.at[s, 1])
    for s in range(2):
        swap_drain(T_ATT0 + s, att_src(s))

    def attended_grads(i):
        part = dot(gm_low[...].reshape(256, 1024), wo[ds(i * 256, 256), :], 1, 1)
        att_own[:, ds(i * 128, 128), :] = part.astype(BF).reshape(2, 128, col)

    loop(4, attended_grads)
    ga_src = lambda p: att_own.at[:, ds(p * 128, 128)]
    ga_dst = lambda p: ga.at[:, ds(p * 128, 128)]
    swap_start(T_GA, ga_src, ga_dst)
    ga[:, tslot, :] = att_own[:, tslot, :]
    for s in range(2):
        gather_drain(T_NF0 + s, nf_slot(s))

    def output_grads(i):
        c = ds(i * 256, 256)
        part = dot(att_rows[:, :, c].reshape(256, 256), gm_low[...].reshape(256, 1024), 0, 0)
        nf[lax.div(i, 2), ds(lax.rem(i, 2) * 256, 256), :] = part.astype(BF)

    loop(4, output_grads)
    op_part = lambda p: nf.at[:, :, ds(p * col, col)]
    reduce_start(T_OP, op_part, d_o.at[1], d_o.at[0])

    def out_parts(i):
        s = lax.div(i, 4)
        rows = ds(s * seg, seg)
        c = ds(lax.rem(i, 4) * 256, 256)
        gpre[rows, c] = dot(act[rows, :], down[:, c]).astype(BF)

    loop(8, out_parts)
    for s in range(2):
        reduce_start(T_OUT0 + s, rows_of(gpre, s), d_a.at[s, 1], d_a.at[s, 0])
    w_drain(DOWN)

    def down_grads(i):
        c = ds(i * 256, 256)
        down[c, :] = (
            dot(act[pl.ds(0, seg), c], go[0], 0, 0) + dot(act[pl.ds(seg, seg), c], go[1], 0, 0)
        ).astype(BF)

    loop(4, down_grads)
    gx_start(DOWN)
    swap_finish(T_GA, ga_dst)
    gz_start(CONV)
    w_finish(CONV)

    def attend_back(s):
        for h in range(2):
            lanes = pl.ds(h * 128, 128)
            vl = pl.ds(col + h * 128, 128)

            def values(i):
                c = ds(i * 512, 512)
                t_v[c, :] = dot(probs[s, h, :, c], ga[s, :, lanes], 0, 0).astype(BF)

            loop(3, values)

            def scores(i):
                rows = ds(i * 128, 128)
                p = probs[s, h, rows, :].astype(F32)
                gp = dot(ga[s, rows, lanes], kv[s, :, vl], 1, 1)
                inner = jnp.sum(p * gp, axis=-1, keepdims=True)
                gs = (p * (gp - inner)).astype(BF)
                probs[s, h, rows, :] = gs
                place = pl.ds(pl.multiple_of(1024 + i * 128, 128), 128)
                t = dot(gs, kv[s, :, lanes])
                t = t * cosines[place, :] - pltpu.roll(t, 64, 1) * sines[place, :]
                t_q[rows, :] = (t * HEAD_DIM ** (-0.5)).astype(BF)

            loop(4, scores)

            def keys(i):
                c = ds(i * 512, 512)
                t = dot(probs[s, h, :, c], qs[s, :, lanes], 0, 0)
                t = t * cosines[c, :] - pltpu.roll(t, 64, 1) * sines[c, :]
                kv[s, c, lanes] = t.astype(BF)
                kv[s, c, vl] = t_v[c, :]

            loop(3, keys)
            qs[s, :, lanes] = t_q[...]

    attend_back(0)
    reduce_mid(T_OP, op_part, d_o.at[1], y_o)
    for s in range(2):
        reduce_mid(T_OUT0 + s, rows_of(gpre, s), d_a.at[s, 1], y_a.at[s])
    gz_start(UP)
    attend_back(1)

    reduce_drain(T_OP, op_part, d_o.at[1])
    l_o[...] = reduce_end(T_OP, op_part, d_o.at[0], y_o).astype(BF).reshape(1024, col)
    gx_start(WO)

    def kv_grads(i):
        c = ds(i * 256, 256)
        total = jnp.zeros((256, 2 * col), F32)
        for p in range(3):
            for s in range(2):
                total += dot(unit[p, s, :, c], kv[s, pl.ds(p * seg, seg), :], 0, 0)
        act[c, pl.ds(col, 2 * col)] = total.astype(BF)
        act[c, pl.ds(0, col)] = (
            dot(unit[2, 0, :, c], qs[0], 0, 0) + dot(unit[2, 1, :, c], qs[1], 0, 0)
        ).astype(BF)

    loop(4, kv_grads)
    gx_start(QKV)

    def hidden_grads(i):
        s = lax.div(i, 4)
        c = ds(lax.rem(i, 4) * 256, 256)
        part = dot(kv[s, pl.ds(1024, seg), :], wqkv[c, pl.ds(col, 2 * col)], 1, 1) + dot(
            qs[s], wqkv[c, pl.ds(0, col)], 1, 1
        )
        gnp[ds(s * seg, seg), c] = part.astype(BF)

    loop(8, hidden_grads)
    for s in range(2):
        reduce_start(T_GN0 + s, rows_of(gnp, s), d_b.at[s, 1], d_b.at[s, 0])
    ld_h = load(hidden, gm_low, 13)
    g_final(CONV, None)
    gz_start(DOWN)
    for s in range(2):
        reduce_mid(T_GN0 + s, rows_of(gnp, s), d_b.at[s, 1], y_b.at[s])

    gather_drain(T_GO, go_slot)
    ld_w = [
        load(conv_all.at[pl.ds(i * seg, seg)], go.at[i], 14 + i) for i in range(2)
    ]
    for s in range(2):
        out = reduce_end(T_OUT0 + s, rows_of(gpre, s), d_a.at[s, 0], y_a.at[s])
        reduce_drain(T_OUT0 + s, rows_of(gpre, s), d_a.at[s, 1])
        y_a[s] = (middle[s] + out).astype(BF)
    st_out = load(y_a, layer_out, 16)
    for d in ld_w:
        d.wait()
    swap_drain(T_GA, ga_src)
    w_tap = lambda i, k: go[i, :, pl.ds(k * col, col)]

    def fresh(s, carry):
        taps = []
        for k in range(4):
            rows = memraw.at[s, 1 - k % 2]
            taps.append(
                dot(rows[:, pl.ds(0, seg)], w_tap(0, k)) + dot(rows[:, pl.ds(seg, seg)], w_tap(1, k))
            )
        at = lax.broadcasted_iota(jnp.int32, taps[0].shape, 0)
        total = taps[1] + taps[2]
        total += jnp.where(at == 0, 0.0, pltpu.roll(taps[0], 1, 0))
        total += jnp.where(at == 255, 0.0, pltpu.roll(taps[3], 255, 0))
        att_own[s, pl.ds(0, 256), :] = total.astype(BF)
        return carry

    lax.fori_loop(0, 2, fresh, 0)
    fr_src = lambda p: att_own.at[:, ds(p * 64, 64)]
    fr_dst = lambda p: fresh_out.at[:, :, ds(p * col, col)]
    swap_start(T_FR, fr_src, fr_dst)
    st_fr = load(fr_src(r), fr_dst(r), 17)

    g_final(UP, gain_f)
    gz_start(WO)
    gz_start(QKV)
    for s in range(2):
        c = reduce_end(T_GN0 + s, rows_of(gnp, s), d_b.at[s, 0], y_b.at[s])
        if s == 0:
            ld_h.wait()
        u, inv = layer_norm(gm_low[s].astype(F32))
        gm[s] = gm[s] + norm_back(c, u, inv)
    st_gi = load(gm, grad_input, 18)
    g_final(DOWN, None)
    g_final(WO, None)
    g_final(QKV, gain_a)

    for p in range(3):
        tm_copy(ctx_src[p], ctx_slot[p](r), T_CTX0 + p, 0, r1).wait_send()
        tm_copy(ctx_src[p], ctx_slot[p](r), T_CTX0 + p, 1, r2).wait_send()
    swap_drain(T_GF, gf_src)
    gather_drain(T_WO, wo_slot)
    for s in range(2):
        reduce_drain(T_GN0 + s, rows_of(gnp, s), d_b.at[s, 1])
    swap_finish(T_FR, fr_dst)
    swap_drain(T_FR, fr_src)
    for d in (st_out, st_fr, st_gi):
        d.wait()
    for g in (QKV, WO, CONV):
        w_drain(g)
    for g in range(5):
        g_drain(g)


def per_device(
    hidden,
    memory,
    compressed,
    reset_flag,
    boundary,
    query_weight,
    key_weight,
    value_weight,
    output_weight,
    up_weight,
    down_weight,
    conv_weight,
    attn_gain,
    ffn_gain,
    grad_out,
    grad_fresh,
):
    groups = lax.axis_size("stream")
    rank = lax.axis_index("tm")
    streams, seg_rows, width = hidden.shape
    own = query_weight.shape[0]
    seg = seg_rows * PARTS
    cols = width // PARTS
    n_z = groups // 2
    ff_rows = down_weight.shape[0] // PARTS
    up_own = lax.dynamic_index_in_dim(
        up_weight.reshape(own, groups, PARTS, ff_rows), rank, 2, keepdims=False
    ).reshape(own, groups * ff_rows)
    halves = memory.reshape(streams, seg_rows // 2, 2, width).transpose(0, 2, 1, 3)
    gain_a = attn_gain.astype(F32)[:, None]
    gain_f = ffn_gain.astype(F32)[:, None]
    spots = jnp.arange(seg)
    places = jnp.concatenate([spots, seg + spots[::2], seg + spots[1::2], 2 * seg + spots])
    half = HEAD_DIM // 2
    frequency = 10000.0 ** (-jnp.arange(half).astype(F32) * 2.0 / HEAD_DIM)
    angles = places.astype(F32)[:, None] * frequency[None, :]
    cosine = jnp.cos(angles)
    sine = jnp.sin(angles)
    cosines = jnp.concatenate([cosine, cosine], axis=1)
    sines = jnp.concatenate([-sine, sine], axis=1)
    documents = jnp.cumsum(boundary, axis=1)
    memory_ok = (reset_flag[:, None] == 0) & (documents == 0)
    docs = documents.astype(F32)
    row_info = jnp.stack([docs, jnp.where(memory_ok, 0.0, -1e30)], axis=2)
    doc_k = docs[:, None, :]

    hbm = pl.BlockSpec(memory_space=pl.ANY)
    vmem = pl.BlockSpec(memory_space=pltpu.VMEM)
    big = (seg * streams, width)
    out_shape = (
        jax.ShapeDtypeStruct(hidden.shape, BF),
        jax.ShapeDtypeStruct(grad_fresh.shape, BF),
        jax.ShapeDtypeStruct(hidden.shape, F32),
        jax.ShapeDtypeStruct((own, width), BF),
        jax.ShapeDtypeStruct((own, width), BF),
        jax.ShapeDtypeStruct((own, width), BF),
        jax.ShapeDtypeStruct((own, width), BF),
        jax.ShapeDtypeStruct((PARTS, own, width), BF),
        jax.ShapeDtypeStruct((PARTS * own, width), BF),
        jax.ShapeDtypeStruct((4, own, width), BF),
        jax.ShapeDtypeStruct((width, width), BF),
    )

    def v(shape, dtype=BF):
        return pltpu.VMEM(shape, dtype)

    seg2 = (streams, seg, cols)
    rows2 = (streams, seg_rows, width)
    wide = (3 * cols, cols, width, width, width)
    sem = pltpu.SemaphoreType.DMA
    scratch = (
        [
            v((3, streams, seg, width)),
            v((streams, 2, seg // 2, width)),
            v((width, 3 * cols)),
            v((width, width)),
            v(big),
            v(big),
            v(seg2),
            v((streams, 3 * seg, 2 * cols)),
            v((streams, 2, seg, 3 * seg)),
            v(seg2),
            v(rows2),
            v(rows2, F32),
            v((streams, seg, width)),
            v((streams, seg, width)),
            v((streams, seg // 2, cols)),
            v(big),
            v(big),
            v(seg2),
            v(rows2, F32),
            v(rows2),
            v(big),
            v((streams, 2, seg_rows, width)),
            v(rows2),
            v((streams, 2, seg_rows, width)),
            v(rows2),
            v((2, streams, seg, cols)),
            v(seg2),
            v((width, cols)),
            v(big),
        ]
        + [v((n_z * own, c)) for c in wide]
        + [v(((n_z - 1) * own, c)) for c in wide]
        + [
            v((3 * seg, HEAD_DIM)),
            v((seg, HEAD_DIM)),
            sem((20,)),
            sem((T_COUNT, 3)),
            sem((T_COUNT, 3)),
            sem((5, 2 * n_z)),
            sem((5, 2 * n_z)),
            sem((5, n_z)),
            sem((5, n_z)),
            sem((5, n_z)),
            sem((5, n_z)),
            sem((10, 3)),
            sem((10, 3)),
        ]
    )
    results = pl.pallas_call(
        functools.partial(kernel, n_z, own),
        out_shape=out_shape,
        in_specs=[hbm] * 12 + [vmem] * 6,
        out_specs=tuple([hbm] * len(out_shape)),
        scratch_shapes=scratch,
        compiler_params=pltpu.CompilerParams(
            collective_id=0, has_side_effects=True, vmem_limit_bytes=64000 * 1024
        ),
        name="layer",
    )(
        hidden,
        halves,
        compressed,
        query_weight,
        key_weight,
        value_weight,
        output_weight,
        up_own,
        down_weight,
        conv_weight,
        grad_out,
        grad_fresh,
        gain_a,
        gain_f,
        cosines,
        sines,
        row_info,
        doc_k,
    )
    layer_out, fresh, grad_input, g_q, g_k, g_v, g_o, g_up, g_down, g_conv, _ = results
    wide = lambda t: t.astype(F32)
    g_up = g_up.reshape(PARTS, own, groups, ff_rows).transpose(1, 2, 0, 3).reshape(up_weight.shape)
    g_q, g_k, g_v, g_o, g_up, g_down, g_conv = map(wide, (g_q, g_k, g_v, g_o, g_up, g_down, g_conv))
    attn_gain_grad = jnp.sum(
        wide(query_weight) * g_q + wide(key_weight) * g_k + wide(value_weight) * g_v, axis=1
    ) / wide(attn_gain)
    ffn_gain_grad = jnp.sum(wide(up_weight) * g_up, axis=1) / wide(ffn_gain)
    return (
        layer_out,
        fresh,
        grad_input,
        g_q,
        g_k,
        g_v,
        g_o,
        g_up,
        g_down,
        g_conv,
        attn_gain_grad,
        ffn_gain_grad,
    )


def solution(mesh):
    act = P("stream", "tm", None)
    row = P("stream", None)
    in_specs = (act, act, act, P("stream"), row) + (row,) * 6 + (
        P(None, "stream", None),
        P("stream"),
        P("stream"),
        act,
        act,
    )
    out_specs = (act, act, act) + (row,) * 6 + (
        P(None, "stream", None),
        P("stream"),
        P("stream"),
    )
    return jax.shard_map(
        per_device, mesh=mesh, in_specs=in_specs, out_specs=out_specs, check_vma=False
    )
```

```python
import functools

import jax
import jax.numpy as jnp
import numpy as np
from jax import lax
from jax.experimental import pallas as pl
from jax.experimental.pallas import tpu as pltpu
from jax.sharding import PartitionSpec as P

HEAD_DIM = 128
PARTS = 4
BF = jnp.bfloat16
F32 = jnp.float32
MESH = pl.DeviceIdType.MESH

QKV, WO, UP, DOWN, CONV = range(5)
(T_CTX0, T_CTX1, T_CTX2, T_GO, T_GF, T_WO, T_ATT0, T_ATT1, T_NF0, T_NF1, T_GNF0, T_GNF1) = range(12)
(T_OUT0, T_OUT1, T_GA, T_OP, T_GN0, T_GN1, T_FR) = range(12, 19)
T_COUNT = 19


def dot(a, b, ca=1, cb=0):
    return lax.dot_general(a, b, (((ca,), (cb,)), ((), ())), preferred_element_type=F32)


def loop(n, body):
    def step(i, carry):
        body(i)
        return carry

    lax.fori_loop(0, n, step, 0)


def ds(start, size):
    return pl.ds(pl.multiple_of(start, size), size)


def mean(x):
    return jnp.sum(x, axis=-1, keepdims=True) * (1.0 / x.shape[-1])


def layer_norm(rows):
    center = rows - mean(rows)
    inv = lax.rsqrt(mean(center * center) + 1e-05)
    return center * inv, inv


def norm_back(c, unit, inv):
    return inv * (c - mean(c) - unit * mean(c * unit))


def kernel(
    n_z,
    own,
    pieces,
    hidden,
    memory,
    compressed,
    query_weight,
    key_weight,
    value_weight,
    output_weight,
    up_weight,
    down_weight,
    conv_weight,
    grad_out,
    grad_fresh,
    reset_flag,
    boundary,
    gains,
    cosines,
    sines,
    layer_out,
    fresh_out,
    grad_input,
    out_q,
    out_k,
    out_v,
    out_o,
    out_up,
    out_down,
    out_conv,
    conv_all,
    unit,
    memraw,
    wqkv,
    wo,
    up,
    down,
    qs,
    kv,
    probs,
    att_own,
    att_rows,
    middle,
    nf,
    go,
    gf,
    act,
    gpre,
    ga,
    gm,
    gm_low,
    gnp,
    d_a,
    y_a,
    d_b,
    y_b,
    d_o,
    y_o,
    l_o,
    l_conv,
    x_qkv,
    x_o,
    x_up,
    x_down,
    x_conv,
    z_qkv,
    z_o,
    z_up,
    z_down,
    z_conv,
    r_qkv,
    r_o,
    r_up,
    r_down,
    r_conv,
    t_v,
    t_q,
    gain_cols,
    row_info,
    doc_k,
    loc,
    tm_s,
    tm_r,
    ag_s,
    ag_r,
    rx_s,
    rx_r,
    rz_s,
    rz_r,
    fin_s,
    fin_r,
    fin_l,
):
    st = lax.axis_index("stream")
    r = lax.axis_index("tm")
    z = lax.div(st, 2)
    x = lax.rem(st, 2)
    core = lax.rem(r, 2)
    r1 = r + 1 - 2 * core
    r2 = lax.rem(r + 2, 4)
    r3 = lax.rem(r1 + 2, 4)
    xn = z * 2 + 1 - x
    seg = 512
    col = 256

    def zpeer(dz):
        return lax.rem(z + dz, n_z)

    def zfrom(dz):
        return lax.rem(z + n_z - dz, n_z)

    def load(src, dst, i):
        d = pltpu.make_async_copy(src, dst, loc.at[i])
        d.start()
        return d

    own_rows = ds(st * own, own)
    rcol = ds(r * col, col)
    ld_q = load(query_weight.at[:, rcol], wqkv.at[own_rows, pl.ds(0, col)], 0)
    ld_k = load(key_weight.at[:, rcol], wqkv.at[own_rows, pl.ds(col, col)], 1)
    ld_v = load(value_weight.at[:, rcol], wqkv.at[own_rows, pl.ds(2 * col, col)], 2)
    ld_o = load(output_weight.at[:, rcol], wo.at[own_rows, rcol], 3)
    if pieces > 1:
        size = 1024 // pieces
        ld_up = [
            load(
                up_weight.at[:, ds((i * PARTS + r) * size, size)],
                up.at[own_rows, pl.ds(i * size, size)],
                18 + i,
            )
            for i in range(pieces)
        ]
    else:
        ld_up = [load(up_weight, up.at[own_rows], 4)]
    ld_dn = load(down_weight.at[ds(r * own, own)], down.at[own_rows], 5)
    ld_cv = [
        load(conv_weight.at[k, :, rcol], conv_all.at[own_rows, pl.ds(k * col, col)], 6 + k)
        for k in range(4)
    ]
    tslot = ds(r * 128, 128)
    ld_m = load(memory, att_rows, 11)
    ld_c = {
        0: load(compressed, unit.at[0, :, tslot], 10),
        2: load(hidden, unit.at[2, :, tslot], 12),
    }
    ld_h = load(hidden, gm_low, 13)
    ld_go = load(grad_out, go.at[:, tslot], 14)
    ld_gf = load(grad_fresh.at[:, :, rcol], gf.at[:, ds(r * 64, 64)], 15)

    barrier = pltpu.get_barrier_semaphore()
    for peer in (r1, r2, r3):
        pl.semaphore_signal(barrier, 1, device_id=(st, peer), device_id_type=MESH)
    pl.semaphore_signal(barrier, 1, device_id=(xn, r), device_id_type=MESH)

    def greet(i):
        pl.semaphore_signal(
            barrier, 1, device_id=(zpeer(i + 1) * 2 + x, r), device_id_type=MESH
        )

    loop(n_z - 1, greet)
    pl.semaphore_wait(barrier, 4 + n_z - 1)

    def tm_copy(src, dst, op, i, peer):
        return pltpu.make_async_remote_copy(
            src, dst, tm_s.at[op, i], tm_r.at[op, i], device_id=(st, peer), device_id_type=MESH
        )

    def gather_start(op, src, slot):
        tm_copy(src, slot(r), op, 1, r2).start()
        tm_copy(src, slot(r), op, 0, r1).start()

    def gather_forward(op, slot):
        tm_copy(slot(r2), slot(r2), op, 1, r2).wait_recv()
        tm_copy(slot(r2), slot(r2), op, 2, r1).start()

    def gather_finish(op, slot):
        tm_copy(slot(r1), slot(r1), op, 0, r1).wait_recv()
        tm_copy(slot(r3), slot(r3), op, 2, r1).wait_recv()

    def gather_drain(op, slot):
        tm_copy(slot(r), slot(r), op, 0, r1).wait_send()
        tm_copy(slot(r), slot(r), op, 1, r2).wait_send()
        tm_copy(slot(r2), slot(r2), op, 2, r1).wait_send()

    peers = ((0, r1), (1, r2), (2, r3))

    def swap_start(op, src, dst):
        for i, p in peers[::-1]:
            tm_copy(src(p), dst(r), op, i, p).start()

    def swap_finish(op, dst):
        for i, p in peers:
            tm_copy(dst(p), dst(p), op, i, p).wait_recv()

    def swap_drain(op, src):
        for i, p in peers:
            tm_copy(src(p), src(p), op, i, p).wait_send()

    def reduce_start(op, part, far, near):
        tm_copy(part(r3), far, op, 0, r1).start()
        tm_copy(part(r1), near, op, 1, r1).start()

    def reduce_mid(op, part, far, land):
        tm_copy(far, far, op, 0, r1).wait_recv()
        far[...] = (far[...].astype(F32) + part(r2)[...].astype(F32)).astype(BF)
        tm_copy(far, land, op, 2, r2).start()

    def reduce_end(op, part, near, land):
        tm_copy(near, near, op, 1, r1).wait_recv()
        tm_copy(land, land, op, 2, r2).wait_recv()
        return part(r)[...].astype(F32) + near[...].astype(F32) + land[...].astype(F32)

    def reduce_drain(op, part, far):
        tm_copy(part(r3), far, op, 0, r1).wait_send()
        tm_copy(part(r1), far, op, 1, r1).wait_send()
        tm_copy(far, far, op, 2, r2).wait_send()

    held = {
        QKV: wqkv,
        WO: wo.at[:, rcol],
        UP: up,
        DOWN: down,
        CONV: conv_all,
    }

    def wslot(g, s):
        return held[g].at[ds(s * own, own)]

    def w_copy(g, s, i, dev, j=None):
        return pltpu.make_async_remote_copy(
            wslot(g, s),
            wslot(g, s),
            ag_s.at[g, i],
            ag_r.at[g, i if j is None else j],
            device_id=(dev, r),
            device_id_type=MESH,
        )

    relay = n_z == 4
    inner = (z == 1) | (z == 2)

    def direct(dz):
        zz = zpeer(dz)
        return (z + 3 != zz) & (zz + 3 != z)

    def w_send(g):
        w_copy(g, st, 0, xn).start()
        if relay:
            for dz in (2, 1, 3):

                @pl.when(direct(dz))
                def _():
                    w_copy(g, st, dz, zpeer(dz) * 2 + x).start()
        else:
            loop(n_z - 1, lambda i: w_copy(g, st, i + 1, zpeer(i + 1) * 2 + x).start())

    def w_pass(g, dz):
        s = zfrom(dz) * 2 + x
        w_copy(g, s, dz, st).wait_recv()
        w_copy(g, s, n_z + dz - 1, xn).start()

    def w_relay(g):
        s = zfrom(2) * 2 + x
        return w_copy(g, s, 2 * n_z - 1, 3 * (z - 1) * 2 + x, 2 * z - 1)

    last = jnp.where(z == 0, 1, 3)

    def w_forward(g):
        if relay:
            s = zfrom(2) * 2 + x
            w_copy(g, s, 2, st).wait_recv()

            @pl.when(inner)
            def _():
                w_relay(g).start()

            w_copy(g, s, n_z + 1, xn).start()
            w_pass(g, 4 - last)
        else:
            loop(n_z - 1, lambda i: w_pass(g, i + 1))

    def w_forward_last(g):
        if relay:
            w_pass(g, last)

    def w_cross(g):
        w_copy(g, xn, 0, xn).wait_recv()
        if relay:
            for dz in (2, 1, 3):

                @pl.when(direct(dz))
                def _():
                    w_copy(g, xn, n_z + dz - 1, zpeer(dz) * 2 + x).start()
        else:
            loop(n_z - 1, lambda i: w_copy(g, xn, n_z + i, zpeer(i + 1) * 2 + x).start())

    def w_relay_cross(g):
        s = zfrom(2) * 2 + 1 - x
        return w_copy(g, s, 2 * n_z, 3 * (z - 1) * 2 + x, n_z + 2 * z - 2)

    def w_cross_pass(g):
        if relay:
            w_copy(g, zfrom(2) * 2 + x, 2, st).wait_recv()
            w_copy(g, zfrom(2) * 2 + 1 - x, n_z + 1, st).wait_recv()

            @pl.when(inner)
            def _():
                w_relay(g).start()
                w_relay_cross(g).start()

    def w_cross_finish(g):
        rest = (1, 3) if relay else range(1, n_z)
        for dz in rest:
            w_copy(g, zfrom(dz) * 2 + x, dz, st).wait_recv()
            w_copy(g, zfrom(dz) * 2 + 1 - x, n_z + dz - 1, st).wait_recv()

    def w_cross_drain(g):
        w_copy(g, st, 0, xn).wait_send()
        for dz in range(1, n_z):
            if relay:

                @pl.when(direct(dz))
                def _():
                    w_copy(g, st, dz, xn).wait_send()
                    w_copy(g, st, n_z + dz - 1, xn).wait_send()
            else:
                w_copy(g, st, dz, xn).wait_send()
                w_copy(g, st, n_z + dz - 1, xn).wait_send()
        if relay:

            @pl.when(inner)
            def _():
                w_relay(g).wait_send()
                w_relay_cross(g).wait_send()

    def w_finish(g):
        w_copy(g, xn, 0, xn).wait_recv()
        loop(n_z - 1, lambda i: w_copy(g, zfrom(i + 1) * 2 + 1 - x, n_z + i, xn).wait_recv())

    def w_drain(g):
        w_copy(g, st, 0, xn).wait_send()
        loop(n_z - 1, lambda i: w_copy(g, st, n_z + i, xn).wait_send())
        if relay:
            for dz in (1, 2, 3):

                @pl.when(direct(dz))
                def _():
                    w_copy(g, st, dz, xn).wait_send()

            @pl.when(inner)
            def _():
                w_relay(g).wait_send()
        else:
            loop(n_z - 1, lambda i: w_copy(g, st, i + 1, xn).wait_send())

    x_buf = {QKV: x_qkv, WO: x_o, UP: x_up, DOWN: x_down, CONV: x_conv}
    r_buf = {QKV: r_qkv, WO: r_o, UP: r_up, DOWN: r_down, CONV: r_conv}
    z_buf = {QKV: z_qkv, WO: z_o, UP: z_up, DOWN: z_down, CONV: z_conv}
    grads = {QKV: act.at[:, pl.ds(0, 3 * col)], WO: l_o, UP: up, DOWN: down, CONV: l_conv}

    def gx_copy(g, zz):
        return pltpu.make_async_remote_copy(
            grads[g].at[ds((zz * 2 + 1 - x) * own, own)],
            x_buf[g].at[ds(zz * own, own)],
            rx_s.at[g, zz],
            rx_r.at[g, zz],
            device_id=(xn, r),
            device_id_type=MESH,
        )

    def gx_start(g):
        loop(n_z, lambda i: gx_copy(g, zpeer(i + 1)).start())

    def gz_copy(g, dz, zz):
        return pltpu.make_async_remote_copy(
            x_buf[g].at[ds(zz * own, own)],
            z_buf[g].at[ds((dz - 1) * own, own)],
            rz_s.at[g, dz],
            rz_r.at[g, dz],
            device_id=(zz * 2 + x, r),
            device_id_type=MESH,
        )

    def gz_fold(g, zz):
        gx_copy(g, zz).wait_recv()
        rows = ds(zz * own, own)
        x_buf[g][rows] = (
            x_buf[g][rows].astype(F32) + grads[g][ds((zz * 2 + x) * own, own)].astype(F32)
        ).astype(BF)

    def gz_far(g, dz, zz):
        return pltpu.make_async_remote_copy(
            x_buf[g].at[ds(zz * own, own)],
            r_buf[g],
            rz_s.at[g, dz],
            rz_r.at[g, 0],
            device_id=(jnp.where(z == 0, 1, 2) * 2 + x, r),
            device_id_type=MESH,
        )

    def gz_start(g):
        if not relay:

            def one(i):
                zz = zpeer(i + 1)
                gz_fold(g, zz)
                gz_copy(g, i + 1, zz).start()

            loop(n_z - 1, one)
            return
        for dz in (1, 3):
            zz = zpeer(dz)
            gz_fold(g, zz)

            @pl.when(direct(dz))
            def _():
                gz_copy(g, dz, zz).start()

            @pl.when(jnp.logical_not(direct(dz)))
            def _():
                gz_far(g, dz, zz).start()

        @pl.when(jnp.logical_not(inner))
        def _():
            gz_fold(g, zpeer(2))
            gz_copy(g, 2, zpeer(2)).start()

    def gz_relay(g):
        if relay:

            @pl.when(inner)
            def _():
                zz = zpeer(2)
                gz_fold(g, zz)
                gz_far(g, 2, zz).wait_recv()
                rows = ds(zz * own, own)
                x_buf[g][rows] = (x_buf[g][rows].astype(F32) + r_buf[g][...].astype(F32)).astype(BF)
                gz_copy(g, 2, zz).start()

    outs = {
        WO: (((0, col), lambda p: out_o.at[:, ds(p * col, col)]),),
        QKV: (
            ((0, col), lambda p: out_q.at[:, ds(p * col, col)]),
            ((col, col), lambda p: out_k.at[:, ds(p * col, col)]),
            ((2 * col, col), lambda p: out_v.at[:, ds(p * col, col)]),
        ),
        UP: tuple(
            (
                (i * (1024 // pieces), 1024 // pieces),
                (lambda i: lambda p: out_up.at[:, ds((i * PARTS + p) * (1024 // pieces), 1024 // pieces)])(i),
            )
            for i in range(pieces)
        ),
        DOWN: (((0, 1024), lambda p: out_down.at[ds(p * own, own)]),),
        CONV: tuple(
            ((k * col, col), (lambda k: lambda p: out_conv.at[k, :, ds(p * col, col)])(k))
            for k in range(4)
        ),
    }
    fin_base = {QKV: 0, WO: 3, DOWN: 4, CONV: 5, UP: 9}

    def fin_copy(g, j, i, p, slot_rank):
        (lane, size), slot = outs[g][j]
        n = fin_base[g] + j
        return pltpu.make_async_remote_copy(
            x_buf[g].at[ds(z * own, own), pl.ds(lane, size)],
            slot(slot_rank),
            fin_s.at[n, i],
            fin_r.at[n, i],
            device_id=(st, p),
            device_id_type=MESH,
        )

    def g_keep(g, j):
        (lane, size), slot = outs[g][j]
        return pltpu.make_async_copy(
            x_buf[g].at[ds(z * own, own), pl.ds(lane, size)], slot(r), fin_l.at[fin_base[g] + j]
        )

    def g_final(g, gain):
        gx_copy(g, z).wait_recv()
        rows = ds(z * own, own)
        total = x_buf[g][rows].astype(F32) + grads[g][ds((z * 2 + x) * own, own)].astype(F32)
        for dz in range(1, n_z):
            if relay:

                @pl.when(direct(n_z - dz))
                def _():
                    gz_copy(g, dz, zpeer(dz)).wait_recv()
            else:
                gz_copy(g, dz, zpeer(dz)).wait_recv()
            total = total + z_buf[g][pl.ds((dz - 1) * own, own)].astype(F32)
        if gain is not None:
            total = total * gain
        x_buf[g][rows] = total.astype(BF)
        for j in range(len(outs[g])):
            fin_copy(g, j, 1, r2, r).start()
            fin_copy(g, j, 0, r1, r).start()
            g_keep(g, j).start()

    def fin_pass(g, j):
        slot = outs[g][j][1](r2)
        n = fin_base[g] + j
        return pltpu.make_async_remote_copy(
            slot, slot, fin_s.at[n, 2], fin_r.at[n, 2], device_id=(st, r1), device_id_type=MESH
        )

    def g_pass(g):
        for j in range(len(outs[g])):
            fin_copy(g, j, 1, r2, r2).wait_recv()
            fin_pass(g, j).start()

    def g_drain(g):
        loop(n_z, lambda i: gx_copy(g, i).wait_send())
        loop(n_z - 1, lambda i: gz_copy(g, i + 1, zpeer(i + 1)).wait_send())
        for j in range(len(outs[g])):
            fin_copy(g, j, 0, r1, r1).wait()
            fin_copy(g, j, 1, r2, r).wait_send()
            fin_pass(g, j).wait()
            g_keep(g, j).wait()

    ctx_slot = (
        lambda p: unit.at[0, :, ds(p * 128, 128)],
        lambda p: memraw.at[:, :, ds(p * 64, 64)],
        lambda p: unit.at[2, :, ds(p * 128, 128)],
    )
    gather_start(T_CTX0, compressed, ctx_slot[0])
    for d in (ld_q, ld_k, ld_v):
        d.wait()
    eye = lax.broadcasted_iota(jnp.int32, (own, own), 0) == lax.broadcasted_iota(
        jnp.int32, (own, own), 1
    )
    gain_cols[...] = dot(eye.astype(F32).astype(BF), gains[...], 1, 1)
    gain_a = gain_cols[:, 0:1]
    gain_f = gain_cols[:, 1:2]
    wqkv[own_rows] = (wqkv[own_rows].astype(F32) * gain_a).astype(BF)
    w_send(QKV)
    ld_m.wait()
    row = lax.broadcasted_iota(jnp.int32, (128, 128), 0)
    source = 2 * lax.rem(row, 64) + lax.div(row, 64)
    pick = (lax.broadcasted_iota(jnp.int32, (128, 128), 1) == source).astype(F32).astype(BF)
    for s in range(2):
        split = dot(pick, att_rows[s]).astype(BF)
        memraw[s, 0, ds(r * 64, 64), :] = split[:64]
        memraw[s, 1, ds(r * 64, 64), :] = split[64:]
    gather_start(T_CTX1, ctx_slot[1](r), ctx_slot[1])
    gather_start(T_CTX2, hidden, ctx_slot[2])
    ctx_src = (compressed, ctx_slot[1](r), hidden)
    gf_src = lambda p: grad_fresh.at[:, :, ds(p * col, col)]
    gf_dst = lambda p: gf.at[:, ds(p * 64, 64)]
    swap_start(T_GF, gf_src, gf_dst)
    ld_o.wait()
    w_send(WO)
    for d in ld_up:
        d.wait()
    up[own_rows] = (up[own_rows].astype(F32) * gain_f).astype(BF)
    w_send(UP)
    ld_dn.wait()
    w_send(DOWN)
    for d in ld_cv:
        d.wait()
    w_send(CONV)

    if relay:
        for end, dz in ((0, 1), (3, 3)):

            @pl.when(z == end)
            def _():
                for g in range(5):
                    z_buf[g][pl.ds((dz - 1) * own, own)] = jnp.zeros((own, z_buf[g].shape[1]), BF)

    before = lax.broadcasted_iota(jnp.int32, (seg, seg), 1) <= lax.broadcasted_iota(
        jnp.int32, (seg, seg), 0
    )
    before = before.astype(F32).astype(BF)
    starts = boundary[...].astype(F32).astype(BF)
    docs = dot(before, starts, 1, 1)
    doc_k[...] = dot(starts, before, 1, 1)
    for s in range(2):
        row_info[s, :, 0:1] = docs[:, s : s + 1]
        away = docs[:, s : s + 1] + reset_flag[s].astype(F32)
        row_info[s, :, 1:2] = jnp.where(away == 0.0, 0.0, -1e30)

    def norm_block(p, rank):
        def one(s):
            if p == 1:
                for half in range(2):
                    raw = memraw[s, half, ds(rank * 64, 64), :]
                    unit[p, s, ds(half * 256 + rank * 64, 64), :] = layer_norm(raw.astype(F32))[
                        0
                    ].astype(BF)
            else:
                rows = ds(rank * 128, 128)
                unit[p, s, rows, :] = layer_norm(unit[p, s, rows, :].astype(F32))[0].astype(BF)

        loop(2, one)

    def context(p):
        op, slot = T_CTX0 + p, ctx_slot[p]
        if p in ld_c:
            ld_c[p].wait()
        norm_block(p, r)
        gather_forward(op, slot)
        tm_copy(slot(r1), slot(r1), op, 0, r1).wait_recv()
        norm_block(p, r1)
        tm_copy(slot(r3), slot(r3), op, 2, r1).wait_recv()
        norm_block(p, r3)
        tm_copy(slot(r2), slot(r2), op, 2, r1).wait_send()
        norm_block(p, r2)

    def project(p):
        def one(i):
            s = lax.div(i, 2)
            at = lax.rem(i, 2) * 256
            rows = ds(at, 256)
            place = pl.ds(pl.multiple_of(p * seg + at, 256), 256)
            a = unit[p, s, rows, :]
            cs = cosines[place, :]
            sn = sines[place, :]

            def rot(t):
                return t * cs + pltpu.roll(t, 64, 1) * sn

            both = dot(a, wqkv[:, pl.ds(col, 2 * col)])
            for h in range(2):
                kv[s, place, pl.ds(h * 128, 128)] = rot(both[:, h * 128 : h * 128 + 128]).astype(BF)
            kv[s, place, pl.ds(col, col)] = both[:, col:].astype(BF)
            if p == 2:
                q = dot(a, wqkv[:, pl.ds(0, col)])
                for h in range(2):
                    qs[s, rows, pl.ds(h * 128, 128)] = (
                        rot(q[:, h * 128 : h * 128 + 128]) * HEAD_DIM ** (-0.5)
                    ).astype(BF)

        loop(4, one)

    context(0)
    w_forward(QKV)
    context(1)
    w_forward(WO)
    w_forward_last(QKV)
    w_finish(QKV)
    project(0)
    project(1)
    w_cross(CONV)

    ld_gf.wait()
    swap_finish(T_GF, gf_dst)

    def conv_grads(i):
        c = ds(i * 256, 256)
        even_acc = jnp.zeros((256, 512), F32)
        odd_acc = jnp.zeros((256, 512), F32)
        for s in range(2):
            g = gf[s].astype(F32)
            at = lax.broadcasted_iota(jnp.int32, g.shape, 0)
            ahead = jnp.where(at == 255, 0.0, pltpu.roll(g, 255, 0))
            behind = jnp.where(at == 0, 0.0, pltpu.roll(g, 1, 0))
            low = gf[s]
            odd_acc += dot(memraw[s, 1, :, c], jnp.concatenate([ahead.astype(BF), low], 1), 0, 0)
            even_acc += dot(memraw[s, 0, :, c], jnp.concatenate([low, behind.astype(BF)], 1), 0, 0)
        l_conv[c, pl.ds(0, col)] = odd_acc[:, :col].astype(BF)
        l_conv[c, pl.ds(col, col)] = even_acc[:, :col].astype(BF)
        l_conv[c, pl.ds(2 * col, col)] = odd_acc[:, col:].astype(BF)
        l_conv[c, pl.ds(3 * col, col)] = even_acc[:, col:].astype(BF)

    loop(4, conv_grads)

    w_forward_last(WO)
    w_forward(UP)
    context(2)
    project(2)
    w_finish(WO)
    wo_slot = lambda p: wo.at[:, ds(p * col, col)]
    gather_start(T_WO, wo_slot(r), wo_slot)

    def attend(s):
        def one(qt):
            rows = ds(qt * 128, 128)
            shape = (128, seg)
            below = lax.broadcasted_iota(jnp.int32, shape, 1) <= (
                lax.broadcasted_iota(jnp.int32, shape, 0) + qt * 128
            )
            info = row_info[s, rows, :]
            same = doc_k[pl.ds(s, 1), :] == info[:, 0:1]
            seen = below & same
            bias = info[:, 1:2]
            for h in range(2):
                lanes = pl.ds(h * 128, 128)
                q = qs[s, rows, lanes]
                far = dot(q, kv[s, pl.ds(0, 1024), lanes], 1, 1) + bias
                near = jnp.where(seen, dot(q, kv[s, pl.ds(1024, seg), lanes], 1, 1), -1e30)
                top = jnp.maximum(
                    jnp.max(far, axis=-1, keepdims=True), jnp.max(near, axis=-1, keepdims=True)
                )
                far = jnp.exp(far - top)
                near = jnp.exp(near - top)
                inv = 1.0 / (
                    jnp.sum(far, axis=-1, keepdims=True) + jnp.sum(near, axis=-1, keepdims=True)
                )
                far = (far * inv).astype(BF)
                near = (near * inv).astype(BF)
                probs[s, h, rows, pl.ds(0, 1024)] = far
                probs[s, h, rows, pl.ds(1024, seg)] = near
                vl = pl.ds(col + h * 128, 128)
                o = dot(far, kv[s, pl.ds(0, 1024), vl]) + dot(near, kv[s, pl.ds(1024, seg), vl])
                att_own[s, rows, lanes] = o.astype(BF)

        loop(4, one)

    att_src = lambda s: lambda p: att_own.at[s, ds(p * 128, 128)]
    att_dst = lambda s: lambda p: att_rows.at[s, :, ds(p * col, col)]

    def attend_send(s):
        swap_start(T_ATT0 + s, att_src(s), att_dst(s))
        att_rows[s, :, rcol] = att_own[s, tslot, :]

    attend(0)
    attend_send(0)
    w_forward_last(UP)
    gather_forward(T_WO, wo_slot)
    attend(1)
    attend_send(1)
    go_slot = lambda p: go.at[:, ds(p * 128, 128)]
    gather_start(T_GO, grad_out, go_slot)
    w_forward(DOWN)

    swap_finish(T_ATT0, att_dst(0))
    swap_finish(T_ATT1, att_dst(1))
    gather_finish(T_WO, wo_slot)
    ld_h.wait()

    def project_out(i):
        c = ds(i * 256, 256)
        mid = dot(att_rows[...].reshape(256, 1024), wo[:, c]).reshape(2, 128, 256)
        middle[:, :, c] = gm_low[:, :, c].astype(F32) + mid

    loop(4, project_out)
    nf_slot = lambda s: lambda p: nf.at[s, ds(p * 128, 128)]
    for s in range(2):
        nf[s, tslot, :] = layer_norm(middle[s])[0].astype(BF)
        gather_start(T_NF0 + s, nf_slot(s)(r), nf_slot(s))
    w_forward_last(DOWN)
    gather_forward(T_GO, go_slot)
    ld_go.wait()
    for s in range(2):
        gather_forward(T_NF0 + s, nf_slot(s))
    gather_finish(T_GO, go_slot)
    gx_start(CONV)
    w_finish(UP)
    w_finish(DOWN)

    def ffn(s):
        def one(i):
            c = ds(i * 256, 256)
            pre = dot(nf[s], up[:, c])
            g_act = dot(go[s], down[c, :], 1, 1)
            phi = 0.5 + 0.5 * lax.erf(pre * 0.7071067811865476)
            act[pl.ds(s * seg, seg), c] = (pre * phi).astype(BF)
            slope = phi + pre * (jnp.exp(pre * pre * -0.5) * 0.3989422804014327)
            gpre[pl.ds(s * seg, seg), c] = (g_act * slope).astype(BF)

        loop(4, one)

        def back(i):
            c = ds(i * 256, 256)
            gnp[pl.ds(s * seg, seg), c] = dot(
                gpre[pl.ds(s * seg, seg), :], up[c, :], 1, 1
            ).astype(BF)

        loop(4, back)

    def rows_of(buf, s):
        return lambda p: buf.at[pl.ds(pl.multiple_of(s * seg + p * 128, 128), 128)]

    for s in range(2):
        gather_finish(T_NF0 + s, nf_slot(s))
        ffn(s)
        reduce_start(T_GNF0 + s, rows_of(gnp, s), d_b.at[s, 1], d_b.at[s, 0])
    for s in range(2):
        reduce_mid(T_GNF0 + s, rows_of(gnp, s), d_b.at[s, 1], y_b.at[s])
    w_cross_pass(CONV)

    w_drain(UP)
    nf2 = nf

    def up_grads(i):
        c = ds(i * 256, 256)
        up[c, :] = (
            dot(nf2[0, :, c], gpre[pl.ds(0, seg), :], 0, 0)
            + dot(nf2[1, :, c], gpre[pl.ds(seg, seg), :], 0, 0)
        ).astype(BF)

    loop(4, up_grads)
    gx_start(UP)

    for s in range(2):
        c = reduce_end(T_GNF0 + s, rows_of(gnp, s), d_b.at[s, 0], y_b.at[s])
        u, inv = layer_norm(middle[s])
        g = go[s, tslot, :].astype(F32) + norm_back(c, u, inv)
        gm[s] = g
        gm_low[s] = g.astype(BF)
        reduce_drain(T_GNF0 + s, rows_of(gnp, s), d_b.at[s, 1])
    for s in range(2):
        swap_drain(T_ATT0 + s, att_src(s))

    def attended_grads(i):
        part = dot(gm_low[...].reshape(256, 1024), wo[ds(i * 256, 256), :], 1, 1)
        att_own[:, ds(i * 128, 128), :] = part.astype(BF).reshape(2, 128, col)

    loop(4, attended_grads)
    ga_src = lambda p: att_own.at[:, ds(p * 128, 128)]
    ga_dst = lambda p: ga.at[:, ds(p * 128, 128)]
    swap_start(T_GA, ga_src, ga_dst)
    ga[:, tslot, :] = att_own[:, tslot, :]
    for s in range(2):
        gather_drain(T_NF0 + s, nf_slot(s))

    def output_grads(i):
        c = ds(i * 256, 256)
        part = dot(att_rows[:, :, c].reshape(256, 256), gm_low[...].reshape(256, 1024), 0, 0)
        nf[lax.div(i, 2), ds(lax.rem(i, 2) * 256, 256), :] = part.astype(BF)

    loop(4, output_grads)
    op_part = lambda p: nf.at[:, :, ds(p * col, col)]
    reduce_start(T_OP, op_part, d_o.at[1], d_o.at[0])

    def out_parts(i):
        s = lax.div(i, 4)
        rows = ds(s * seg, seg)
        c = ds(lax.rem(i, 4) * 256, 256)
        gpre[rows, c] = dot(act[rows, :], down[:, c]).astype(BF)

    loop(8, out_parts)
    for s in range(2):
        reduce_start(T_OUT0 + s, rows_of(gpre, s), d_a.at[s, 1], d_a.at[s, 0])
    w_drain(DOWN)

    def down_grads(i):
        c = ds(i * 256, 256)
        down[c, :] = (
            dot(act[pl.ds(0, seg), c], go[0], 0, 0) + dot(act[pl.ds(seg, seg), c], go[1], 0, 0)
        ).astype(BF)

    loop(4, down_grads)
    gx_start(DOWN)
    swap_finish(T_GA, ga_dst)

    def attend_back(s, h):
        if True:
            lanes = pl.ds(h * 128, 128)
            vl = pl.ds(col + h * 128, 128)

            def values(i):
                c = ds(i * 512, 512)
                t_v[c, :] = dot(probs[s, h, :, c], ga[s, :, lanes], 0, 0).astype(BF)

            loop(3, values)

            def scores(i):
                rows = ds(i * 128, 128)
                p = probs[s, h, rows, :].astype(F32)
                gp = dot(ga[s, rows, lanes], kv[s, :, vl], 1, 1)
                inner = jnp.sum(p * gp, axis=-1, keepdims=True)
                gs = (p * (gp - inner)).astype(BF)
                probs[s, h, rows, :] = gs
                place = pl.ds(pl.multiple_of(1024 + i * 128, 128), 128)
                t = dot(gs, kv[s, :, lanes])
                t = t * cosines[place, :] - pltpu.roll(t, 64, 1) * sines[place, :]
                t_q[rows, :] = (t * HEAD_DIM ** (-0.5)).astype(BF)

            loop(4, scores)

            def keys(i):
                c = ds(i * 512, 512)
                t = dot(probs[s, h, :, c], qs[s, :, lanes], 0, 0)
                t = t * cosines[c, :] - pltpu.roll(t, 64, 1) * sines[c, :]
                kv[s, c, lanes] = t.astype(BF)
                kv[s, c, vl] = t_v[c, :]

            loop(3, keys)
            qs[s, :, lanes] = t_q[...]

    gz_start(CONV)
    attend_back(0, 0)
    reduce_mid(T_OP, op_part, d_o.at[1], y_o)
    for s in range(2):
        reduce_mid(T_OUT0 + s, rows_of(gpre, s), d_a.at[s, 1], y_a.at[s])
    gz_relay(CONV)
    attend_back(0, 1)
    attend_back(1, 0)
    gz_start(UP)
    attend_back(1, 1)
    g_final(CONV, None)

    reduce_drain(T_OP, op_part, d_o.at[1])
    l_o[...] = reduce_end(T_OP, op_part, d_o.at[0], y_o).astype(BF).reshape(1024, col)
    gx_start(WO)

    def kv_grads(i):
        c = ds(i * 256, 256)
        total = jnp.zeros((256, 2 * col), F32)
        for p in range(3):
            for s in range(2):
                total += dot(unit[p, s, :, c], kv[s, pl.ds(p * seg, seg), :], 0, 0)
        act[c, pl.ds(col, 2 * col)] = total.astype(BF)
        act[c, pl.ds(0, col)] = (
            dot(unit[2, 0, :, c], qs[0], 0, 0) + dot(unit[2, 1, :, c], qs[1], 0, 0)
        ).astype(BF)

    loop(4, kv_grads)
    gx_start(QKV)

    def hidden_grads(i):
        s = lax.div(i, 4)
        c = ds(lax.rem(i, 4) * 256, 256)
        part = dot(kv[s, pl.ds(1024, seg), :], wqkv[c, pl.ds(col, 2 * col)], 1, 1) + dot(
            qs[s], wqkv[c, pl.ds(0, col)], 1, 1
        )
        gnp[ds(s * seg, seg), c] = part.astype(BF)

    loop(8, hidden_grads)
    for s in range(2):
        reduce_start(T_GN0 + s, rows_of(gnp, s), d_b.at[s, 1], d_b.at[s, 0])
    ld_h = load(hidden, gm_low, 13)
    w_cross_finish(CONV)
    gather_drain(T_GO, go_slot)
    ld_w = [
        load(conv_all.at[pl.ds(i * seg, seg)], go.at[i], 14 + i) for i in range(2)
    ]
    for s in range(2):
        out = reduce_end(T_OUT0 + s, rows_of(gpre, s), d_a.at[s, 0], y_a.at[s])
        reduce_drain(T_OUT0 + s, rows_of(gpre, s), d_a.at[s, 1])
        y_a[s] = (middle[s] + out).astype(BF)
    st_out = load(y_a, layer_out, 16)
    for s in range(2):
        reduce_mid(T_GN0 + s, rows_of(gnp, s), d_b.at[s, 1], y_b.at[s])
    for d in ld_w:
        d.wait()
    swap_drain(T_GA, ga_src)
    w_tap = lambda i, k: go[i, :, pl.ds(k * col, col)]

    def fresh(s, carry):
        taps = []
        for k in range(4):
            rows = memraw.at[s, 1 - k % 2]
            taps.append(
                dot(rows[:, pl.ds(0, seg)], w_tap(0, k)) + dot(rows[:, pl.ds(seg, seg)], w_tap(1, k))
            )
        at = lax.broadcasted_iota(jnp.int32, taps[0].shape, 0)
        total = taps[1] + taps[2]
        total += jnp.where(at == 0, 0.0, pltpu.roll(taps[0], 1, 0))
        total += jnp.where(at == 255, 0.0, pltpu.roll(taps[3], 255, 0))
        att_own[s, pl.ds(0, 256), :] = total.astype(BF)
        return carry

    lax.fori_loop(0, 2, fresh, 0)
    fr_src = lambda p: att_own.at[:, ds(p * 64, 64)]
    fr_dst = lambda p: fresh_out.at[:, :, ds(p * col, col)]
    swap_start(T_FR, fr_src, fr_dst)
    st_fr = load(fr_src(r), fr_dst(r), 17)

    for s in range(2):
        c = reduce_end(T_GN0 + s, rows_of(gnp, s), d_b.at[s, 0], y_b.at[s])
        if s == 0:
            ld_h.wait()
        u, inv = layer_norm(gm_low[s].astype(F32))
        gm[s] = gm[s] + norm_back(c, u, inv)
    st_gi = load(gm, grad_input, 18)
    gz_relay(UP)
    g_pass(CONV)
    gz_start(DOWN)
    g_final(UP, gain_f)
    gz_relay(DOWN)
    gz_start(WO)
    gz_start(QKV)
    g_pass(UP)
    gz_relay(WO)
    g_final(DOWN, None)
    gz_relay(QKV)
    g_final(WO, None)
    g_pass(DOWN)
    g_final(QKV, gain_a)
    g_pass(WO)
    g_pass(QKV)

    for p in range(3):
        tm_copy(ctx_src[p], ctx_slot[p](r), T_CTX0 + p, 0, r1).wait_send()
        tm_copy(ctx_src[p], ctx_slot[p](r), T_CTX0 + p, 1, r2).wait_send()
    swap_drain(T_GF, gf_src)
    gather_drain(T_WO, wo_slot)
    for s in range(2):
        reduce_drain(T_GN0 + s, rows_of(gnp, s), d_b.at[s, 1])
    swap_finish(T_FR, fr_dst)
    swap_drain(T_FR, fr_src)
    for d in (st_out, st_fr, st_gi):
        d.wait()
    w_drain(QKV)
    w_drain(WO)
    w_cross_drain(CONV)
    for g in range(5):
        g_drain(g)


def widen(*refs):
    ins, weights, outs = refs[:10], refs[10:14], refs[14:]
    for src, dst in zip(ins, outs):
        dst[...] = src[...].astype(dst.dtype)
    total = jnp.zeros(outs[10].shape, F32)
    for w, g in zip(weights[:3], ins[3:6]):
        total += jnp.sum(w[...].astype(F32) * g[...].astype(F32), axis=-1, keepdims=True)
    outs[10][...] = total
    outs[11][...] = jnp.sum(
        weights[3][...].astype(F32) * ins[7][...].astype(F32), axis=-1, keepdims=True
    )


def per_device(
    hidden,
    memory,
    compressed,
    reset_flag,
    boundary,
    query_weight,
    key_weight,
    value_weight,
    output_weight,
    up_weight,
    down_weight,
    conv_weight,
    attn_gain,
    ffn_gain,
    grad_out,
    grad_fresh,
):
    groups = lax.axis_size("stream")
    rank = lax.axis_index("tm")
    streams, seg_rows, width = hidden.shape
    own = query_weight.shape[0]
    seg = seg_rows * PARTS
    cols = width // PARTS
    n_z = groups // 2
    ff_rows = down_weight.shape[0] // PARTS
    pieces = groups if ff_rows % 128 == 0 else 1
    up_in = up_weight
    if pieces == 1:
        up_in = lax.dynamic_index_in_dim(
            up_weight.reshape(own, groups, PARTS, ff_rows), rank, 2, keepdims=False
        ).reshape(own, groups * ff_rows)
    gains = jnp.stack([attn_gain, ffn_gain])
    spots = np.arange(seg)
    places = np.concatenate([spots, seg + spots[::2], seg + spots[1::2], 2 * seg + spots])
    half = HEAD_DIM // 2
    frequency = 10000.0 ** (-np.arange(half) * 2.0 / HEAD_DIM)
    angles = places[:, None] * frequency[None, :]
    cosine = np.cos(angles).astype(np.float32)
    sine = np.sin(angles).astype(np.float32)
    cosines = np.concatenate([cosine, cosine], axis=1)
    sines = np.concatenate([-sine, sine], axis=1)

    hbm = pl.BlockSpec(memory_space=pl.ANY)
    vmem = pl.BlockSpec(memory_space=pltpu.VMEM)
    big = (seg * streams, width)
    out_shape = (
        jax.ShapeDtypeStruct(hidden.shape, BF),
        jax.ShapeDtypeStruct(grad_fresh.shape, BF),
        jax.ShapeDtypeStruct(hidden.shape, F32),
        jax.ShapeDtypeStruct((own, width), BF),
        jax.ShapeDtypeStruct((own, width), BF),
        jax.ShapeDtypeStruct((own, width), BF),
        jax.ShapeDtypeStruct((own, width), BF),
        jax.ShapeDtypeStruct((own, width * PARTS), BF),
        jax.ShapeDtypeStruct((PARTS * own, width), BF),
        jax.ShapeDtypeStruct((4, own, width), BF),
        jax.ShapeDtypeStruct((width, width), BF),
    )

    def v(shape, dtype=BF):
        return pltpu.VMEM(shape, dtype)

    seg2 = (streams, seg, cols)
    rows2 = (streams, seg_rows, width)
    wide = (3 * cols, cols, width, width, width)
    sem = pltpu.SemaphoreType.DMA
    scratch = (
        [
            v((3, streams, seg, width)),
            v((streams, 2, seg // 2, width)),
            v((width, 3 * cols)),
            v((width, width)),
            v(big),
            v(big),
            v(seg2),
            v((streams, 3 * seg, 2 * cols)),
            v((streams, 2, seg, 3 * seg)),
            v(seg2),
            v(rows2),
            v(rows2, F32),
            v((streams, seg, width)),
            v((streams, seg, width)),
            v((streams, seg // 2, cols)),
            v(big),
            v(big),
            v(seg2),
            v(rows2, F32),
            v(rows2),
            v(big),
            v((streams, 2, seg_rows, width)),
            v(rows2),
            v((streams, 2, seg_rows, width)),
            v(rows2),
            v((2, streams, seg, cols)),
            v(seg2),
            v((width, cols)),
            v(big),
        ]
        + [v((n_z * own, c)) for c in wide]
        + [v(((n_z - 1) * own, c)) for c in wide]
        + [v((own, c)) for c in wide]
        + [
            v((3 * seg, HEAD_DIM)),
            v((seg, HEAD_DIM)),
            v((own, 2), F32),
            v((streams, seg, 2), F32),
            v((streams, seg), F32),
            sem((18 + pieces,)),
            sem((T_COUNT, 3)),
            sem((T_COUNT, 3)),
            sem((5, 2 * n_z + 1)),
            sem((5, 2 * n_z + 1)),
            sem((5, n_z)),
            sem((5, n_z)),
            sem((5, n_z)),
            sem((5, n_z)),
            sem((9 + pieces, 3)),
            sem((9 + pieces, 3)),
            sem((9 + pieces,)),
        ]
    )
    results = pl.pallas_call(
        functools.partial(kernel, n_z, own, pieces),
        out_shape=out_shape,
        in_specs=[hbm] * 12 + [pl.BlockSpec(memory_space=pltpu.SMEM)] + [vmem] * 4,
        out_specs=tuple([hbm] * len(out_shape)),
        scratch_shapes=scratch,
        compiler_params=pltpu.CompilerParams(
            collective_id=0, has_side_effects=True, vmem_limit_bytes=64000 * 1024
        ),
        name="layer",
    )(
        hidden,
        memory,
        compressed,
        query_weight,
        key_weight,
        value_weight,
        output_weight,
        up_in,
        down_weight,
        conv_weight,
        grad_out,
        grad_fresh,
        reset_flag,
        boundary,
        gains,
        cosines,
        sines,
    )
    g_up = results[7]
    if pieces == 1:
        g_up = (
            g_up.reshape(own, PARTS, groups, ff_rows)
            .transpose(0, 2, 1, 3)
            .reshape(up_weight.shape)
        )
    steps = max(1, own // 32)
    moved = [*results[:7], g_up, *results[8:10]]
    weights = (query_weight, key_weight, value_weight, up_weight)

    def cut(t):
        shape = list(t.shape)
        dim = len(shape) - 2
        shape[dim] //= steps
        return pl.BlockSpec(tuple(shape), lambda i: (0,) * dim + (i, 0))

    out_types = (BF, BF) + (F32,) * 8
    sums = jax.ShapeDtypeStruct((own, 1), F32)
    done = pl.pallas_call(
        widen,
        grid=(steps,),
        out_shape=tuple(jax.ShapeDtypeStruct(t.shape, d) for t, d in zip(moved, out_types))
        + (sums, sums),
        in_specs=[cut(t) for t in moved] + [cut(t) for t in weights],
        out_specs=tuple([cut(t) for t in moved] + [cut(sums)] * 2),
        compiler_params=pltpu.CompilerParams(vmem_limit_bytes=64000 * 1024),
        name="widen",
    )(*moved, *weights)
    attn_gain_grad = done[10][:, 0] / attn_gain.astype(F32)
    ffn_gain_grad = done[11][:, 0] / ffn_gain.astype(F32)
    return tuple(done[:10]) + (attn_gain_grad, ffn_gain_grad)


def solution(mesh):
    act = P("stream", "tm", None)
    row = P("stream", None)
    in_specs = (act, act, act, P("stream"), row) + (row,) * 6 + (
        P(None, "stream", None),
        P("stream"),
        P("stream"),
        act,
        act,
    )
    out_specs = (act, act, act) + (row,) * 6 + (
        P(None, "stream", None),
        P("stream"),
        P("stream"),
    )
    return jax.shard_map(
        per_device, mesh=mesh, in_specs=in_specs, out_specs=out_specs, check_vma=False
    )
```

```python
import functools

import jax
import jax.numpy as jnp
import numpy as np
from jax import lax
from jax.experimental import pallas as pl
from jax.experimental.pallas import tpu as pltpu
from jax.sharding import PartitionSpec as P

HEAD_DIM = 128
PARTS = 4
BF = jnp.bfloat16
F32 = jnp.float32
MESH = pl.DeviceIdType.MESH

QKV, WO, UP, DOWN, CONV = range(5)
(T_CTX0, T_CTX1, T_CTX2, T_GO, T_GF, T_WO, T_ATT0, T_ATT1, T_NF0, T_NF1, T_GNF0, T_GNF1) = range(12)
(T_OUT0, T_OUT1, T_GA, T_OP, T_GN0, T_GN1, T_FR) = range(12, 19)
T_COUNT = 19


def dot(a, b, ca=1, cb=0):
    return lax.dot_general(a, b, (((ca,), (cb,)), ((), ())), preferred_element_type=F32)


def loop(n, body):
    def step(i, carry):
        body(i)
        return carry

    lax.fori_loop(0, n, step, 0)


def ds(start, size):
    return pl.ds(pl.multiple_of(start, size), size)


def mean(x):
    return jnp.sum(x, axis=-1, keepdims=True) * (1.0 / x.shape[-1])


def layer_norm(rows):
    center = rows - mean(rows)
    inv = lax.rsqrt(mean(center * center) + 1e-05)
    return center * inv, inv


def norm_back(c, unit, inv):
    return inv * (c - mean(c) - unit * mean(c * unit))


def kernel(
    n_z,
    own,
    pieces,
    hidden,
    memory,
    compressed,
    query_weight,
    key_weight,
    value_weight,
    output_weight,
    up_weight,
    down_weight,
    conv_weight,
    grad_out,
    grad_fresh,
    reset_flag,
    boundary,
    gains,
    cosines,
    sines,
    layer_out,
    fresh_out,
    grad_input,
    out_q,
    out_k,
    out_v,
    out_o,
    out_up,
    out_down,
    out_conv,
    conv_all,
    unit,
    memraw,
    wqkv,
    wo,
    up,
    down,
    qs,
    kv,
    probs,
    att_own,
    att_rows,
    middle,
    nf,
    go,
    gf,
    act,
    gpre,
    ga,
    gm,
    gm_low,
    gnp,
    d_a,
    y_a,
    d_b,
    y_b,
    d_o,
    y_o,
    l_o,
    l_conv,
    x_qkv,
    x_o,
    x_up,
    x_down,
    x_conv,
    z_qkv,
    z_o,
    z_up,
    z_down,
    z_conv,
    r_qkv,
    r_o,
    r_up,
    r_down,
    r_conv,
    t_v,
    t_q,
    gain_cols,
    row_info,
    doc_k,
    loc,
    tm_s,
    tm_r,
    ag_s,
    ag_r,
    rx_s,
    rx_r,
    rz_s,
    rz_r,
    fin_s,
    fin_r,
    fin_l,
):
    st = lax.axis_index("stream")
    r = lax.axis_index("tm")
    z = lax.div(st, 2)
    x = lax.rem(st, 2)
    core = lax.rem(r, 2)
    r1 = r + 1 - 2 * core
    r2 = lax.rem(r + 2, 4)
    r3 = lax.rem(r1 + 2, 4)
    xn = z * 2 + 1 - x
    seg = 512
    col = 256

    def zpeer(dz):
        return lax.rem(z + dz, n_z)

    def zfrom(dz):
        return lax.rem(z + n_z - dz, n_z)

    def load(src, dst, i):
        d = pltpu.make_async_copy(src, dst, loc.at[i])
        d.start()
        return d

    own_rows = ds(st * own, own)
    rcol = ds(r * col, col)
    ld_q = load(query_weight.at[:, rcol], wqkv.at[own_rows, pl.ds(0, col)], 0)
    ld_k = load(key_weight.at[:, rcol], wqkv.at[own_rows, pl.ds(col, col)], 1)
    ld_v = load(value_weight.at[:, rcol], wqkv.at[own_rows, pl.ds(2 * col, col)], 2)
    ld_o = load(output_weight.at[:, rcol], wo.at[own_rows, rcol], 3)
    if pieces > 1:
        size = 1024 // pieces
        ld_up = [
            load(
                up_weight.at[:, ds((i * PARTS + r) * size, size)],
                up.at[own_rows, pl.ds(i * size, size)],
                18 + i,
            )
            for i in range(pieces)
        ]
    else:
        ld_up = [load(up_weight, up.at[own_rows], 4)]
    ld_dn = load(down_weight.at[ds(r * own, own)], down.at[own_rows], 5)
    ld_cv = [
        load(conv_weight.at[k, :, rcol], conv_all.at[own_rows, pl.ds(k * col, col)], 6 + k)
        for k in range(4)
    ]
    tslot = ds(r * 128, 128)
    ld_m = load(memory, att_rows, 11)
    ld_c = {
        0: load(compressed, unit.at[0, :, tslot], 10),
        2: load(hidden, unit.at[2, :, tslot], 12),
    }
    ld_h = load(hidden, gm_low, 13)
    ld_go = load(grad_out, go.at[:, tslot], 14)
    ld_gf = load(grad_fresh.at[:, :, rcol], gf.at[:, ds(r * 64, 64)], 15)

    barrier = pltpu.get_barrier_semaphore()
    for peer in (r1, r2, r3):
        pl.semaphore_signal(barrier, 1, device_id=(st, peer), device_id_type=MESH)
    pl.semaphore_signal(barrier, 1, device_id=(xn, r), device_id_type=MESH)

    def greet(i):
        pl.semaphore_signal(
            barrier, 1, device_id=(zpeer(i + 1) * 2 + x, r), device_id_type=MESH
        )

    loop(n_z - 1, greet)
    pl.semaphore_wait(barrier, 4 + n_z - 1)

    def tm_copy(src, dst, op, i, peer):
        return pltpu.make_async_remote_copy(
            src, dst, tm_s.at[op, i], tm_r.at[op, i], device_id=(st, peer), device_id_type=MESH
        )

    def gather_start(op, src, slot):
        tm_copy(src, slot(r), op, 1, r2).start()
        tm_copy(src, slot(r), op, 0, r1).start()

    def gather_forward(op, slot):
        tm_copy(slot(r2), slot(r2), op, 1, r2).wait_recv()
        tm_copy(slot(r2), slot(r2), op, 2, r1).start()

    def gather_finish(op, slot):
        tm_copy(slot(r1), slot(r1), op, 0, r1).wait_recv()
        tm_copy(slot(r3), slot(r3), op, 2, r1).wait_recv()

    def gather_drain(op, slot):
        tm_copy(slot(r), slot(r), op, 0, r1).wait_send()
        tm_copy(slot(r), slot(r), op, 1, r2).wait_send()
        tm_copy(slot(r2), slot(r2), op, 2, r1).wait_send()

    peers = ((0, r1), (1, r2), (2, r3))

    def swap_start(op, src, dst):
        for i, p in peers[::-1]:
            tm_copy(src(p), dst(r), op, i, p).start()

    def swap_finish(op, dst):
        for i, p in peers:
            tm_copy(dst(p), dst(p), op, i, p).wait_recv()

    def swap_drain(op, src):
        for i, p in peers:
            tm_copy(src(p), src(p), op, i, p).wait_send()

    def reduce_start(op, part, far, near):
        tm_copy(part(r3), far, op, 0, r1).start()
        tm_copy(part(r1), near, op, 1, r1).start()

    def reduce_mid(op, part, far, land):
        tm_copy(far, far, op, 0, r1).wait_recv()
        far[...] = (far[...].astype(F32) + part(r2)[...].astype(F32)).astype(BF)
        tm_copy(far, land, op, 2, r2).start()

    def reduce_end(op, part, near, land):
        tm_copy(near, near, op, 1, r1).wait_recv()
        tm_copy(land, land, op, 2, r2).wait_recv()
        return part(r)[...].astype(F32) + near[...].astype(F32) + land[...].astype(F32)

    def reduce_drain(op, part, far):
        tm_copy(part(r3), far, op, 0, r1).wait_send()
        tm_copy(part(r1), far, op, 1, r1).wait_send()
        tm_copy(far, far, op, 2, r2).wait_send()

    held = {
        QKV: wqkv,
        WO: wo.at[:, rcol],
        UP: up,
        DOWN: down,
        CONV: conv_all,
    }

    def wslot(g, s):
        return held[g].at[ds(s * own, own)]

    def w_copy(g, s, i, dev, j=None):
        return pltpu.make_async_remote_copy(
            wslot(g, s),
            wslot(g, s),
            ag_s.at[g, i],
            ag_r.at[g, i if j is None else j],
            device_id=(dev, r),
            device_id_type=MESH,
        )

    relay = n_z == 4
    inner = (z == 1) | (z == 2)

    def direct(dz):
        zz = zpeer(dz)
        return (z + 3 != zz) & (zz + 3 != z)

    def w_send_x(g):
        w_copy(g, st, 0, xn).start()

    def w_send_z(g):
        if relay:
            for dz in (2, 1, 3):

                @pl.when(direct(dz))
                def _():
                    w_copy(g, st, dz, zpeer(dz) * 2 + x).start()
        else:
            loop(n_z - 1, lambda i: w_copy(g, st, i + 1, zpeer(i + 1) * 2 + x).start())

    def w_pass(g, dz):
        s = zfrom(dz) * 2 + x
        w_copy(g, s, dz, st).wait_recv()
        w_copy(g, s, n_z + dz - 1, xn).start()

    def w_relay(g):
        s = zfrom(2) * 2 + x
        return w_copy(g, s, 2 * n_z - 1, 3 * (z - 1) * 2 + x, 2 * z - 1)

    last = jnp.where(z == 0, 1, 3)

    def w_forward(g):
        if relay:
            s = zfrom(2) * 2 + x
            w_copy(g, s, 2, st).wait_recv()

            @pl.when(inner)
            def _():
                w_relay(g).start()

            w_copy(g, s, n_z + 1, xn).start()
            w_pass(g, 4 - last)
        else:
            loop(n_z - 1, lambda i: w_pass(g, i + 1))

    def w_forward_last(g):
        if relay:
            w_pass(g, last)

    def w_cross(g):
        w_copy(g, xn, 0, xn).wait_recv()
        if relay:
            for dz in (2, 1, 3):

                @pl.when(direct(dz))
                def _():
                    w_copy(g, xn, n_z + dz - 1, zpeer(dz) * 2 + x).start()
        else:
            loop(n_z - 1, lambda i: w_copy(g, xn, n_z + i, zpeer(i + 1) * 2 + x).start())

    def w_relay_cross(g):
        s = zfrom(2) * 2 + 1 - x
        return w_copy(g, s, 2 * n_z, 3 * (z - 1) * 2 + x, n_z + 2 * z - 2)

    def w_cross_pass(g):
        if relay:
            w_copy(g, zfrom(2) * 2 + x, 2, st).wait_recv()
            w_copy(g, zfrom(2) * 2 + 1 - x, n_z + 1, st).wait_recv()

            @pl.when(inner)
            def _():
                w_relay(g).start()
                w_relay_cross(g).start()

    def w_cross_finish(g):
        rest = (1, 3) if relay else range(1, n_z)
        for dz in rest:
            w_copy(g, zfrom(dz) * 2 + x, dz, st).wait_recv()
            w_copy(g, zfrom(dz) * 2 + 1 - x, n_z + dz - 1, st).wait_recv()

    def w_cross_drain(g):
        w_copy(g, st, 0, xn).wait_send()
        for dz in range(1, n_z):
            if relay:

                @pl.when(direct(dz))
                def _():
                    w_copy(g, st, dz, xn).wait_send()
                    w_copy(g, st, n_z + dz - 1, xn).wait_send()
            else:
                w_copy(g, st, dz, xn).wait_send()
                w_copy(g, st, n_z + dz - 1, xn).wait_send()
        if relay:

            @pl.when(inner)
            def _():
                w_relay(g).wait_send()
                w_relay_cross(g).wait_send()

    def w_finish(g):
        w_copy(g, xn, 0, xn).wait_recv()
        loop(n_z - 1, lambda i: w_copy(g, zfrom(i + 1) * 2 + 1 - x, n_z + i, xn).wait_recv())

    def w_drain(g):
        w_copy(g, st, 0, xn).wait_send()
        loop(n_z - 1, lambda i: w_copy(g, st, n_z + i, xn).wait_send())
        if relay:
            for dz in (1, 2, 3):

                @pl.when(direct(dz))
                def _():
                    w_copy(g, st, dz, xn).wait_send()

            @pl.when(inner)
            def _():
                w_relay(g).wait_send()
        else:
            loop(n_z - 1, lambda i: w_copy(g, st, i + 1, xn).wait_send())

    x_buf = {QKV: x_qkv, WO: x_o, UP: x_up, DOWN: x_down, CONV: x_conv}
    r_buf = {QKV: r_qkv, WO: r_o, UP: r_up, DOWN: r_down, CONV: r_conv}
    z_buf = {QKV: z_qkv, WO: z_o, UP: z_up, DOWN: z_down, CONV: z_conv}
    grads = {QKV: act.at[:, pl.ds(0, 3 * col)], WO: l_o, UP: up, DOWN: down, CONV: l_conv}

    def gx_copy(g, zz):
        return pltpu.make_async_remote_copy(
            grads[g].at[ds((zz * 2 + 1 - x) * own, own)],
            x_buf[g].at[ds(zz * own, own)],
            rx_s.at[g, zz],
            rx_r.at[g, zz],
            device_id=(xn, r),
            device_id_type=MESH,
        )

    def gx_start(g):
        if relay:
            for dz in (1, 3, 2, 0):
                gx_copy(g, zpeer(dz)).start()
        else:
            loop(n_z, lambda i: gx_copy(g, zpeer(i + 1)).start())

    def gz_copy(g, dz, zz):
        return pltpu.make_async_remote_copy(
            x_buf[g].at[ds(zz * own, own)],
            z_buf[g].at[ds((dz - 1) * own, own)],
            rz_s.at[g, dz],
            rz_r.at[g, dz],
            device_id=(zz * 2 + x, r),
            device_id_type=MESH,
        )

    def gz_fold(g, zz):
        gx_copy(g, zz).wait_recv()
        rows = ds(zz * own, own)
        x_buf[g][rows] = (
            x_buf[g][rows].astype(F32) + grads[g][ds((zz * 2 + x) * own, own)].astype(F32)
        ).astype(BF)

    def gz_far(g, dz, zz):
        return pltpu.make_async_remote_copy(
            x_buf[g].at[ds(zz * own, own)],
            r_buf[g],
            rz_s.at[g, dz],
            rz_r.at[g, 0],
            device_id=(jnp.where(z == 0, 1, 2) * 2 + x, r),
            device_id_type=MESH,
        )

    def gz_start(g):
        if not relay:

            def one(i):
                zz = zpeer(i + 1)
                gz_fold(g, zz)
                gz_copy(g, i + 1, zz).start()

            loop(n_z - 1, one)
            return
        for dz in (1, 3):
            zz = zpeer(dz)
            gz_fold(g, zz)

            @pl.when(direct(dz))
            def _():
                gz_copy(g, dz, zz).start()

            @pl.when(jnp.logical_not(direct(dz)))
            def _():
                gz_far(g, dz, zz).start()

        @pl.when(jnp.logical_not(inner))
        def _():
            gz_fold(g, zpeer(2))
            gz_copy(g, 2, zpeer(2)).start()

    def gz_relay(g):
        if relay:

            @pl.when(inner)
            def _():
                zz = zpeer(2)
                gz_fold(g, zz)
                gz_far(g, 2, zz).wait_recv()
                rows = ds(zz * own, own)
                x_buf[g][rows] = (x_buf[g][rows].astype(F32) + r_buf[g][...].astype(F32)).astype(BF)
                gz_copy(g, 2, zz).start()

    outs = {
        WO: (((0, col), lambda p: out_o.at[:, ds(p * col, col)]),),
        QKV: (
            ((0, col), lambda p: out_q.at[:, ds(p * col, col)]),
            ((col, col), lambda p: out_k.at[:, ds(p * col, col)]),
            ((2 * col, col), lambda p: out_v.at[:, ds(p * col, col)]),
        ),
        UP: tuple(
            (
                (i * (1024 // pieces), 1024 // pieces),
                (lambda i: lambda p: out_up.at[:, ds((i * PARTS + p) * (1024 // pieces), 1024 // pieces)])(i),
            )
            for i in range(pieces)
        ),
        DOWN: (((0, 1024), lambda p: out_down.at[ds(p * own, own)]),),
        CONV: tuple(
            ((k * col, col), (lambda k: lambda p: out_conv.at[k, :, ds(p * col, col)])(k))
            for k in range(4)
        ),
    }
    fin_base = {QKV: 0, WO: 3, DOWN: 4, CONV: 5, UP: 9}

    def fin_copy(g, j, i, p, slot_rank):
        (lane, size), slot = outs[g][j]
        n = fin_base[g] + j
        return pltpu.make_async_remote_copy(
            x_buf[g].at[ds(z * own, own), pl.ds(lane, size)],
            slot(slot_rank),
            fin_s.at[n, i],
            fin_r.at[n, i],
            device_id=(st, p),
            device_id_type=MESH,
        )

    def g_keep(g, j):
        (lane, size), slot = outs[g][j]
        return pltpu.make_async_copy(
            x_buf[g].at[ds(z * own, own), pl.ds(lane, size)], slot(r), fin_l.at[fin_base[g] + j]
        )

    def g_final(g, gain):
        gx_copy(g, z).wait_recv()
        rows = ds(z * own, own)
        total = x_buf[g][rows].astype(F32) + grads[g][ds((z * 2 + x) * own, own)].astype(F32)
        for dz in range(1, n_z):
            if relay:

                @pl.when(direct(n_z - dz))
                def _():
                    gz_copy(g, dz, zpeer(dz)).wait_recv()
            else:
                gz_copy(g, dz, zpeer(dz)).wait_recv()
            total = total + z_buf[g][pl.ds((dz - 1) * own, own)].astype(F32)
        if gain is not None:
            total = total * gain
        x_buf[g][rows] = total.astype(BF)
        for j in range(len(outs[g])):
            fin_copy(g, j, 1, r2, r).start()
            fin_copy(g, j, 0, r1, r).start()
            g_keep(g, j).start()

    def fin_pass(g, j):
        slot = outs[g][j][1](r2)
        n = fin_base[g] + j
        return pltpu.make_async_remote_copy(
            slot, slot, fin_s.at[n, 2], fin_r.at[n, 2], device_id=(st, r1), device_id_type=MESH
        )

    def g_pass(g):
        for j in range(len(outs[g])):
            fin_copy(g, j, 1, r2, r2).wait_recv()
            fin_pass(g, j).start()

    def g_drain(g):
        loop(n_z, lambda i: gx_copy(g, i).wait_send())
        loop(n_z - 1, lambda i: gz_copy(g, i + 1, zpeer(i + 1)).wait_send())
        for j in range(len(outs[g])):
            fin_copy(g, j, 0, r1, r1).wait()
            fin_copy(g, j, 1, r2, r).wait_send()
            fin_pass(g, j).wait()
            g_keep(g, j).wait()

    ctx_slot = (
        lambda p: unit.at[0, :, ds(p * 128, 128)],
        lambda p: memraw.at[:, :, ds(p * 64, 64)],
        lambda p: unit.at[2, :, ds(p * 128, 128)],
    )
    gather_start(T_CTX0, compressed, ctx_slot[0])
    for d in (ld_q, ld_k, ld_v):
        d.wait()
    eye = lax.broadcasted_iota(jnp.int32, (own, own), 0) == lax.broadcasted_iota(
        jnp.int32, (own, own), 1
    )
    gain_cols[...] = dot(eye.astype(F32).astype(BF), gains[...], 1, 1)
    gain_a = gain_cols[:, 0:1]
    gain_f = gain_cols[:, 1:2]
    wqkv[own_rows] = (wqkv[own_rows].astype(F32) * gain_a).astype(BF)
    w_send_x(QKV)
    w_send_z(QKV)
    ld_m.wait()
    row = lax.broadcasted_iota(jnp.int32, (128, 128), 0)
    source = 2 * lax.rem(row, 64) + lax.div(row, 64)
    pick = (lax.broadcasted_iota(jnp.int32, (128, 128), 1) == source).astype(F32).astype(BF)
    for s in range(2):
        split = dot(pick, att_rows[s]).astype(BF)
        memraw[s, 0, ds(r * 64, 64), :] = split[:64]
        memraw[s, 1, ds(r * 64, 64), :] = split[64:]
    gather_start(T_CTX1, ctx_slot[1](r), ctx_slot[1])
    gather_start(T_CTX2, hidden, ctx_slot[2])
    ctx_src = (compressed, ctx_slot[1](r), hidden)
    gf_src = lambda p: grad_fresh.at[:, :, ds(p * col, col)]
    gf_dst = lambda p: gf.at[:, ds(p * 64, 64)]
    swap_start(T_GF, gf_src, gf_dst)
    ld_o.wait()
    w_send_x(WO)
    w_send_z(WO)
    for d in ld_up:
        d.wait()
    up[own_rows] = (up[own_rows].astype(F32) * gain_f).astype(BF)
    w_send_z(UP)
    ld_dn.wait()
    w_send_z(DOWN)
    if relay:
        for end, dz in ((0, 1), (3, 3)):

            @pl.when(z == end)
            def _():
                for g in range(5):
                    z_buf[g][pl.ds((dz - 1) * own, own)] = jnp.zeros((own, z_buf[g].shape[1]), BF)

    before = lax.broadcasted_iota(jnp.int32, (seg, seg), 1) <= lax.broadcasted_iota(
        jnp.int32, (seg, seg), 0
    )
    before = before.astype(F32).astype(BF)
    starts = boundary[...].astype(F32).astype(BF)
    docs = dot(before, starts, 1, 1)
    doc_k[...] = dot(starts, before, 1, 1)
    for s in range(2):
        row_info[s, :, 0:1] = docs[:, s : s + 1]
        away = docs[:, s : s + 1] + reset_flag[s].astype(F32)
        row_info[s, :, 1:2] = jnp.where(away == 0.0, 0.0, -1e30)

    def norm_block(p, rank):
        def one(s):
            if p == 1:
                for half in range(2):
                    raw = memraw[s, half, ds(rank * 64, 64), :]
                    unit[p, s, ds(half * 256 + rank * 64, 64), :] = layer_norm(raw.astype(F32))[
                        0
                    ].astype(BF)
            else:
                rows = ds(rank * 128, 128)
                unit[p, s, rows, :] = layer_norm(unit[p, s, rows, :].astype(F32))[0].astype(BF)

        loop(2, one)

    def context(p, meanwhile=None):
        op, slot = T_CTX0 + p, ctx_slot[p]
        if p in ld_c:
            ld_c[p].wait()
        norm_block(p, r)
        gather_forward(op, slot)
        if meanwhile is not None:
            meanwhile()
        tm_copy(slot(r1), slot(r1), op, 0, r1).wait_recv()
        norm_block(p, r1)
        tm_copy(slot(r3), slot(r3), op, 2, r1).wait_recv()
        norm_block(p, r3)
        tm_copy(slot(r2), slot(r2), op, 2, r1).wait_send()
        norm_block(p, r2)

    def project(p):
        def one(i):
            s = lax.div(i, 2)
            at = lax.rem(i, 2) * 256
            rows = ds(at, 256)
            place = pl.ds(pl.multiple_of(p * seg + at, 256), 256)
            a = unit[p, s, rows, :]
            cs = cosines[place, :]
            sn = sines[place, :]

            def rot(t):
                return t * cs + pltpu.roll(t, 64, 1) * sn

            both = dot(a, wqkv[:, pl.ds(col, 2 * col)])
            for h in range(2):
                kv[s, place, pl.ds(h * 128, 128)] = rot(both[:, h * 128 : h * 128 + 128]).astype(BF)
            kv[s, place, pl.ds(col, col)] = both[:, col:].astype(BF)
            if p == 2:
                q = dot(a, wqkv[:, pl.ds(0, col)])
                for h in range(2):
                    qs[s, rows, pl.ds(h * 128, 128)] = (
                        rot(q[:, h * 128 : h * 128 + 128]) * HEAD_DIM ** (-0.5)
                    ).astype(BF)

        loop(4, one)

    context(0)
    w_forward(QKV)
    w_forward(WO)
    for d in ld_cv:
        d.wait()
    w_send_x(CONV)
    w_send_z(CONV)
    context(1)
    w_forward_last(QKV)
    w_forward_last(WO)
    w_send_x(UP)
    w_send_x(DOWN)
    w_finish(QKV)
    project(0)
    project(1)
    w_forward(UP)
    w_cross(CONV)
    wo_slot = lambda p: wo.at[:, ds(p * col, col)]
    go_slot = lambda p: go.at[:, ds(p * 128, 128)]

    def gather_wo():
        w_finish(WO)
        gather_start(T_WO, wo_slot(r), wo_slot)

    context(2, gather_wo)
    w_forward_last(UP)
    project(2)

    ld_gf.wait()
    swap_finish(T_GF, gf_dst)

    def conv_grads(i):
        c = ds(i * 256, 256)
        even_acc = jnp.zeros((256, 512), F32)
        odd_acc = jnp.zeros((256, 512), F32)
        for s in range(2):
            g = gf[s].astype(F32)
            at = lax.broadcasted_iota(jnp.int32, g.shape, 0)
            ahead = jnp.where(at == 255, 0.0, pltpu.roll(g, 255, 0))
            behind = jnp.where(at == 0, 0.0, pltpu.roll(g, 1, 0))
            low = gf[s]
            odd_acc += dot(memraw[s, 1, :, c], jnp.concatenate([ahead.astype(BF), low], 1), 0, 0)
            even_acc += dot(memraw[s, 0, :, c], jnp.concatenate([low, behind.astype(BF)], 1), 0, 0)
        l_conv[c, pl.ds(0, col)] = odd_acc[:, :col].astype(BF)
        l_conv[c, pl.ds(col, col)] = even_acc[:, :col].astype(BF)
        l_conv[c, pl.ds(2 * col, col)] = odd_acc[:, col:].astype(BF)
        l_conv[c, pl.ds(3 * col, col)] = even_acc[:, col:].astype(BF)

    loop(4, conv_grads)

    def attend(s):
        def one(qt):
            rows = ds(qt * 128, 128)
            shape = (128, seg)
            below = lax.broadcasted_iota(jnp.int32, shape, 1) <= (
                lax.broadcasted_iota(jnp.int32, shape, 0) + qt * 128
            )
            info = row_info[s, rows, :]
            same = doc_k[pl.ds(s, 1), :] == info[:, 0:1]
            seen = below & same
            bias = info[:, 1:2]
            for h in range(2):
                lanes = pl.ds(h * 128, 128)
                q = qs[s, rows, lanes]
                far = dot(q, kv[s, pl.ds(0, 1024), lanes], 1, 1) + bias
                near = jnp.where(seen, dot(q, kv[s, pl.ds(1024, seg), lanes], 1, 1), -1e30)
                top = jnp.maximum(
                    jnp.max(far, axis=-1, keepdims=True), jnp.max(near, axis=-1, keepdims=True)
                )
                far = jnp.exp(far - top)
                near = jnp.exp(near - top)
                inv = 1.0 / (
                    jnp.sum(far, axis=-1, keepdims=True) + jnp.sum(near, axis=-1, keepdims=True)
                )
                far = (far * inv).astype(BF)
                near = (near * inv).astype(BF)
                probs[s, h, rows, pl.ds(0, 1024)] = far
                probs[s, h, rows, pl.ds(1024, seg)] = near
                vl = pl.ds(col + h * 128, 128)
                o = dot(far, kv[s, pl.ds(0, 1024), vl]) + dot(near, kv[s, pl.ds(1024, seg), vl])
                att_own[s, rows, lanes] = o.astype(BF)

        loop(4, one)

    att_src = lambda s: lambda p: att_own.at[s, ds(p * 128, 128)]
    att_dst = lambda s: lambda p: att_rows.at[s, :, ds(p * col, col)]

    def attend_send(s):
        swap_start(T_ATT0 + s, att_src(s), att_dst(s))
        att_rows[s, :, rcol] = att_own[s, tslot, :]

    gather_start(T_GO, grad_out, go_slot)
    attend(0)
    attend_send(0)
    w_forward(DOWN)
    gather_forward(T_WO, wo_slot)
    attend(1)
    attend_send(1)
    w_forward_last(DOWN)
    gx_start(CONV)
    gather_forward(T_GO, go_slot)

    swap_finish(T_ATT0, att_dst(0))
    swap_finish(T_ATT1, att_dst(1))
    gather_finish(T_WO, wo_slot)
    ld_h.wait()

    def project_out(i):
        c = ds(i * 256, 256)
        mid = dot(att_rows[...].reshape(256, 1024), wo[:, c]).reshape(2, 128, 256)
        middle[:, :, c] = gm_low[:, :, c].astype(F32) + mid

    loop(4, project_out)
    nf_slot = lambda s: lambda p: nf.at[s, ds(p * 128, 128)]
    for s in range(2):
        nf[s, tslot, :] = layer_norm(middle[s])[0].astype(BF)
        gather_start(T_NF0 + s, nf_slot(s)(r), nf_slot(s))
    ld_go.wait()
    for s in range(2):
        gather_forward(T_NF0 + s, nf_slot(s))
    gather_finish(T_GO, go_slot)
    w_finish(UP)
    w_finish(DOWN)

    def ffn(s):
        def one(i):
            c = ds(i * 256, 256)
            pre = dot(nf[s], up[:, c])
            g_act = dot(go[s], down[c, :], 1, 1)
            phi = 0.5 + 0.5 * lax.erf(pre * 0.7071067811865476)
            act[pl.ds(s * seg, seg), c] = (pre * phi).astype(BF)
            slope = phi + pre * (jnp.exp(pre * pre * -0.5) * 0.3989422804014327)
            gpre[pl.ds(s * seg, seg), c] = (g_act * slope).astype(BF)

        loop(4, one)

        def back(i):
            c = ds(i * 256, 256)
            gnp[pl.ds(s * seg, seg), c] = dot(
                gpre[pl.ds(s * seg, seg), :], up[c, :], 1, 1
            ).astype(BF)

        loop(4, back)

    def rows_of(buf, s):
        return lambda p: buf.at[pl.ds(pl.multiple_of(s * seg + p * 128, 128), 128)]

    for s in range(2):
        gather_finish(T_NF0 + s, nf_slot(s))
        ffn(s)
        reduce_start(T_GNF0 + s, rows_of(gnp, s), d_b.at[s, 1], d_b.at[s, 0])
    for s in range(2):
        reduce_mid(T_GNF0 + s, rows_of(gnp, s), d_b.at[s, 1], y_b.at[s])
    w_cross_pass(CONV)

    w_drain(UP)
    nf2 = nf

    def up_grads(i):
        c = ds(i * 256, 256)
        up[c, :] = (
            dot(nf2[0, :, c], gpre[pl.ds(0, seg), :], 0, 0)
            + dot(nf2[1, :, c], gpre[pl.ds(seg, seg), :], 0, 0)
        ).astype(BF)

    loop(4, up_grads)
    gx_start(UP)
    gz_start(CONV)

    for s in range(2):
        c = reduce_end(T_GNF0 + s, rows_of(gnp, s), d_b.at[s, 0], y_b.at[s])
        u, inv = layer_norm(middle[s])
        g = go[s, tslot, :].astype(F32) + norm_back(c, u, inv)
        gm[s] = g
        gm_low[s] = g.astype(BF)
        reduce_drain(T_GNF0 + s, rows_of(gnp, s), d_b.at[s, 1])
    for s in range(2):
        swap_drain(T_ATT0 + s, att_src(s))

    def attended_grads(i):
        part = dot(gm_low[...].reshape(256, 1024), wo[ds(i * 256, 256), :], 1, 1)
        att_own[:, ds(i * 128, 128), :] = part.astype(BF).reshape(2, 128, col)

    loop(4, attended_grads)
    ga_src = lambda p: att_own.at[:, ds(p * 128, 128)]
    ga_dst = lambda p: ga.at[:, ds(p * 128, 128)]
    swap_start(T_GA, ga_src, ga_dst)
    ga[:, tslot, :] = att_own[:, tslot, :]
    for s in range(2):
        gather_drain(T_NF0 + s, nf_slot(s))

    def output_grads(i):
        c = ds(i * 256, 256)
        part = dot(att_rows[:, :, c].reshape(256, 256), gm_low[...].reshape(256, 1024), 0, 0)
        nf[lax.div(i, 2), ds(lax.rem(i, 2) * 256, 256), :] = part.astype(BF)

    loop(4, output_grads)
    op_part = lambda p: nf.at[:, :, ds(p * col, col)]
    reduce_start(T_OP, op_part, d_o.at[1], d_o.at[0])

    def out_parts(i):
        s = lax.div(i, 4)
        rows = ds(s * seg, seg)
        c = ds(lax.rem(i, 4) * 256, 256)
        gpre[rows, c] = dot(act[rows, :], down[:, c]).astype(BF)

    loop(8, out_parts)
    for s in range(2):
        reduce_start(T_OUT0 + s, rows_of(gpre, s), d_a.at[s, 1], d_a.at[s, 0])
    w_drain(DOWN)

    def down_grads(i):
        c = ds(i * 256, 256)
        down[c, :] = (
            dot(act[pl.ds(0, seg), c], go[0], 0, 0) + dot(act[pl.ds(seg, seg), c], go[1], 0, 0)
        ).astype(BF)

    loop(4, down_grads)
    gx_start(DOWN)
    gz_relay(CONV)
    swap_finish(T_GA, ga_dst)

    def attend_back(s, h):
        if True:
            lanes = pl.ds(h * 128, 128)
            vl = pl.ds(col + h * 128, 128)

            def values(i):
                c = ds(i * 512, 512)
                t_v[c, :] = dot(probs[s, h, :, c], ga[s, :, lanes], 0, 0).astype(BF)

            loop(3, values)

            def scores(i):
                rows = ds(i * 128, 128)
                p = probs[s, h, rows, :].astype(F32)
                gp = dot(ga[s, rows, lanes], kv[s, :, vl], 1, 1)
                inner = jnp.sum(p * gp, axis=-1, keepdims=True)
                gs = (p * (gp - inner)).astype(BF)
                probs[s, h, rows, :] = gs
                place = pl.ds(pl.multiple_of(1024 + i * 128, 128), 128)
                t = dot(gs, kv[s, :, lanes])
                t = t * cosines[place, :] - pltpu.roll(t, 64, 1) * sines[place, :]
                t_q[rows, :] = (t * HEAD_DIM ** (-0.5)).astype(BF)

            loop(4, scores)

            def keys(i):
                c = ds(i * 512, 512)
                t = dot(probs[s, h, :, c], qs[s, :, lanes], 0, 0)
                t = t * cosines[c, :] - pltpu.roll(t, 64, 1) * sines[c, :]
                kv[s, c, lanes] = t.astype(BF)
                kv[s, c, vl] = t_v[c, :]

            loop(3, keys)
            qs[s, :, lanes] = t_q[...]

    attend_back(0, 0)
    reduce_mid(T_OP, op_part, d_o.at[1], y_o)
    gz_start(UP)
    attend_back(0, 1)
    for s in range(2):
        reduce_mid(T_OUT0 + s, rows_of(gpre, s), d_a.at[s, 1], y_a.at[s])
    g_final(CONV, None)
    attend_back(1, 0)
    gz_relay(UP)
    attend_back(1, 1)
    gz_start(DOWN)

    reduce_drain(T_OP, op_part, d_o.at[1])
    l_o[...] = reduce_end(T_OP, op_part, d_o.at[0], y_o).astype(BF).reshape(1024, col)
    gx_start(WO)

    def kv_grads(i):
        c = ds(i * 256, 256)
        total = jnp.zeros((256, 2 * col), F32)
        for p in range(3):
            for s in range(2):
                total += dot(unit[p, s, :, c], kv[s, pl.ds(p * seg, seg), :], 0, 0)
        act[c, pl.ds(col, 2 * col)] = total.astype(BF)
        act[c, pl.ds(0, col)] = (
            dot(unit[2, 0, :, c], qs[0], 0, 0) + dot(unit[2, 1, :, c], qs[1], 0, 0)
        ).astype(BF)

    loop(4, kv_grads)
    gx_start(QKV)
    g_final(UP, gain_f)
    gz_relay(DOWN)

    def hidden_grads(i):
        s = lax.div(i, 4)
        c = ds(lax.rem(i, 4) * 256, 256)
        part = dot(kv[s, pl.ds(1024, seg), :], wqkv[c, pl.ds(col, 2 * col)], 1, 1) + dot(
            qs[s], wqkv[c, pl.ds(0, col)], 1, 1
        )
        gnp[ds(s * seg, seg), c] = part.astype(BF)

    loop(8, hidden_grads)
    for s in range(2):
        reduce_start(T_GN0 + s, rows_of(gnp, s), d_b.at[s, 1], d_b.at[s, 0])
    ld_h = load(hidden, gm_low, 13)
    g_pass(CONV)
    for s in range(2):
        reduce_mid(T_GN0 + s, rows_of(gnp, s), d_b.at[s, 1], y_b.at[s])
    gz_start(WO)
    gz_relay(WO)
    w_cross_finish(CONV)
    gather_drain(T_GO, go_slot)
    ld_w = [
        load(conv_all.at[pl.ds(i * seg, seg)], go.at[i], 14 + i) for i in range(2)
    ]
    for s in range(2):
        out = reduce_end(T_OUT0 + s, rows_of(gpre, s), d_a.at[s, 0], y_a.at[s])
        reduce_drain(T_OUT0 + s, rows_of(gpre, s), d_a.at[s, 1])
        y_a[s] = (middle[s] + out).astype(BF)
    st_out = load(y_a, layer_out, 16)
    for d in ld_w:
        d.wait()
    swap_drain(T_GA, ga_src)
    w_tap = lambda i, k: go[i, :, pl.ds(k * col, col)]

    def fresh(s, carry):
        taps = []
        for k in range(4):
            rows = memraw.at[s, 1 - k % 2]
            taps.append(
                dot(rows[:, pl.ds(0, seg)], w_tap(0, k)) + dot(rows[:, pl.ds(seg, seg)], w_tap(1, k))
            )
        at = lax.broadcasted_iota(jnp.int32, taps[0].shape, 0)
        total = taps[1] + taps[2]
        total += jnp.where(at == 0, 0.0, pltpu.roll(taps[0], 1, 0))
        total += jnp.where(at == 255, 0.0, pltpu.roll(taps[3], 255, 0))
        att_own[s, pl.ds(0, 256), :] = total.astype(BF)
        return carry

    lax.fori_loop(0, 2, fresh, 0)
    fr_src = lambda p: att_own.at[:, ds(p * 64, 64)]
    fr_dst = lambda p: fresh_out.at[:, :, ds(p * col, col)]
    swap_start(T_FR, fr_src, fr_dst)
    st_fr = load(fr_src(r), fr_dst(r), 17)
    gz_start(QKV)
    g_pass(UP)
    g_final(DOWN, None)
    gz_relay(QKV)

    for s in range(2):
        c = reduce_end(T_GN0 + s, rows_of(gnp, s), d_b.at[s, 0], y_b.at[s])
        if s == 0:
            ld_h.wait()
        u, inv = layer_norm(gm_low[s].astype(F32))
        gm[s] = gm[s] + norm_back(c, u, inv)
    st_gi = load(gm, grad_input, 18)
    g_final(WO, None)
    g_pass(DOWN)
    g_final(QKV, gain_a)
    g_pass(WO)
    g_pass(QKV)

    for p in range(3):
        tm_copy(ctx_src[p], ctx_slot[p](r), T_CTX0 + p, 0, r1).wait_send()
        tm_copy(ctx_src[p], ctx_slot[p](r), T_CTX0 + p, 1, r2).wait_send()
    swap_drain(T_GF, gf_src)
    gather_drain(T_WO, wo_slot)
    for s in range(2):
        reduce_drain(T_GN0 + s, rows_of(gnp, s), d_b.at[s, 1])
    swap_finish(T_FR, fr_dst)
    swap_drain(T_FR, fr_src)
    for d in (st_out, st_fr, st_gi):
        d.wait()
    w_drain(QKV)
    w_drain(WO)
    w_cross_drain(CONV)
    for g in range(5):
        g_drain(g)


def widen(*refs):
    ins, weights, outs = refs[:10], refs[10:14], refs[14:]
    for src, dst in zip(ins, outs):
        dst[...] = src[...].astype(dst.dtype)
    total = jnp.zeros(outs[10].shape, F32)
    for w, g in zip(weights[:3], ins[3:6]):
        total += jnp.sum(w[...].astype(F32) * g[...].astype(F32), axis=-1, keepdims=True)
    outs[10][...] = total
    outs[11][...] = jnp.sum(
        weights[3][...].astype(F32) * ins[7][...].astype(F32), axis=-1, keepdims=True
    )


def per_device(
    hidden,
    memory,
    compressed,
    reset_flag,
    boundary,
    query_weight,
    key_weight,
    value_weight,
    output_weight,
    up_weight,
    down_weight,
    conv_weight,
    attn_gain,
    ffn_gain,
    grad_out,
    grad_fresh,
):
    groups = lax.axis_size("stream")
    rank = lax.axis_index("tm")
    streams, seg_rows, width = hidden.shape
    own = query_weight.shape[0]
    seg = seg_rows * PARTS
    cols = width // PARTS
    n_z = groups // 2
    ff_rows = down_weight.shape[0] // PARTS
    pieces = groups if ff_rows % 128 == 0 else 1
    up_in = up_weight
    if pieces == 1:
        up_in = lax.dynamic_index_in_dim(
            up_weight.reshape(own, groups, PARTS, ff_rows), rank, 2, keepdims=False
        ).reshape(own, groups * ff_rows)
    gains = jnp.stack([attn_gain, ffn_gain])
    spots = np.arange(seg)
    places = np.concatenate([spots, seg + spots[::2], seg + spots[1::2], 2 * seg + spots])
    half = HEAD_DIM // 2
    frequency = 10000.0 ** (-np.arange(half) * 2.0 / HEAD_DIM)
    angles = places[:, None] * frequency[None, :]
    cosine = np.cos(angles).astype(np.float32)
    sine = np.sin(angles).astype(np.float32)
    cosines = np.concatenate([cosine, cosine], axis=1)
    sines = np.concatenate([-sine, sine], axis=1)

    hbm = pl.BlockSpec(memory_space=pl.ANY)
    vmem = pl.BlockSpec(memory_space=pltpu.VMEM)
    big = (seg * streams, width)
    out_shape = (
        jax.ShapeDtypeStruct(hidden.shape, BF),
        jax.ShapeDtypeStruct(grad_fresh.shape, BF),
        jax.ShapeDtypeStruct(hidden.shape, F32),
        jax.ShapeDtypeStruct((own, width), BF),
        jax.ShapeDtypeStruct((own, width), BF),
        jax.ShapeDtypeStruct((own, width), BF),
        jax.ShapeDtypeStruct((own, width), BF),
        jax.ShapeDtypeStruct((own, width * PARTS), BF),
        jax.ShapeDtypeStruct((PARTS * own, width), BF),
        jax.ShapeDtypeStruct((4, own, width), BF),
        jax.ShapeDtypeStruct((width, width), BF),
    )

    def v(shape, dtype=BF):
        return pltpu.VMEM(shape, dtype)

    seg2 = (streams, seg, cols)
    rows2 = (streams, seg_rows, width)
    wide = (3 * cols, cols, width, width, width)
    sem = pltpu.SemaphoreType.DMA
    scratch = (
        [
            v((3, streams, seg, width)),
            v((streams, 2, seg // 2, width)),
            v((width, 3 * cols)),
            v((width, width)),
            v(big),
            v(big),
            v(seg2),
            v((streams, 3 * seg, 2 * cols)),
            v((streams, 2, seg, 3 * seg)),
            v(seg2),
            v(rows2),
            v(rows2, F32),
            v((streams, seg, width)),
            v((streams, seg, width)),
            v((streams, seg // 2, cols)),
            v(big),
            v(big),
            v(seg2),
            v(rows2, F32),
            v(rows2),
            v(big),
            v((streams, 2, seg_rows, width)),
            v(rows2),
            v((streams, 2, seg_rows, width)),
            v(rows2),
            v((2, streams, seg, cols)),
            v(seg2),
            v((width, cols)),
            v(big),
        ]
        + [v((n_z * own, c)) for c in wide]
        + [v(((n_z - 1) * own, c)) for c in wide]
        + [v((own, c)) for c in wide]
        + [
            v((3 * seg, HEAD_DIM)),
            v((seg, HEAD_DIM)),
            v((own, 2), F32),
            v((streams, seg, 2), F32),
            v((streams, seg), F32),
            sem((18 + pieces,)),
            sem((T_COUNT, 3)),
            sem((T_COUNT, 3)),
            sem((5, 2 * n_z + 1)),
            sem((5, 2 * n_z + 1)),
            sem((5, n_z)),
            sem((5, n_z)),
            sem((5, n_z)),
            sem((5, n_z)),
            sem((9 + pieces, 3)),
            sem((9 + pieces, 3)),
            sem((9 + pieces,)),
        ]
    )
    results = pl.pallas_call(
        functools.partial(kernel, n_z, own, pieces),
        out_shape=out_shape,
        in_specs=[hbm] * 12 + [pl.BlockSpec(memory_space=pltpu.SMEM)] + [vmem] * 4,
        out_specs=tuple([hbm] * len(out_shape)),
        scratch_shapes=scratch,
        compiler_params=pltpu.CompilerParams(
            collective_id=0, has_side_effects=True, vmem_limit_bytes=64000 * 1024
        ),
        name="layer",
    )(
        hidden,
        memory,
        compressed,
        query_weight,
        key_weight,
        value_weight,
        output_weight,
        up_in,
        down_weight,
        conv_weight,
        grad_out,
        grad_fresh,
        reset_flag,
        boundary,
        gains,
        cosines,
        sines,
    )
    g_up = results[7]
    if pieces == 1:
        g_up = (
            g_up.reshape(own, PARTS, groups, ff_rows)
            .transpose(0, 2, 1, 3)
            .reshape(up_weight.shape)
        )
    steps = max(1, own // 32)
    moved = [*results[:7], g_up, *results[8:10]]
    weights = (query_weight, key_weight, value_weight, up_weight)

    def cut(t):
        shape = list(t.shape)
        dim = len(shape) - 2
        shape[dim] //= steps
        return pl.BlockSpec(tuple(shape), lambda i: (0,) * dim + (i, 0))

    out_types = (BF, BF) + (F32,) * 8
    sums = jax.ShapeDtypeStruct((own, 1), F32)
    done = pl.pallas_call(
        widen,
        grid=(steps,),
        out_shape=tuple(jax.ShapeDtypeStruct(t.shape, d) for t, d in zip(moved, out_types))
        + (sums, sums),
        in_specs=[cut(t) for t in moved] + [cut(t) for t in weights],
        out_specs=tuple([cut(t) for t in moved] + [cut(sums)] * 2),
        compiler_params=pltpu.CompilerParams(vmem_limit_bytes=64000 * 1024),
        name="widen",
    )(*moved, *weights)
    attn_gain_grad = done[10][:, 0] / attn_gain.astype(F32)
    ffn_gain_grad = done[11][:, 0] / ffn_gain.astype(F32)
    return tuple(done[:10]) + (attn_gain_grad, ffn_gain_grad)


def solution(mesh):
    act = P("stream", "tm", None)
    row = P("stream", None)
    in_specs = (act, act, act, P("stream"), row) + (row,) * 6 + (
        P(None, "stream", None),
        P("stream"),
        P("stream"),
        act,
        act,
    )
    out_specs = (act, act, act) + (row,) * 6 + (
        P(None, "stream", None),
        P("stream"),
        P("stream"),
    )
    return jax.shard_map(
        per_device, mesh=mesh, in_specs=in_specs, out_specs=out_specs, check_vma=False
    )
```

```python
import functools

import jax
import jax.numpy as jnp
import numpy as np
from jax import lax
from jax.experimental import pallas as pl
from jax.experimental.pallas import tpu as pltpu
from jax.sharding import PartitionSpec as P

HEAD_DIM = 128
PARTS = 4
BF = jnp.bfloat16
F32 = jnp.float32
MESH = pl.DeviceIdType.MESH

QKV, WO, UP, DOWN, CONV = range(5)
(T_CTX0, T_CTX1, T_CTX2, T_GO, T_GF, T_WO, T_ATT0, T_ATT1, T_NF0, T_NF1, T_GNF0, T_GNF1) = range(12)
(T_OUT0, T_OUT1, T_GA, T_OP, T_GN0, T_GN1, T_FR, T_GO1) = range(12, 20)
T_COUNT = 20


def dot(a, b, ca=1, cb=0):
    return lax.dot_general(a, b, (((ca,), (cb,)), ((), ())), preferred_element_type=F32)


def loop(n, body):
    def step(i, carry):
        body(i)
        return carry

    lax.fori_loop(0, n, step, 0)


def ds(start, size):
    return pl.ds(pl.multiple_of(start, size), size)


def mean(x):
    return jnp.sum(x, axis=-1, keepdims=True) * (1.0 / x.shape[-1])


def layer_norm(rows):
    center = rows - mean(rows)
    inv = lax.rsqrt(mean(center * center) + 1e-05)
    return center * inv, inv


def norm_back(c, unit, inv):
    return inv * (c - mean(c) - unit * mean(c * unit))


def kernel(
    n_z,
    own,
    pieces,
    hidden,
    memory,
    compressed,
    query_weight,
    key_weight,
    value_weight,
    output_weight,
    up_weight,
    down_weight,
    conv_weight,
    grad_out,
    grad_fresh,
    boundary_in,
    gains_in,
    cosines_in,
    sines_in,
    reset_flag,
    layer_out,
    fresh_out,
    grad_input,
    out_q,
    out_k,
    out_v,
    out_o,
    out_up,
    out_down,
    out_conv,
    conv_all,
    unit,
    memraw,
    wqkv,
    wo,
    up,
    down,
    qs,
    kv,
    probs,
    att_own,
    att_rows,
    middle,
    nf,
    go,
    gf,
    act,
    gpre,
    ga,
    gm,
    gm_low,
    gnp,
    d_a,
    y_a,
    d_b,
    y_b,
    d_o,
    y_o,
    l_o,
    l_conv,
    x_qkv,
    x_o,
    x_up,
    x_down,
    x_conv,
    z_qkv,
    z_o,
    z_up,
    z_down,
    z_conv,
    r_qkv,
    r_o,
    r_up,
    r_down,
    r_conv,
    t_v,
    t_q,
    gain_cols,
    row_info,
    doc_k,
    boundary,
    gains,
    cosines,
    sines,
    loc,
    tm_s,
    tm_r,
    ag_s,
    ag_r,
    rx_s,
    rx_r,
    rz_s,
    rz_r,
    fin_s,
    fin_r,
    fin_l,
):
    st = lax.axis_index("stream")
    r = lax.axis_index("tm")
    z = lax.div(st, 2)
    x = lax.rem(st, 2)
    core = lax.rem(r, 2)
    r1 = r + 1 - 2 * core
    r2 = lax.rem(r + 2, 4)
    r3 = lax.rem(r1 + 2, 4)
    xn = z * 2 + 1 - x
    seg = 512
    col = 256

    def zpeer(dz):
        return lax.rem(z + dz, n_z)

    def zfrom(dz):
        return lax.rem(z + n_z - dz, n_z)

    def load(src, dst, i):
        d = pltpu.make_async_copy(src, dst, loc.at[i])
        d.start()
        return d

    own_rows = ds(st * own, own)
    rcol = ds(r * col, col)
    ld_g = load(gains_in, gains, 16)
    ld_b = load(boundary_in, boundary, 17)
    ld_q = load(query_weight.at[:, rcol], wqkv.at[own_rows, pl.ds(0, col)], 0)
    ld_k = load(key_weight.at[:, rcol], wqkv.at[own_rows, pl.ds(col, col)], 1)
    ld_v = load(value_weight.at[:, rcol], wqkv.at[own_rows, pl.ds(2 * col, col)], 2)
    ld_o = load(output_weight.at[:, rcol], wo.at[own_rows, rcol], 3)
    if pieces > 1:
        size = 1024 // pieces
        ld_up = [
            load(
                up_weight.at[:, ds((i * PARTS + r) * size, size)],
                up.at[own_rows, pl.ds(i * size, size)],
                18 + i,
            )
            for i in range(pieces)
        ]
    else:
        ld_up = [load(up_weight, up.at[own_rows], 4)]
    ld_dn = load(down_weight.at[ds(r * own, own)], down.at[own_rows], 5)
    ld_cv = [
        load(conv_weight.at[k, :, rcol], conv_all.at[own_rows, pl.ds(k * col, col)], 6 + k)
        for k in range(4)
    ]
    tslot = ds(r * 128, 128)
    ld_m = load(memory, att_rows, 11)
    ld_c = {
        0: load(compressed, unit.at[0, :, tslot], 10),
        2: load(hidden, unit.at[2, :, tslot], 12),
    }
    ld_h = load(hidden, gm_low, 13)
    ld_t = [load(cosines_in, cosines, 18 + pieces), load(sines_in, sines, 19 + pieces)]
    ld_go = load(grad_out, go.at[:, tslot], 14)
    ld_gf = load(grad_fresh.at[:, :, rcol], gf.at[:, ds(r * 64, 64)], 15)

    barrier = pltpu.get_barrier_semaphore()
    for peer in (r1, r2, r3):
        pl.semaphore_signal(barrier, 1, device_id=(st, peer), device_id_type=MESH)
    pl.semaphore_signal(barrier, 1, device_id=(xn, r), device_id_type=MESH)

    def greet(i):
        pl.semaphore_signal(
            barrier, 1, device_id=(zpeer(i + 1) * 2 + x, r), device_id_type=MESH
        )

    loop(n_z - 1, greet)

    ld_g.wait()
    eye = lax.broadcasted_iota(jnp.int32, (own, own), 0) == lax.broadcasted_iota(
        jnp.int32, (own, own), 1
    )
    gain_cols[...] = dot(eye.astype(F32).astype(BF), gains[...].astype(BF), 1, 1)
    gain_a = gain_cols[:, 0:1]
    gain_f = gain_cols[:, 1:2]
    for d in (ld_q, ld_k, ld_v):
        d.wait()
    wqkv[own_rows] = (wqkv[own_rows].astype(F32) * gain_a).astype(BF)
    ld_m.wait()
    row = lax.broadcasted_iota(jnp.int32, (128, 128), 0)
    source = 2 * lax.rem(row, 64) + lax.div(row, 64)
    pick = (lax.broadcasted_iota(jnp.int32, (128, 128), 1) == source).astype(F32).astype(BF)
    for s in range(2):
        split = dot(pick, att_rows[s]).astype(BF)
        memraw[s, 0, ds(r * 64, 64), :] = split[:64]
        memraw[s, 1, ds(r * 64, 64), :] = split[64:]
    for d in ld_up:
        d.wait()
    up[own_rows] = (up[own_rows].astype(F32) * gain_f).astype(BF)
    for d in (ld_o, ld_dn):
        d.wait()
    pl.semaphore_wait(barrier, 4 + n_z - 1)

    def tm_copy(src, dst, op, i, peer):
        return pltpu.make_async_remote_copy(
            src, dst, tm_s.at[op, i], tm_r.at[op, i], device_id=(st, peer), device_id_type=MESH
        )

    def gather_start(op, src, slot):
        tm_copy(src, slot(r), op, 1, r2).start()
        tm_copy(src, slot(r), op, 0, r1).start()

    def gather_forward(op, slot):
        tm_copy(slot(r2), slot(r2), op, 1, r2).wait_recv()
        tm_copy(slot(r2), slot(r2), op, 2, r1).start()

    def gather_finish(op, slot):
        tm_copy(slot(r1), slot(r1), op, 0, r1).wait_recv()
        tm_copy(slot(r3), slot(r3), op, 2, r1).wait_recv()

    def gather_drain(op, slot):
        tm_copy(slot(r), slot(r), op, 0, r1).wait_send()
        tm_copy(slot(r), slot(r), op, 1, r2).wait_send()
        tm_copy(slot(r2), slot(r2), op, 2, r1).wait_send()

    peers = ((0, r1), (1, r2), (2, r3))

    def swap_start(op, src, dst):
        for i, p in peers[::-1]:
            tm_copy(src(p), dst(r), op, i, p).start()

    def swap_finish(op, dst):
        for i, p in peers:
            tm_copy(dst(p), dst(p), op, i, p).wait_recv()

    def swap_drain(op, src):
        for i, p in peers:
            tm_copy(src(p), src(p), op, i, p).wait_send()

    def reduce_start(op, part, far, near):
        tm_copy(part(r3), far, op, 0, r1).start()
        tm_copy(part(r1), near, op, 1, r1).start()

    def reduce_mid(op, part, far, land):
        tm_copy(far, far, op, 0, r1).wait_recv()
        far[...] = (far[...].astype(F32) + part(r2)[...].astype(F32)).astype(BF)
        tm_copy(far, land, op, 2, r2).start()

    def reduce_end(op, part, near, land):
        tm_copy(near, near, op, 1, r1).wait_recv()
        tm_copy(land, land, op, 2, r2).wait_recv()
        return part(r)[...].astype(F32) + near[...].astype(F32) + land[...].astype(F32)

    def reduce_drain(op, part, far):
        tm_copy(part(r3), far, op, 0, r1).wait_send()
        tm_copy(part(r1), far, op, 1, r1).wait_send()
        tm_copy(far, far, op, 2, r2).wait_send()

    held = {
        QKV: wqkv,
        WO: wo.at[:, rcol],
        UP: up,
        DOWN: down,
        CONV: conv_all,
    }

    def wslot(g, s):
        return held[g].at[ds(s * own, own)]

    def w_copy(g, s, i, dev, j=None):
        return pltpu.make_async_remote_copy(
            wslot(g, s),
            wslot(g, s),
            ag_s.at[g, i],
            ag_r.at[g, i if j is None else j],
            device_id=(dev, r),
            device_id_type=MESH,
        )

    relay = n_z == 4
    inner = (z == 1) | (z == 2)

    def direct(dz):
        zz = zpeer(dz)
        return (z + 3 != zz) & (zz + 3 != z)

    def w_send_x(g):
        w_copy(g, st, 0, xn).start()

    def w_send_z(g):
        if relay:
            for dz in (2, 1, 3):

                @pl.when(direct(dz))
                def _():
                    w_copy(g, st, dz, zpeer(dz) * 2 + x).start()
        else:
            loop(n_z - 1, lambda i: w_copy(g, st, i + 1, zpeer(i + 1) * 2 + x).start())

    def w_pass(g, dz):
        s = zfrom(dz) * 2 + x
        w_copy(g, s, dz, st).wait_recv()
        w_copy(g, s, n_z + dz - 1, xn).start()

    def w_relay(g):
        s = zfrom(2) * 2 + x
        return w_copy(g, s, 2 * n_z - 1, 3 * (z - 1) * 2 + x, 2 * z - 1)

    last = jnp.where(z == 0, 1, 3)

    def w_forward(g):
        if relay:
            s = zfrom(2) * 2 + x
            w_copy(g, s, 2, st).wait_recv()

            @pl.when(inner)
            def _():
                w_relay(g).start()

            w_copy(g, s, n_z + 1, xn).start()
            w_pass(g, 4 - last)
        else:
            loop(n_z - 1, lambda i: w_pass(g, i + 1))

    def w_forward_last(g):
        if relay:
            w_pass(g, last)

    def w_cross(g):
        w_copy(g, xn, 0, xn).wait_recv()
        if relay:
            for dz in (2, 1, 3):

                @pl.when(direct(dz))
                def _():
                    w_copy(g, xn, n_z + dz - 1, zpeer(dz) * 2 + x).start()
        else:
            loop(n_z - 1, lambda i: w_copy(g, xn, n_z + i, zpeer(i + 1) * 2 + x).start())

    def w_relay_cross(g):
        s = zfrom(2) * 2 + 1 - x
        return w_copy(g, s, 2 * n_z, 3 * (z - 1) * 2 + x, n_z + 2 * z - 2)

    def w_cross_pass(g):
        if relay:
            w_copy(g, zfrom(2) * 2 + x, 2, st).wait_recv()
            w_copy(g, zfrom(2) * 2 + 1 - x, n_z + 1, st).wait_recv()

            @pl.when(inner)
            def _():
                w_relay(g).start()
                w_relay_cross(g).start()

    def w_cross_finish(g):
        rest = (1, 3) if relay else range(1, n_z)
        for dz in rest:
            w_copy(g, zfrom(dz) * 2 + x, dz, st).wait_recv()
            w_copy(g, zfrom(dz) * 2 + 1 - x, n_z + dz - 1, st).wait_recv()

    def w_cross_drain(g):
        w_copy(g, st, 0, xn).wait_send()
        for dz in range(1, n_z):
            if relay:

                @pl.when(direct(dz))
                def _():
                    w_copy(g, st, dz, xn).wait_send()
                    w_copy(g, st, n_z + dz - 1, xn).wait_send()
            else:
                w_copy(g, st, dz, xn).wait_send()
                w_copy(g, st, n_z + dz - 1, xn).wait_send()
        if relay:

            @pl.when(inner)
            def _():
                w_relay(g).wait_send()
                w_relay_cross(g).wait_send()

    def w_finish(g):
        w_copy(g, xn, 0, xn).wait_recv()
        loop(n_z - 1, lambda i: w_copy(g, zfrom(i + 1) * 2 + 1 - x, n_z + i, xn).wait_recv())

    def w_drain(g):
        w_copy(g, st, 0, xn).wait_send()
        loop(n_z - 1, lambda i: w_copy(g, st, n_z + i, xn).wait_send())
        if relay:
            for dz in (1, 2, 3):

                @pl.when(direct(dz))
                def _():
                    w_copy(g, st, dz, xn).wait_send()

            @pl.when(inner)
            def _():
                w_relay(g).wait_send()
        else:
            loop(n_z - 1, lambda i: w_copy(g, st, i + 1, xn).wait_send())

    x_buf = {QKV: x_qkv, WO: x_o, UP: x_up, DOWN: x_down, CONV: x_conv}
    r_buf = {QKV: r_qkv, WO: r_o, UP: r_up, DOWN: r_down, CONV: r_conv}
    z_buf = {QKV: z_qkv, WO: z_o, UP: z_up, DOWN: z_down, CONV: z_conv}
    grads = {QKV: act.at[:, pl.ds(0, 3 * col)], WO: l_o, UP: up, DOWN: down, CONV: l_conv}

    def gx_copy(g, zz):
        return pltpu.make_async_remote_copy(
            grads[g].at[ds((zz * 2 + 1 - x) * own, own)],
            x_buf[g].at[ds(zz * own, own)],
            rx_s.at[g, zz],
            rx_r.at[g, zz],
            device_id=(xn, r),
            device_id_type=MESH,
        )

    def gx_start(g):
        if relay:
            for dz in (1, 3, 2, 0):
                gx_copy(g, zpeer(dz)).start()
        else:
            loop(n_z, lambda i: gx_copy(g, zpeer(i + 1)).start())

    def gz_copy(g, dz, zz):
        return pltpu.make_async_remote_copy(
            x_buf[g].at[ds(zz * own, own)],
            z_buf[g].at[ds((dz - 1) * own, own)],
            rz_s.at[g, dz],
            rz_r.at[g, dz],
            device_id=(zz * 2 + x, r),
            device_id_type=MESH,
        )

    def gz_fold(g, zz):
        gx_copy(g, zz).wait_recv()
        rows = ds(zz * own, own)
        x_buf[g][rows] = (
            x_buf[g][rows].astype(F32) + grads[g][ds((zz * 2 + x) * own, own)].astype(F32)
        ).astype(BF)

    def gz_far(g, dz, zz):
        return pltpu.make_async_remote_copy(
            x_buf[g].at[ds(zz * own, own)],
            r_buf[g],
            rz_s.at[g, dz],
            rz_r.at[g, 0],
            device_id=(jnp.where(z == 0, 1, 2) * 2 + x, r),
            device_id_type=MESH,
        )

    def gz_start(g):
        if not relay:

            def one(i):
                zz = zpeer(i + 1)
                gz_fold(g, zz)
                gz_copy(g, i + 1, zz).start()

            loop(n_z - 1, one)
            return
        for dz in (1, 3):
            zz = zpeer(dz)
            gz_fold(g, zz)

            @pl.when(direct(dz))
            def _():
                gz_copy(g, dz, zz).start()

            @pl.when(jnp.logical_not(direct(dz)))
            def _():
                gz_far(g, dz, zz).start()

        @pl.when(jnp.logical_not(inner))
        def _():
            gz_fold(g, zpeer(2))
            gz_copy(g, 2, zpeer(2)).start()

    def gz_relay(g):
        if relay:

            @pl.when(inner)
            def _():
                zz = zpeer(2)
                gz_fold(g, zz)
                gz_far(g, 2, zz).wait_recv()
                rows = ds(zz * own, own)
                x_buf[g][rows] = (x_buf[g][rows].astype(F32) + r_buf[g][...].astype(F32)).astype(BF)
                gz_copy(g, 2, zz).start()

    outs = {
        WO: (((0, col), lambda p: out_o.at[:, ds(p * col, col)]),),
        QKV: (
            ((0, col), lambda p: out_q.at[:, ds(p * col, col)]),
            ((col, col), lambda p: out_k.at[:, ds(p * col, col)]),
            ((2 * col, col), lambda p: out_v.at[:, ds(p * col, col)]),
        ),
        UP: tuple(
            (
                (i * (1024 // pieces), 1024 // pieces),
                (lambda i: lambda p: out_up.at[:, ds((i * PARTS + p) * (1024 // pieces), 1024 // pieces)])(i),
            )
            for i in range(pieces)
        ),
        DOWN: (((0, 1024), lambda p: out_down.at[ds(p * own, own)]),),
        CONV: tuple(
            ((k * col, col), (lambda k: lambda p: out_conv.at[k, :, ds(p * col, col)])(k))
            for k in range(4)
        ),
    }
    fin_base = {QKV: 0, WO: 3, DOWN: 4, CONV: 5, UP: 9}

    def fin_copy(g, j, i, p, slot_rank):
        (lane, size), slot = outs[g][j]
        n = fin_base[g] + j
        return pltpu.make_async_remote_copy(
            x_buf[g].at[ds(z * own, own), pl.ds(lane, size)],
            slot(slot_rank),
            fin_s.at[n, i],
            fin_r.at[n, i],
            device_id=(st, p),
            device_id_type=MESH,
        )

    def g_keep(g, j):
        (lane, size), slot = outs[g][j]
        return pltpu.make_async_copy(
            x_buf[g].at[ds(z * own, own), pl.ds(lane, size)], slot(r), fin_l.at[fin_base[g] + j]
        )

    def g_final(g, gain):
        gx_copy(g, z).wait_recv()
        rows = ds(z * own, own)
        total = x_buf[g][rows].astype(F32) + grads[g][ds((z * 2 + x) * own, own)].astype(F32)
        for dz in range(1, n_z):
            if relay:

                @pl.when(direct(n_z - dz))
                def _():
                    gz_copy(g, dz, zpeer(dz)).wait_recv()
            else:
                gz_copy(g, dz, zpeer(dz)).wait_recv()
            total = total + z_buf[g][pl.ds((dz - 1) * own, own)].astype(F32)
        if gain is not None:
            total = total * gain
        x_buf[g][rows] = total.astype(BF)
        for j in range(len(outs[g])):
            fin_copy(g, j, 1, r2, r).start()
            fin_copy(g, j, 0, r1, r).start()
            g_keep(g, j).start()

    def fin_pass(g, j):
        slot = outs[g][j][1](r2)
        n = fin_base[g] + j
        return pltpu.make_async_remote_copy(
            slot, slot, fin_s.at[n, 2], fin_r.at[n, 2], device_id=(st, r1), device_id_type=MESH
        )

    def g_pass(g):
        for j in range(len(outs[g])):
            fin_copy(g, j, 1, r2, r2).wait_recv()
            fin_pass(g, j).start()

    def g_drain(g):
        loop(n_z, lambda i: gx_copy(g, i).wait_send())
        loop(n_z - 1, lambda i: gz_copy(g, i + 1, zpeer(i + 1)).wait_send())
        for j in range(len(outs[g])):
            fin_copy(g, j, 0, r1, r1).wait()
            fin_copy(g, j, 1, r2, r).wait_send()
            fin_pass(g, j).wait()
            g_keep(g, j).wait()

    ctx_slot = (
        lambda p: unit.at[0, :, ds(p * 128, 128)],
        lambda p: memraw.at[:, :, ds(p * 64, 64)],
        lambda p: unit.at[2, :, ds(p * 128, 128)],
    )
    gather_start(T_CTX0, compressed, ctx_slot[0])
    w_send_x(QKV)
    w_send_z(QKV)
    gather_start(T_CTX1, ctx_slot[1](r), ctx_slot[1])
    gather_start(T_CTX2, hidden, ctx_slot[2])
    ctx_src = (compressed, ctx_slot[1](r), hidden)
    gf_src = lambda p: grad_fresh.at[:, :, ds(p * col, col)]
    gf_dst = lambda p: gf.at[:, ds(p * 64, 64)]
    swap_start(T_GF, gf_src, gf_dst)
    w_send_x(WO)
    w_send_z(WO)
    w_send_z(UP)
    w_send_z(DOWN)
    if relay:
        for end, dz in ((0, 1), (3, 3)):

            @pl.when(z == end)
            def _():
                for g in range(5):
                    z_buf[g][pl.ds((dz - 1) * own, own)] = jnp.zeros((own, z_buf[g].shape[1]), BF)

    before = lax.broadcasted_iota(jnp.int32, (seg, seg), 1) <= lax.broadcasted_iota(
        jnp.int32, (seg, seg), 0
    )
    before = before.astype(F32).astype(BF)
    ld_b.wait()
    starts = boundary[...].astype(F32).astype(BF)
    docs = dot(before, starts, 1, 1)
    doc_k[...] = dot(starts, before, 1, 1)
    for s in range(2):
        row_info[s, :, 0:1] = docs[:, s : s + 1]
        away = docs[:, s : s + 1] + reset_flag[s].astype(F32)
        row_info[s, :, 1:2] = jnp.where(away == 0.0, 0.0, -1e30)

    def norm_block(p, rank):
        def one(s):
            if p == 1:
                for half in range(2):
                    raw = memraw[s, half, ds(rank * 64, 64), :]
                    unit[p, s, ds(half * 256 + rank * 64, 64), :] = layer_norm(raw.astype(F32))[
                        0
                    ].astype(BF)
            else:
                rows = ds(rank * 128, 128)
                unit[p, s, rows, :] = layer_norm(unit[p, s, rows, :].astype(F32))[0].astype(BF)

        loop(2, one)

    def context(p, meanwhile=None):
        op, slot = T_CTX0 + p, ctx_slot[p]
        if p in ld_c:
            ld_c[p].wait()
        norm_block(p, r)
        gather_forward(op, slot)
        if meanwhile is not None:
            meanwhile()
        tm_copy(slot(r1), slot(r1), op, 0, r1).wait_recv()
        norm_block(p, r1)
        tm_copy(slot(r3), slot(r3), op, 2, r1).wait_recv()
        norm_block(p, r3)
        tm_copy(slot(r2), slot(r2), op, 2, r1).wait_send()
        norm_block(p, r2)

    def project(p):
        def one(i):
            s = lax.div(i, 2)
            at = lax.rem(i, 2) * 256
            rows = ds(at, 256)
            place = pl.ds(pl.multiple_of(p * seg + at, 256), 256)
            a = unit[p, s, rows, :]
            cs = cosines[place, :]
            sn = sines[place, :]

            def rot(t):
                return t * cs + pltpu.roll(t, 64, 1) * sn

            both = dot(a, wqkv[:, pl.ds(col, 2 * col)])
            for h in range(2):
                kv[s, place, pl.ds(h * 128, 128)] = rot(both[:, h * 128 : h * 128 + 128]).astype(BF)
            kv[s, place, pl.ds(col, col)] = both[:, col:].astype(BF)
            if p == 2:
                q = dot(a, wqkv[:, pl.ds(0, col)])
                for h in range(2):
                    qs[s, rows, pl.ds(h * 128, 128)] = (
                        rot(q[:, h * 128 : h * 128 + 128]) * HEAD_DIM ** (-0.5)
                    ).astype(BF)

        loop(4, one)

    context(0)
    w_forward(QKV)
    w_forward(WO)
    for d in ld_cv:
        d.wait()
    w_send_x(CONV)
    w_send_z(CONV)
    for d in ld_t:
        d.wait()
    context(1)
    w_forward_last(QKV)
    w_forward_last(WO)
    w_send_x(UP)
    w_send_x(DOWN)
    w_finish(QKV)
    project(0)
    project(1)
    w_forward(UP)
    w_cross(CONV)
    wo_slot = lambda p: wo.at[:, ds(p * col, col)]
    go_slot = lambda s: lambda p: go.at[s, ds(p * 128, 128)]

    def gather_wo():
        w_finish(WO)
        gather_start(T_WO, wo_slot(r), wo_slot)

    context(2, gather_wo)
    w_forward_last(UP)
    project(2)

    ld_gf.wait()
    swap_finish(T_GF, gf_dst)

    def conv_grads(i):
        c = ds(i * 256, 256)
        even_acc = jnp.zeros((256, 512), F32)
        odd_acc = jnp.zeros((256, 512), F32)
        for s in range(2):
            g = gf[s].astype(F32)
            at = lax.broadcasted_iota(jnp.int32, g.shape, 0)
            ahead = jnp.where(at == 255, 0.0, pltpu.roll(g, 255, 0))
            behind = jnp.where(at == 0, 0.0, pltpu.roll(g, 1, 0))
            low = gf[s]
            odd_acc += dot(memraw[s, 1, :, c], jnp.concatenate([ahead.astype(BF), low], 1), 0, 0)
            even_acc += dot(memraw[s, 0, :, c], jnp.concatenate([low, behind.astype(BF)], 1), 0, 0)
        l_conv[c, pl.ds(0, col)] = odd_acc[:, :col].astype(BF)
        l_conv[c, pl.ds(col, col)] = even_acc[:, :col].astype(BF)
        l_conv[c, pl.ds(2 * col, col)] = odd_acc[:, col:].astype(BF)
        l_conv[c, pl.ds(3 * col, col)] = even_acc[:, col:].astype(BF)

    loop(4, conv_grads)

    def attend(s):
        def one(qt):
            rows = ds(qt * 128, 128)
            shape = (128, seg)
            below = lax.broadcasted_iota(jnp.int32, shape, 1) <= (
                lax.broadcasted_iota(jnp.int32, shape, 0) + qt * 128
            )
            info = row_info[s, rows, :]
            same = doc_k[pl.ds(s, 1), :] == info[:, 0:1]
            seen = below & same
            bias = info[:, 1:2]
            for h in range(2):
                lanes = pl.ds(h * 128, 128)
                q = qs[s, rows, lanes]
                far = dot(q, kv[s, pl.ds(0, 1024), lanes], 1, 1) + bias
                near = jnp.where(seen, dot(q, kv[s, pl.ds(1024, seg), lanes], 1, 1), -1e30)
                top = jnp.maximum(
                    jnp.max(far, axis=-1, keepdims=True), jnp.max(near, axis=-1, keepdims=True)
                )
                far = jnp.exp(far - top)
                near = jnp.exp(near - top)
                inv = 1.0 / (
                    jnp.sum(far, axis=-1, keepdims=True) + jnp.sum(near, axis=-1, keepdims=True)
                )
                far = (far * inv).astype(BF)
                near = (near * inv).astype(BF)
                probs[s, h, rows, pl.ds(0, 1024)] = far
                probs[s, h, rows, pl.ds(1024, seg)] = near
                vl = pl.ds(col + h * 128, 128)
                o = dot(far, kv[s, pl.ds(0, 1024), vl]) + dot(near, kv[s, pl.ds(1024, seg), vl])
                att_own[s, rows, lanes] = o.astype(BF)

        loop(4, one)

    att_src = lambda s: lambda p: att_own.at[s, ds(p * 128, 128)]
    att_dst = lambda s: lambda p: att_rows.at[s, :, ds(p * col, col)]

    def attend_send(s):
        swap_start(T_ATT0 + s, att_src(s), att_dst(s))
        att_rows[s, :, rcol] = att_own[s, tslot, :]

    gather_start(T_GO, grad_out.at[0], go_slot(0))
    attend(0)
    attend_send(0)
    w_forward(DOWN)
    gather_forward(T_WO, wo_slot)
    attend(1)
    attend_send(1)
    w_forward_last(DOWN)
    gx_start(CONV)
    gather_forward(T_GO, go_slot(0))

    swap_finish(T_ATT0, att_dst(0))
    swap_finish(T_ATT1, att_dst(1))
    gather_finish(T_WO, wo_slot)
    ld_h.wait()

    def project_out(i):
        c = ds(i * 256, 256)
        mid = dot(att_rows[...].reshape(256, 1024), wo[:, c]).reshape(2, 128, 256)
        middle[:, :, c] = gm_low[:, :, c].astype(F32) + mid

    loop(4, project_out)
    nf_slot = lambda s: lambda p: nf.at[s, ds(p * 128, 128)]
    for s in range(2):
        nf[s, tslot, :] = layer_norm(middle[s])[0].astype(BF)
        gather_start(T_NF0 + s, nf_slot(s)(r), nf_slot(s))
    gather_start(T_GO1, grad_out.at[1], go_slot(1))
    ld_go.wait()
    gather_forward(T_NF0, nf_slot(0))
    gather_finish(T_GO, go_slot(0))
    w_finish(UP)
    w_finish(DOWN)

    def ffn(s):
        def one(i):
            c = ds(i * 256, 256)
            pre = dot(nf[s], up[:, c])
            g_act = dot(go[s], down[c, :], 1, 1)
            phi = 0.5 + 0.5 * lax.erf(pre * 0.7071067811865476)
            act[pl.ds(s * seg, seg), c] = (pre * phi).astype(BF)
            slope = phi + pre * (jnp.exp(pre * pre * -0.5) * 0.3989422804014327)
            gpre[pl.ds(s * seg, seg), c] = (g_act * slope).astype(BF)

        loop(4, one)

        def back(i):
            c = ds(i * 256, 256)
            gnp[pl.ds(s * seg, seg), c] = dot(
                gpre[pl.ds(s * seg, seg), :], up[c, :], 1, 1
            ).astype(BF)

        loop(4, back)

    def rows_of(buf, s):
        return lambda p: buf.at[pl.ds(pl.multiple_of(s * seg + p * 128, 128), 128)]

    def gnf_start(s):
        reduce_start(T_GNF0 + s, rows_of(gnp, s), d_b.at[s, 1], d_b.at[s, 0])

    def gnf_mid(s):
        reduce_mid(T_GNF0 + s, rows_of(gnp, s), d_b.at[s, 1], y_b.at[s])

    gather_finish(T_NF0, nf_slot(0))
    gather_forward(T_NF1, nf_slot(1))
    ffn(0)
    gnf_start(0)
    gather_forward(T_GO1, go_slot(1))
    gnf_mid(0)
    gather_finish(T_NF1, nf_slot(1))
    gather_finish(T_GO1, go_slot(1))
    ffn(1)
    gnf_start(1)
    gnf_mid(1)

    w_cross_pass(CONV)
    w_drain(UP)
    nf2 = nf

    def up_grads(i):
        c = ds(i * 256, 256)
        up[c, :] = (
            dot(nf2[0, :, c], gpre[pl.ds(0, seg), :], 0, 0)
            + dot(nf2[1, :, c], gpre[pl.ds(seg, seg), :], 0, 0)
        ).astype(BF)

    loop(4, up_grads)
    gx_start(UP)
    gz_start(CONV)

    for s in range(2):
        c = reduce_end(T_GNF0 + s, rows_of(gnp, s), d_b.at[s, 0], y_b.at[s])
        u, inv = layer_norm(middle[s])
        g = go[s, tslot, :].astype(F32) + norm_back(c, u, inv)
        gm[s] = g
        gm_low[s] = g.astype(BF)
        reduce_drain(T_GNF0 + s, rows_of(gnp, s), d_b.at[s, 1])
    for s in range(2):
        swap_drain(T_ATT0 + s, att_src(s))

    def attended_grads(i):
        part = dot(gm_low[...].reshape(256, 1024), wo[ds(i * 256, 256), :], 1, 1)
        att_own[:, ds(i * 128, 128), :] = part.astype(BF).reshape(2, 128, col)

    loop(4, attended_grads)
    ga_src = lambda p: att_own.at[:, ds(p * 128, 128)]
    ga_dst = lambda p: ga.at[:, ds(p * 128, 128)]
    swap_start(T_GA, ga_src, ga_dst)
    ga[:, tslot, :] = att_own[:, tslot, :]
    for s in range(2):
        gather_drain(T_NF0 + s, nf_slot(s))

    def output_grads(i):
        c = ds(i * 256, 256)
        part = dot(att_rows[:, :, c].reshape(256, 256), gm_low[...].reshape(256, 1024), 0, 0)
        nf[lax.div(i, 2), ds(lax.rem(i, 2) * 256, 256), :] = part.astype(BF)

    loop(4, output_grads)
    op_part = lambda p: nf.at[:, :, ds(p * col, col)]
    reduce_start(T_OP, op_part, d_o.at[1], d_o.at[0])

    def out_parts(i):
        s = lax.div(i, 4)
        rows = ds(s * seg, seg)
        c = ds(lax.rem(i, 4) * 256, 256)
        gpre[rows, c] = dot(act[rows, :], down[:, c]).astype(BF)

    loop(8, out_parts)
    for s in range(2):
        reduce_start(T_OUT0 + s, rows_of(gpre, s), d_a.at[s, 1], d_a.at[s, 0])
    w_drain(DOWN)

    def down_grads(i):
        c = ds(i * 256, 256)
        down[c, :] = (
            dot(act[pl.ds(0, seg), c], go[0], 0, 0) + dot(act[pl.ds(seg, seg), c], go[1], 0, 0)
        ).astype(BF)

    loop(4, down_grads)
    gx_start(DOWN)
    gz_relay(CONV)
    reduce_mid(T_OP, op_part, d_o.at[1], y_o)
    swap_finish(T_GA, ga_dst)

    def attend_back(s, h):
        if True:
            lanes = pl.ds(h * 128, 128)
            vl = pl.ds(col + h * 128, 128)

            def values(i):
                c = ds(i * 512, 512)
                t_v[c, :] = dot(probs[s, h, :, c], ga[s, :, lanes], 0, 0).astype(BF)

            loop(3, values)

            def scores(i):
                rows = ds(i * 128, 128)
                p = probs[s, h, rows, :].astype(F32)
                gp = dot(ga[s, rows, lanes], kv[s, :, vl], 1, 1)
                inner = jnp.sum(p * gp, axis=-1, keepdims=True)
                gs = (p * (gp - inner)).astype(BF)
                probs[s, h, rows, :] = gs
                place = pl.ds(pl.multiple_of(1024 + i * 128, 128), 128)
                t = dot(gs, kv[s, :, lanes])
                t = t * cosines[place, :] - pltpu.roll(t, 64, 1) * sines[place, :]
                t_q[rows, :] = (t * HEAD_DIM ** (-0.5)).astype(BF)

            loop(4, scores)

            def keys(i):
                c = ds(i * 512, 512)
                t = dot(probs[s, h, :, c], qs[s, :, lanes], 0, 0)
                t = t * cosines[c, :] - pltpu.roll(t, 64, 1) * sines[c, :]
                kv[s, c, lanes] = t.astype(BF)
                kv[s, c, vl] = t_v[c, :]

            loop(3, keys)
            qs[s, :, lanes] = t_q[...]

    attend_back(0, 0)
    for s in range(2):
        reduce_mid(T_OUT0 + s, rows_of(gpre, s), d_a.at[s, 1], y_a.at[s])
    gz_start(UP)
    attend_back(0, 1)
    g_final(CONV, None)
    attend_back(1, 0)
    gz_relay(UP)
    attend_back(1, 1)
    gz_start(DOWN)

    reduce_drain(T_OP, op_part, d_o.at[1])
    l_o[...] = reduce_end(T_OP, op_part, d_o.at[0], y_o).astype(BF).reshape(1024, col)
    gx_start(WO)

    def kv_grads(i):
        c = ds(i * 256, 256)
        total = jnp.zeros((256, 2 * col), F32)
        for p in range(3):
            for s in range(2):
                total += dot(unit[p, s, :, c], kv[s, pl.ds(p * seg, seg), :], 0, 0)
        act[c, pl.ds(col, 2 * col)] = total.astype(BF)
        act[c, pl.ds(0, col)] = (
            dot(unit[2, 0, :, c], qs[0], 0, 0) + dot(unit[2, 1, :, c], qs[1], 0, 0)
        ).astype(BF)

    loop(4, kv_grads)
    gx_start(QKV)
    g_final(UP, gain_f)
    gz_relay(DOWN)

    def hidden_grads(i):
        s = lax.div(i, 4)
        c = ds(lax.rem(i, 4) * 256, 256)
        part = dot(kv[s, pl.ds(1024, seg), :], wqkv[c, pl.ds(col, 2 * col)], 1, 1) + dot(
            qs[s], wqkv[c, pl.ds(0, col)], 1, 1
        )
        gnp[ds(s * seg, seg), c] = part.astype(BF)

    loop(8, hidden_grads)
    for s in range(2):
        reduce_start(T_GN0 + s, rows_of(gnp, s), d_b.at[s, 1], d_b.at[s, 0])
    ld_h = load(hidden, gm_low, 13)
    g_pass(CONV)
    for s in range(2):
        reduce_mid(T_GN0 + s, rows_of(gnp, s), d_b.at[s, 1], y_b.at[s])
    gz_start(WO)
    gz_relay(WO)
    w_cross_finish(CONV)
    gather_drain(T_GO, go_slot(0))
    gather_drain(T_GO1, go_slot(1))
    ld_w = [
        load(conv_all.at[pl.ds(i * seg, seg)], go.at[i], 14 + i) for i in range(2)
    ]
    for s in range(2):
        out = reduce_end(T_OUT0 + s, rows_of(gpre, s), d_a.at[s, 0], y_a.at[s])
        reduce_drain(T_OUT0 + s, rows_of(gpre, s), d_a.at[s, 1])
        y_a[s] = (middle[s] + out).astype(BF)
    st_out = load(y_a, layer_out, 16)
    for d in ld_w:
        d.wait()
    swap_drain(T_GA, ga_src)
    w_tap = lambda i, k: go[i, :, pl.ds(k * col, col)]

    def fresh(s, carry):
        taps = []
        for k in range(4):
            rows = memraw.at[s, 1 - k % 2]
            taps.append(
                dot(rows[:, pl.ds(0, seg)], w_tap(0, k)) + dot(rows[:, pl.ds(seg, seg)], w_tap(1, k))
            )
        at = lax.broadcasted_iota(jnp.int32, taps[0].shape, 0)
        total = taps[1] + taps[2]
        total += jnp.where(at == 0, 0.0, pltpu.roll(taps[0], 1, 0))
        total += jnp.where(at == 255, 0.0, pltpu.roll(taps[3], 255, 0))
        att_own[s, pl.ds(0, 256), :] = total.astype(BF)
        return carry

    lax.fori_loop(0, 2, fresh, 0)
    fr_src = lambda p: att_own.at[:, ds(p * 64, 64)]
    fr_dst = lambda p: fresh_out.at[:, :, ds(p * col, col)]
    swap_start(T_FR, fr_src, fr_dst)
    st_fr = load(fr_src(r), fr_dst(r), 17)
    gz_start(QKV)
    g_pass(UP)
    g_final(DOWN, None)
    gz_relay(QKV)

    for s in range(2):
        c = reduce_end(T_GN0 + s, rows_of(gnp, s), d_b.at[s, 0], y_b.at[s])
        if s == 0:
            ld_h.wait()
        u, inv = layer_norm(gm_low[s].astype(F32))
        gm[s] = gm[s] + norm_back(c, u, inv)
    st_gi = load(gm, grad_input, 18)
    g_final(WO, None)
    g_pass(DOWN)
    g_final(QKV, gain_a)
    g_pass(WO)
    g_pass(QKV)

    for p in range(3):
        tm_copy(ctx_src[p], ctx_slot[p](r), T_CTX0 + p, 0, r1).wait_send()
        tm_copy(ctx_src[p], ctx_slot[p](r), T_CTX0 + p, 1, r2).wait_send()
    swap_drain(T_GF, gf_src)
    gather_drain(T_WO, wo_slot)
    for s in range(2):
        reduce_drain(T_GN0 + s, rows_of(gnp, s), d_b.at[s, 1])
    swap_finish(T_FR, fr_dst)
    swap_drain(T_FR, fr_src)
    for d in (st_out, st_fr, st_gi):
        d.wait()
    w_drain(QKV)
    w_drain(WO)
    w_cross_drain(CONV)
    for g in range(5):
        g_drain(g)


def widen(steps, *refs):
    ins, weights, gains, outs, kept = refs[:10], refs[10:14], refs[14], refs[15:27], refs[27]
    for src, dst in zip(ins, outs):
        dst[...] = src[...].astype(dst.dtype)
    step = pl.program_id(0)
    block = weights[0].shape[0]
    rows = pl.ds(pl.multiple_of(step * block, block), block)
    total = jnp.zeros((block, 1), F32)
    for w, g in zip(weights[:3], ins[3:6]):
        total += jnp.sum(w[...].astype(F32) * g[...].astype(F32), axis=-1, keepdims=True)
    kept[rows, 0:1] = total
    kept[rows, 1:2] = jnp.sum(
        weights[3][...].astype(F32) * ins[7][...].astype(F32), axis=-1, keepdims=True
    )

    @pl.when(step == steps - 1)
    def _():
        own = kept.shape[0]
        eye = lax.broadcasted_iota(jnp.int32, (own, own), 0) == lax.broadcasted_iota(
            jnp.int32, (own, own), 1
        )
        for i in range(2):
            line = jnp.sum(jnp.where(eye, kept[:, i : i + 1], 0.0), axis=0, keepdims=True)
            outs[10 + i][...] = line / gains[i : i + 1, :]


def per_device(
    hidden,
    memory,
    compressed,
    reset_flag,
    boundary,
    query_weight,
    key_weight,
    value_weight,
    output_weight,
    up_weight,
    down_weight,
    conv_weight,
    attn_gain,
    ffn_gain,
    grad_out,
    grad_fresh,
):
    groups = lax.axis_size("stream")
    rank = lax.axis_index("tm")
    streams, seg_rows, width = hidden.shape
    own = query_weight.shape[0]
    seg = seg_rows * PARTS
    cols = width // PARTS
    n_z = groups // 2
    ff_rows = down_weight.shape[0] // PARTS
    pieces = groups if ff_rows % 128 == 0 else 1
    up_in = up_weight
    if pieces == 1:
        up_in = lax.dynamic_index_in_dim(
            up_weight.reshape(own, groups, PARTS, ff_rows), rank, 2, keepdims=False
        ).reshape(own, groups * ff_rows)
    gains = jnp.stack([attn_gain, ffn_gain]).astype(F32)
    spots = np.arange(seg)
    places = np.concatenate([spots, seg + spots[::2], seg + spots[1::2], 2 * seg + spots])
    half = HEAD_DIM // 2
    frequency = 10000.0 ** (-np.arange(half) * 2.0 / HEAD_DIM)
    angles = places[:, None] * frequency[None, :]
    cosine = np.cos(angles).astype(np.float32)
    sine = np.sin(angles).astype(np.float32)
    cosines = np.concatenate([cosine, cosine], axis=1)
    sines = np.concatenate([-sine, sine], axis=1)

    hbm = pl.BlockSpec(memory_space=pl.ANY)
    big = (seg * streams, width)
    out_shape = (
        jax.ShapeDtypeStruct(hidden.shape, BF),
        jax.ShapeDtypeStruct(grad_fresh.shape, BF),
        jax.ShapeDtypeStruct(hidden.shape, F32),
        jax.ShapeDtypeStruct((own, width), BF),
        jax.ShapeDtypeStruct((own, width), BF),
        jax.ShapeDtypeStruct((own, width), BF),
        jax.ShapeDtypeStruct((own, width), BF),
        jax.ShapeDtypeStruct((own, width * PARTS), BF),
        jax.ShapeDtypeStruct((PARTS * own, width), BF),
        jax.ShapeDtypeStruct((4, own, width), BF),
        jax.ShapeDtypeStruct((width, width), BF),
    )

    def v(shape, dtype=BF):
        return pltpu.VMEM(shape, dtype)

    seg2 = (streams, seg, cols)
    rows2 = (streams, seg_rows, width)
    wide = (3 * cols, cols, width, width, width)
    sem = pltpu.SemaphoreType.DMA
    scratch = (
        [
            v((3, streams, seg, width)),
            v((streams, 2, seg // 2, width)),
            v((width, 3 * cols)),
            v((width, width)),
            v(big),
            v(big),
            v(seg2),
            v((streams, 3 * seg, 2 * cols)),
            v((streams, 2, seg, 3 * seg)),
            v(seg2),
            v(rows2),
            v(rows2, F32),
            v((streams, seg, width)),
            v((streams, seg, width)),
            v((streams, seg // 2, cols)),
            v(big),
            v(big),
            v(seg2),
            v(rows2, F32),
            v(rows2),
            v(big),
            v((streams, 2, seg_rows, width)),
            v(rows2),
            v((streams, 2, seg_rows, width)),
            v(rows2),
            v((2, streams, seg, cols)),
            v(seg2),
            v((width, cols)),
            v(big),
        ]
        + [v((n_z * own, c)) for c in wide]
        + [v(((n_z - 1) * own, c)) for c in wide]
        + [v((own, c)) for c in wide]
        + [
            v((3 * seg, HEAD_DIM)),
            v((seg, HEAD_DIM)),
            v((own, 2), F32),
            v((streams, seg, 2), F32),
            v((streams, seg), F32),
            v(boundary.shape, jnp.int32),
            v(gains.shape, F32),
            v(cosines.shape, F32),
            v(sines.shape, F32),
            sem((20 + pieces,)),
            sem((T_COUNT, 3)),
            sem((T_COUNT, 3)),
            sem((5, 2 * n_z + 1)),
            sem((5, 2 * n_z + 1)),
            sem((5, n_z)),
            sem((5, n_z)),
            sem((5, n_z)),
            sem((5, n_z)),
            sem((9 + pieces, 3)),
            sem((9 + pieces, 3)),
            sem((9 + pieces,)),
        ]
    )
    results = pl.pallas_call(
        functools.partial(kernel, n_z, own, pieces),
        out_shape=out_shape,
        in_specs=[hbm] * 16 + [pl.BlockSpec(memory_space=pltpu.SMEM)],
        out_specs=tuple([hbm] * len(out_shape)),
        scratch_shapes=scratch,
        compiler_params=pltpu.CompilerParams(
            collective_id=0, has_side_effects=True, vmem_limit_bytes=64000 * 1024
        ),
        name="layer",
    )(
        hidden,
        memory,
        compressed,
        query_weight,
        key_weight,
        value_weight,
        output_weight,
        up_in,
        down_weight,
        conv_weight,
        grad_out,
        grad_fresh,
        boundary,
        gains,
        cosines,
        sines,
        reset_flag,
    )
    g_up = results[7]
    if pieces == 1:
        g_up = (
            g_up.reshape(own, PARTS, groups, ff_rows)
            .transpose(0, 2, 1, 3)
            .reshape(up_weight.shape)
        )
    steps = max(1, own // 32)
    moved = [*results[:7], g_up, *results[8:10]]
    weights = (query_weight, key_weight, value_weight, up_weight)

    def cut(t):
        shape = list(t.shape)
        dim = len(shape) - 2
        shape[dim] //= steps
        return pl.BlockSpec(tuple(shape), lambda i: (0,) * dim + (i, 0))

    out_types = (BF, BF) + (F32,) * 8
    line = jax.ShapeDtypeStruct((1, own), F32)
    whole = lambda t: pl.BlockSpec(t.shape, lambda i: (0, 0))
    done = pl.pallas_call(
        functools.partial(widen, steps),
        grid=(steps,),
        out_shape=tuple(jax.ShapeDtypeStruct(t.shape, d) for t, d in zip(moved, out_types))
        + (line, line),
        in_specs=[cut(t) for t in moved] + [cut(t) for t in weights] + [whole(gains)],
        out_specs=tuple([cut(t) for t in moved] + [whole(line)] * 2),
        scratch_shapes=[pltpu.VMEM((own, 2), F32)],
        compiler_params=pltpu.CompilerParams(vmem_limit_bytes=64000 * 1024),
        name="widen",
    )(*moved, *weights, gains)
    return tuple(done[:10]) + (done[10].reshape(own), done[11].reshape(own))


def solution(mesh):
    act = P("stream", "tm", None)
    row = P("stream", None)
    in_specs = (act, act, act, P("stream"), row) + (row,) * 6 + (
        P(None, "stream", None),
        P("stream"),
        P("stream"),
        act,
        act,
    )
    out_specs = (act, act, act) + (row,) * 6 + (
        P(None, "stream", None),
        P("stream"),
        P("stream"),
    )
    return jax.shard_map(
        per_device, mesh=mesh, in_specs=in_specs, out_specs=out_specs, check_vma=False
    )
```

```python
import functools

import jax
import jax.numpy as jnp
import numpy as np
from jax import lax
from jax.experimental import pallas as pl
from jax.experimental.pallas import tpu as pltpu
from jax.sharding import PartitionSpec as P

HEAD_DIM = 128
PARTS = 4
BF = jnp.bfloat16
F32 = jnp.float32
MESH = pl.DeviceIdType.MESH

QKV, WO, UP, DOWN, CONV = range(5)
(T_CTX0, T_CTX1, T_CTX2, T_GO, T_GF, T_WO, T_ATT0, T_ATT1, T_NF0, T_NF1, T_GNF0, T_GNF1) = range(12)
(T_OUT0, T_OUT1, T_GA, T_OP, T_GN0, T_GN1, T_FR, T_GO1) = range(12, 20)
T_COUNT = 20


def dot(a, b, ca=1, cb=0):
    return lax.dot_general(a, b, (((ca,), (cb,)), ((), ())), preferred_element_type=F32)


def loop(n, body):
    def step(i, carry):
        body(i)
        return carry

    lax.fori_loop(0, n, step, 0)


def ds(start, size):
    return pl.ds(pl.multiple_of(start, size), size)


def mean(x):
    return jnp.sum(x, axis=-1, keepdims=True) * (1.0 / x.shape[-1])


def layer_norm(rows):
    center = rows - mean(rows)
    inv = lax.rsqrt(mean(center * center) + 1e-05)
    return center * inv, inv


def norm_back(c, unit, inv):
    return inv * (c - mean(c) - unit * mean(c * unit))


def kernel(
    n_z,
    own,
    pieces,
    hidden,
    memory,
    compressed,
    query_weight,
    key_weight,
    value_weight,
    output_weight,
    up_weight,
    down_weight,
    conv_weight,
    grad_out,
    grad_fresh,
    boundary_in,
    gains_in,
    cosines_in,
    sines_in,
    reset_flag,
    layer_out,
    fresh_out,
    grad_input,
    out_qkv,
    out_o,
    out_up,
    out_down,
    out_conv,
    conv_all,
    unit,
    memraw,
    wqkv,
    wo,
    up,
    down,
    qs,
    kv,
    probs,
    att_own,
    att_rows,
    middle,
    nf,
    go,
    gf,
    act,
    gpre,
    ga,
    gm,
    gm_low,
    gnp,
    d_a,
    y_a,
    d_b,
    y_b,
    d_o,
    y_o,
    l_o,
    l_conv,
    x_qkv,
    x_o,
    x_up,
    x_down,
    x_conv,
    z_qkv,
    z_o,
    z_up,
    z_down,
    z_conv,
    r_qkv,
    r_o,
    r_up,
    r_down,
    r_conv,
    t_v,
    t_q,
    gain_cols,
    row_info,
    doc_k,
    boundary,
    gains,
    cosines,
    sines,
    loc,
    tm_s,
    tm_r,
    ag_s,
    ag_r,
    rx_s,
    rx_r,
    rz_s,
    rz_r,
    fin_s,
    fin_r,
    fin_l,
):
    st = lax.axis_index("stream")
    r = lax.axis_index("tm")
    z = lax.div(st, 2)
    x = lax.rem(st, 2)
    core = lax.rem(r, 2)
    r1 = r + 1 - 2 * core
    r2 = lax.rem(r + 2, 4)
    r3 = lax.rem(r1 + 2, 4)
    xn = z * 2 + 1 - x
    seg = 512
    col = 256

    def zpeer(dz):
        return lax.rem(z + dz, n_z)

    def zfrom(dz):
        return lax.rem(z + n_z - dz, n_z)

    def load(src, dst, i):
        d = pltpu.make_async_copy(src, dst, loc.at[i])
        d.start()
        return d

    own_rows = ds(st * own, own)
    rcol = ds(r * col, col)
    ld_g = load(gains_in, gains, 16)
    ld_b = load(boundary_in, boundary, 17)
    ld_q = load(query_weight.at[:, rcol], wqkv.at[own_rows, pl.ds(0, col)], 0)
    ld_k = load(key_weight.at[:, rcol], wqkv.at[own_rows, pl.ds(col, col)], 1)
    ld_v = load(value_weight.at[:, rcol], wqkv.at[own_rows, pl.ds(2 * col, col)], 2)
    ld_o = load(output_weight.at[:, rcol], wo.at[own_rows, rcol], 3)
    if pieces > 1:
        size = 1024 // pieces
        ld_up = [
            load(
                up_weight.at[:, ds((i * PARTS + r) * size, size)],
                up.at[own_rows, pl.ds(i * size, size)],
                18 + i,
            )
            for i in range(pieces)
        ]
    else:
        ld_up = [load(up_weight, up.at[own_rows], 4)]
    ld_dn = load(down_weight.at[ds(r * own, own)], down.at[own_rows], 5)
    ld_cv = [
        load(conv_weight.at[k, :, rcol], conv_all.at[own_rows, pl.ds(k * col, col)], 6 + k)
        for k in range(4)
    ]
    tslot = ds(r * 128, 128)
    ld_m = load(memory, att_rows, 11)
    ld_c = {
        0: load(compressed, unit.at[0, :, tslot], 10),
        2: load(hidden, unit.at[2, :, tslot], 12),
    }
    ld_h = load(hidden, gm_low, 13)
    ld_t = [load(cosines_in, cosines, 18 + pieces), load(sines_in, sines, 19 + pieces)]
    ld_go = load(grad_out, go.at[:, tslot], 14)
    ld_gf = load(grad_fresh.at[:, :, rcol], gf.at[:, ds(r * 64, 64)], 15)

    barrier = pltpu.get_barrier_semaphore()
    for peer in (r1, r2, r3):
        pl.semaphore_signal(barrier, 1, device_id=(st, peer), device_id_type=MESH)
    pl.semaphore_signal(barrier, 1, device_id=(xn, r), device_id_type=MESH)

    def greet(i):
        pl.semaphore_signal(
            barrier, 1, device_id=(zpeer(i + 1) * 2 + x, r), device_id_type=MESH
        )

    loop(n_z - 1, greet)

    ld_g.wait()
    eye = lax.broadcasted_iota(jnp.int32, (own, own), 0) == lax.broadcasted_iota(
        jnp.int32, (own, own), 1
    )
    gain_cols[...] = dot(eye.astype(F32).astype(BF), gains[...].astype(BF), 1, 1)
    gain_a = gain_cols[:, 0:1]
    gain_f = gain_cols[:, 1:2]
    for d in (ld_q, ld_k, ld_v):
        d.wait()
    wqkv[own_rows] = (wqkv[own_rows].astype(F32) * gain_a).astype(BF)
    ld_m.wait()
    row = lax.broadcasted_iota(jnp.int32, (128, 128), 0)
    source = 2 * lax.rem(row, 64) + lax.div(row, 64)
    pick = (lax.broadcasted_iota(jnp.int32, (128, 128), 1) == source).astype(F32).astype(BF)
    for s in range(2):
        split = dot(pick, att_rows[s]).astype(BF)
        memraw[s, 0, ds(r * 64, 64), :] = split[:64]
        memraw[s, 1, ds(r * 64, 64), :] = split[64:]
    for d in ld_up:
        d.wait()
    up[own_rows] = (up[own_rows].astype(F32) * gain_f).astype(BF)
    for d in (ld_o, ld_dn):
        d.wait()
    pl.semaphore_wait(barrier, 4 + n_z - 1)

    def tm_copy(src, dst, op, i, peer):
        return pltpu.make_async_remote_copy(
            src, dst, tm_s.at[op, i], tm_r.at[op, i], device_id=(st, peer), device_id_type=MESH
        )

    def gather_start(op, src, slot):
        tm_copy(src, slot(r), op, 1, r2).start()
        tm_copy(src, slot(r), op, 0, r1).start()

    def gather_forward(op, slot):
        tm_copy(slot(r2), slot(r2), op, 1, r2).wait_recv()
        tm_copy(slot(r2), slot(r2), op, 2, r1).start()

    def gather_finish(op, slot):
        tm_copy(slot(r1), slot(r1), op, 0, r1).wait_recv()
        tm_copy(slot(r3), slot(r3), op, 2, r1).wait_recv()

    def gather_drain(op, slot):
        tm_copy(slot(r), slot(r), op, 0, r1).wait_send()
        tm_copy(slot(r), slot(r), op, 1, r2).wait_send()
        tm_copy(slot(r2), slot(r2), op, 2, r1).wait_send()

    peers = ((0, r1), (1, r2), (2, r3))

    def swap_start(op, src, dst):
        for i, p in peers[::-1]:
            tm_copy(src(p), dst(r), op, i, p).start()

    def swap_finish(op, dst):
        for i, p in peers:
            tm_copy(dst(p), dst(p), op, i, p).wait_recv()

    def swap_drain(op, src):
        for i, p in peers:
            tm_copy(src(p), src(p), op, i, p).wait_send()

    def reduce_start(op, part, far, near):
        tm_copy(part(r3), far, op, 0, r1).start()
        tm_copy(part(r1), near, op, 1, r1).start()

    def reduce_mid(op, part, far, land):
        tm_copy(far, far, op, 0, r1).wait_recv()
        far[...] = (far[...].astype(F32) + part(r2)[...].astype(F32)).astype(BF)
        tm_copy(far, land, op, 2, r2).start()

    def reduce_end(op, part, near, land):
        tm_copy(near, near, op, 1, r1).wait_recv()
        tm_copy(land, land, op, 2, r2).wait_recv()
        return part(r)[...].astype(F32) + near[...].astype(F32) + land[...].astype(F32)

    def reduce_drain(op, part, far):
        tm_copy(part(r3), far, op, 0, r1).wait_send()
        tm_copy(part(r1), far, op, 1, r1).wait_send()
        tm_copy(far, far, op, 2, r2).wait_send()

    held = {
        QKV: wqkv,
        WO: wo.at[:, rcol],
        UP: up,
        DOWN: down,
        CONV: conv_all,
    }

    def wslot(g, s):
        return held[g].at[ds(s * own, own)]

    def w_copy(g, s, i, dev, j=None):
        return pltpu.make_async_remote_copy(
            wslot(g, s),
            wslot(g, s),
            ag_s.at[g, i],
            ag_r.at[g, i if j is None else j],
            device_id=(dev, r),
            device_id_type=MESH,
        )

    relay = n_z == 4
    inner = (z == 1) | (z == 2)

    def direct(dz):
        zz = zpeer(dz)
        return (z + 3 != zz) & (zz + 3 != z)

    def w_send_x(g):
        w_copy(g, st, 0, xn).start()

    def w_send_z(g):
        if relay:
            for dz in (2, 1, 3):

                @pl.when(direct(dz))
                def _():
                    w_copy(g, st, dz, zpeer(dz) * 2 + x).start()
        else:
            loop(n_z - 1, lambda i: w_copy(g, st, i + 1, zpeer(i + 1) * 2 + x).start())

    def w_pass(g, dz):
        s = zfrom(dz) * 2 + x
        w_copy(g, s, dz, st).wait_recv()
        w_copy(g, s, n_z + dz - 1, xn).start()

    def w_relay(g):
        s = zfrom(2) * 2 + x
        return w_copy(g, s, 2 * n_z - 1, 3 * (z - 1) * 2 + x, 2 * z - 1)

    last = jnp.where(z == 0, 1, 3)

    def w_forward(g):
        if relay:
            s = zfrom(2) * 2 + x
            w_copy(g, s, 2, st).wait_recv()

            @pl.when(inner)
            def _():
                w_relay(g).start()

            w_copy(g, s, n_z + 1, xn).start()
            w_pass(g, 4 - last)
        else:
            loop(n_z - 1, lambda i: w_pass(g, i + 1))

    def w_forward_last(g):
        if relay:
            w_pass(g, last)

    def w_cross(g):
        w_copy(g, xn, 0, xn).wait_recv()
        if relay:
            for dz in (2, 1, 3):

                @pl.when(direct(dz))
                def _():
                    w_copy(g, xn, n_z + dz - 1, zpeer(dz) * 2 + x).start()
        else:
            loop(n_z - 1, lambda i: w_copy(g, xn, n_z + i, zpeer(i + 1) * 2 + x).start())

    def w_relay_cross(g):
        s = zfrom(2) * 2 + 1 - x
        return w_copy(g, s, 2 * n_z, 3 * (z - 1) * 2 + x, n_z + 2 * z - 2)

    def w_cross_pass(g):
        if relay:
            w_copy(g, zfrom(2) * 2 + x, 2, st).wait_recv()
            w_copy(g, zfrom(2) * 2 + 1 - x, n_z + 1, st).wait_recv()

            @pl.when(inner)
            def _():
                w_relay(g).start()
                w_relay_cross(g).start()

    def w_cross_finish(g):
        rest = (1, 3) if relay else range(1, n_z)
        for dz in rest:
            w_copy(g, zfrom(dz) * 2 + x, dz, st).wait_recv()
            w_copy(g, zfrom(dz) * 2 + 1 - x, n_z + dz - 1, st).wait_recv()

    def w_cross_drain(g):
        w_copy(g, st, 0, xn).wait_send()
        for dz in range(1, n_z):
            if relay:

                @pl.when(direct(dz))
                def _():
                    w_copy(g, st, dz, xn).wait_send()
                    w_copy(g, st, n_z + dz - 1, xn).wait_send()
            else:
                w_copy(g, st, dz, xn).wait_send()
                w_copy(g, st, n_z + dz - 1, xn).wait_send()
        if relay:

            @pl.when(inner)
            def _():
                w_relay(g).wait_send()
                w_relay_cross(g).wait_send()

    def w_finish(g):
        w_copy(g, xn, 0, xn).wait_recv()
        loop(n_z - 1, lambda i: w_copy(g, zfrom(i + 1) * 2 + 1 - x, n_z + i, xn).wait_recv())

    def w_drain(g):
        w_copy(g, st, 0, xn).wait_send()
        loop(n_z - 1, lambda i: w_copy(g, st, n_z + i, xn).wait_send())
        if relay:
            for dz in (1, 2, 3):

                @pl.when(direct(dz))
                def _():
                    w_copy(g, st, dz, xn).wait_send()

            @pl.when(inner)
            def _():
                w_relay(g).wait_send()
        else:
            loop(n_z - 1, lambda i: w_copy(g, st, i + 1, xn).wait_send())

    x_buf = {QKV: x_qkv, WO: x_o, UP: x_up, DOWN: x_down, CONV: x_conv}
    r_buf = {QKV: r_qkv, WO: r_o, UP: r_up, DOWN: r_down, CONV: r_conv}
    z_buf = {QKV: z_qkv, WO: z_o, UP: z_up, DOWN: z_down, CONV: z_conv}
    grads = {QKV: act.at[:, pl.ds(0, 3 * col)], WO: l_o, UP: up, DOWN: down, CONV: l_conv}

    def gx_copy(g, zz):
        return pltpu.make_async_remote_copy(
            grads[g].at[ds((zz * 2 + 1 - x) * own, own)],
            x_buf[g].at[ds(zz * own, own)],
            rx_s.at[g, zz],
            rx_r.at[g, zz],
            device_id=(xn, r),
            device_id_type=MESH,
        )

    def gx_start(g):
        if relay:
            for dz in (1, 3, 2, 0):
                gx_copy(g, zpeer(dz)).start()
        else:
            loop(n_z, lambda i: gx_copy(g, zpeer(i + 1)).start())

    def gz_copy(g, dz, zz):
        return pltpu.make_async_remote_copy(
            x_buf[g].at[ds(zz * own, own)],
            z_buf[g].at[ds((dz - 1) * own, own)],
            rz_s.at[g, dz],
            rz_r.at[g, dz],
            device_id=(zz * 2 + x, r),
            device_id_type=MESH,
        )

    def gz_fold(g, zz):
        gx_copy(g, zz).wait_recv()
        rows = ds(zz * own, own)
        x_buf[g][rows] = (
            x_buf[g][rows].astype(F32) + grads[g][ds((zz * 2 + x) * own, own)].astype(F32)
        ).astype(BF)

    def gz_far(g, dz, zz):
        return pltpu.make_async_remote_copy(
            x_buf[g].at[ds(zz * own, own)],
            r_buf[g],
            rz_s.at[g, dz],
            rz_r.at[g, 0],
            device_id=(jnp.where(z == 0, 1, 2) * 2 + x, r),
            device_id_type=MESH,
        )

    def gz_start(g):
        if not relay:

            def one(i):
                zz = zpeer(i + 1)
                gz_fold(g, zz)
                gz_copy(g, i + 1, zz).start()

            loop(n_z - 1, one)
            return
        for dz in (1, 3):
            zz = zpeer(dz)
            gz_fold(g, zz)

            @pl.when(direct(dz))
            def _():
                gz_copy(g, dz, zz).start()

            @pl.when(jnp.logical_not(direct(dz)))
            def _():
                gz_far(g, dz, zz).start()

        @pl.when(jnp.logical_not(inner))
        def _():
            gz_fold(g, zpeer(2))
            gz_copy(g, 2, zpeer(2)).start()

    def gz_relay(g):
        if relay:

            @pl.when(inner)
            def _():
                zz = zpeer(2)
                gz_fold(g, zz)
                gz_far(g, 2, zz).wait_recv()
                rows = ds(zz * own, own)
                x_buf[g][rows] = (x_buf[g][rows].astype(F32) + r_buf[g][...].astype(F32)).astype(BF)
                gz_copy(g, 2, zz).start()

    outs = {
        QKV: (((0, 3 * col), lambda p: out_qkv.at[p]),),
        WO: (((0, col), lambda p: out_o.at[p]),),
        UP: (((0, 1024), lambda p: out_up.at[p]),),
        DOWN: (((0, 1024), lambda p: out_down.at[ds(p * own, own)]),),
        CONV: (((0, 1024), lambda p: out_conv.at[p]),),
    }
    fin_base = {g: g for g in range(5)}

    def fin_copy(g, j, i, p, slot_rank):
        (lane, size), slot = outs[g][j]
        n = fin_base[g] + j
        return pltpu.make_async_remote_copy(
            x_buf[g].at[ds(z * own, own), pl.ds(lane, size)],
            slot(slot_rank),
            fin_s.at[n, i],
            fin_r.at[n, i],
            device_id=(st, p),
            device_id_type=MESH,
        )

    def g_keep(g, j):
        (lane, size), slot = outs[g][j]
        return pltpu.make_async_copy(
            x_buf[g].at[ds(z * own, own), pl.ds(lane, size)], slot(r), fin_l.at[fin_base[g] + j]
        )

    def g_final(g, gain):
        gx_copy(g, z).wait_recv()
        rows = ds(z * own, own)
        total = x_buf[g][rows].astype(F32) + grads[g][ds((z * 2 + x) * own, own)].astype(F32)
        for dz in range(1, n_z):
            if relay:

                @pl.when(direct(n_z - dz))
                def _():
                    gz_copy(g, dz, zpeer(dz)).wait_recv()
            else:
                gz_copy(g, dz, zpeer(dz)).wait_recv()
            total = total + z_buf[g][pl.ds((dz - 1) * own, own)].astype(F32)
        if gain is not None:
            total = total * gain
        x_buf[g][rows] = total.astype(BF)
        for j in range(len(outs[g])):
            fin_copy(g, j, 1, r2, r).start()
            fin_copy(g, j, 0, r1, r).start()
            g_keep(g, j).start()

    def fin_pass(g, j):
        slot = outs[g][j][1](r2)
        n = fin_base[g] + j
        return pltpu.make_async_remote_copy(
            slot, slot, fin_s.at[n, 2], fin_r.at[n, 2], device_id=(st, r1), device_id_type=MESH
        )

    def g_pass(g):
        for j in range(len(outs[g])):
            fin_copy(g, j, 1, r2, r2).wait_recv()
            fin_pass(g, j).start()

    def g_drain(g):
        loop(n_z, lambda i: gx_copy(g, i).wait_send())
        loop(n_z - 1, lambda i: gz_copy(g, i + 1, zpeer(i + 1)).wait_send())
        for j in range(len(outs[g])):
            fin_copy(g, j, 0, r1, r1).wait()
            fin_copy(g, j, 1, r2, r).wait_send()
            fin_pass(g, j).wait()
            g_keep(g, j).wait()

    ctx_slot = (
        lambda p: unit.at[0, :, ds(p * 128, 128)],
        lambda p: memraw.at[:, :, ds(p * 64, 64)],
        lambda p: unit.at[2, :, ds(p * 128, 128)],
    )
    gather_start(T_CTX0, compressed, ctx_slot[0])
    w_send_x(QKV)
    w_send_z(QKV)
    gather_start(T_CTX1, ctx_slot[1](r), ctx_slot[1])
    gather_start(T_CTX2, hidden, ctx_slot[2])
    ctx_src = (compressed, ctx_slot[1](r), hidden)
    gf_src = lambda p: grad_fresh.at[:, :, ds(p * col, col)]
    gf_dst = lambda p: gf.at[:, ds(p * 64, 64)]
    swap_start(T_GF, gf_src, gf_dst)
    w_send_x(WO)
    w_send_z(WO)
    w_send_z(UP)
    w_send_z(DOWN)
    if relay:
        for end, dz in ((0, 1), (3, 3)):

            @pl.when(z == end)
            def _():
                for g in range(5):
                    z_buf[g][pl.ds((dz - 1) * own, own)] = jnp.zeros((own, z_buf[g].shape[1]), BF)

    before = lax.broadcasted_iota(jnp.int32, (seg, seg), 1) <= lax.broadcasted_iota(
        jnp.int32, (seg, seg), 0
    )
    before = before.astype(F32).astype(BF)
    ld_b.wait()
    starts = boundary[...].astype(F32).astype(BF)
    docs = dot(before, starts, 1, 1)
    doc_k[...] = dot(starts, before, 1, 1)
    for s in range(2):
        row_info[s, :, 0:1] = docs[:, s : s + 1]
        away = docs[:, s : s + 1] + reset_flag[s].astype(F32)
        row_info[s, :, 1:2] = jnp.where(away == 0.0, 0.0, -1e30)

    def norm_block(p, rank):
        def one(s):
            if p == 1:
                for half in range(2):
                    raw = memraw[s, half, ds(rank * 64, 64), :]
                    unit[p, s, ds(half * 256 + rank * 64, 64), :] = layer_norm(raw.astype(F32))[
                        0
                    ].astype(BF)
            else:
                rows = ds(rank * 128, 128)
                unit[p, s, rows, :] = layer_norm(unit[p, s, rows, :].astype(F32))[0].astype(BF)

        loop(2, one)

    def context(p, meanwhile=None):
        op, slot = T_CTX0 + p, ctx_slot[p]
        if p in ld_c:
            ld_c[p].wait()
        norm_block(p, r)
        gather_forward(op, slot)
        if meanwhile is not None:
            meanwhile()
        tm_copy(slot(r1), slot(r1), op, 0, r1).wait_recv()
        norm_block(p, r1)
        tm_copy(slot(r3), slot(r3), op, 2, r1).wait_recv()
        norm_block(p, r3)
        tm_copy(slot(r2), slot(r2), op, 2, r1).wait_send()
        norm_block(p, r2)

    def project(p):
        def one(i):
            s = lax.div(i, 2)
            at = lax.rem(i, 2) * 256
            rows = ds(at, 256)
            place = pl.ds(pl.multiple_of(p * seg + at, 256), 256)
            a = unit[p, s, rows, :]
            cs = cosines[place, :]
            sn = sines[place, :]

            def rot(t):
                return t * cs + pltpu.roll(t, 64, 1) * sn

            both = dot(a, wqkv[:, pl.ds(col, 2 * col)])
            for h in range(2):
                kv[s, place, pl.ds(h * 128, 128)] = rot(both[:, h * 128 : h * 128 + 128]).astype(BF)
            kv[s, place, pl.ds(col, col)] = both[:, col:].astype(BF)
            if p == 2:
                q = dot(a, wqkv[:, pl.ds(0, col)])
                for h in range(2):
                    qs[s, rows, pl.ds(h * 128, 128)] = (
                        rot(q[:, h * 128 : h * 128 + 128]) * HEAD_DIM ** (-0.5)
                    ).astype(BF)

        loop(4, one)

    context(0)
    w_forward(QKV)
    w_forward(WO)
    for d in ld_cv:
        d.wait()
    w_send_x(CONV)
    w_send_z(CONV)
    for d in ld_t:
        d.wait()
    context(1)
    w_forward_last(QKV)
    w_forward_last(WO)
    w_send_x(UP)
    w_send_x(DOWN)
    w_finish(QKV)
    project(0)
    project(1)
    w_forward(UP)
    w_cross(CONV)
    wo_slot = lambda p: wo.at[:, ds(p * col, col)]
    go_slot = lambda s: lambda p: go.at[s, ds(p * 128, 128)]

    def gather_wo():
        w_finish(WO)
        gather_start(T_WO, wo_slot(r), wo_slot)

    context(2, gather_wo)
    w_forward_last(UP)
    project(2)

    ld_gf.wait()
    swap_finish(T_GF, gf_dst)

    def conv_grads(i):
        c = ds(i * 256, 256)
        even_acc = jnp.zeros((256, 512), F32)
        odd_acc = jnp.zeros((256, 512), F32)
        for s in range(2):
            g = gf[s].astype(F32)
            at = lax.broadcasted_iota(jnp.int32, g.shape, 0)
            ahead = jnp.where(at == 255, 0.0, pltpu.roll(g, 255, 0))
            behind = jnp.where(at == 0, 0.0, pltpu.roll(g, 1, 0))
            low = gf[s]
            odd_acc += dot(memraw[s, 1, :, c], jnp.concatenate([ahead.astype(BF), low], 1), 0, 0)
            even_acc += dot(memraw[s, 0, :, c], jnp.concatenate([low, behind.astype(BF)], 1), 0, 0)
        l_conv[c, pl.ds(0, col)] = odd_acc[:, :col].astype(BF)
        l_conv[c, pl.ds(col, col)] = even_acc[:, :col].astype(BF)
        l_conv[c, pl.ds(2 * col, col)] = odd_acc[:, col:].astype(BF)
        l_conv[c, pl.ds(3 * col, col)] = even_acc[:, col:].astype(BF)

    loop(4, conv_grads)

    def attend(s):
        def one(qt):
            rows = ds(qt * 128, 128)
            shape = (128, seg)
            below = lax.broadcasted_iota(jnp.int32, shape, 1) <= (
                lax.broadcasted_iota(jnp.int32, shape, 0) + qt * 128
            )
            info = row_info[s, rows, :]
            same = doc_k[pl.ds(s, 1), :] == info[:, 0:1]
            seen = below & same
            bias = info[:, 1:2]
            for h in range(2):
                lanes = pl.ds(h * 128, 128)
                q = qs[s, rows, lanes]
                far = dot(q, kv[s, pl.ds(0, 1024), lanes], 1, 1) + bias
                near = jnp.where(seen, dot(q, kv[s, pl.ds(1024, seg), lanes], 1, 1), -1e30)
                top = jnp.maximum(
                    jnp.max(far, axis=-1, keepdims=True), jnp.max(near, axis=-1, keepdims=True)
                )
                far = jnp.exp(far - top)
                near = jnp.exp(near - top)
                inv = 1.0 / (
                    jnp.sum(far, axis=-1, keepdims=True) + jnp.sum(near, axis=-1, keepdims=True)
                )
                far = (far * inv).astype(BF)
                near = (near * inv).astype(BF)
                probs[s, h, rows, pl.ds(0, 1024)] = far
                probs[s, h, rows, pl.ds(1024, seg)] = near
                vl = pl.ds(col + h * 128, 128)
                o = dot(far, kv[s, pl.ds(0, 1024), vl]) + dot(near, kv[s, pl.ds(1024, seg), vl])
                att_own[s, rows, lanes] = o.astype(BF)

        loop(4, one)

    att_src = lambda s: lambda p: att_own.at[s, ds(p * 128, 128)]
    att_dst = lambda s: lambda p: att_rows.at[s, :, ds(p * col, col)]

    def attend_send(s):
        swap_start(T_ATT0 + s, att_src(s), att_dst(s))
        att_rows[s, :, rcol] = att_own[s, tslot, :]

    gather_start(T_GO, grad_out.at[0], go_slot(0))
    attend(0)
    attend_send(0)
    w_forward(DOWN)
    gather_forward(T_WO, wo_slot)
    attend(1)
    attend_send(1)
    w_forward_last(DOWN)
    gx_start(CONV)
    gather_forward(T_GO, go_slot(0))

    swap_finish(T_ATT0, att_dst(0))
    swap_finish(T_ATT1, att_dst(1))
    gather_finish(T_WO, wo_slot)
    ld_h.wait()

    def project_out(i):
        c = ds(i * 256, 256)
        mid = dot(att_rows[...].reshape(256, 1024), wo[:, c]).reshape(2, 128, 256)
        middle[:, :, c] = gm_low[:, :, c].astype(F32) + mid

    loop(4, project_out)
    nf_slot = lambda s: lambda p: nf.at[s, ds(p * 128, 128)]
    for s in range(2):
        nf[s, tslot, :] = layer_norm(middle[s])[0].astype(BF)
        gather_start(T_NF0 + s, nf_slot(s)(r), nf_slot(s))
    gather_start(T_GO1, grad_out.at[1], go_slot(1))
    ld_go.wait()
    gather_forward(T_NF0, nf_slot(0))
    gather_finish(T_GO, go_slot(0))
    w_finish(UP)
    w_finish(DOWN)

    def ffn(s):
        def one(i):
            c = ds(i * 256, 256)
            pre = dot(nf[s], up[:, c])
            g_act = dot(go[s], down[c, :], 1, 1)
            phi = 0.5 + 0.5 * lax.erf(pre * 0.7071067811865476)
            act[pl.ds(s * seg, seg), c] = (pre * phi).astype(BF)
            slope = phi + pre * (jnp.exp(pre * pre * -0.5) * 0.3989422804014327)
            gpre[pl.ds(s * seg, seg), c] = (g_act * slope).astype(BF)

        loop(4, one)

        def back(i):
            c = ds(i * 256, 256)
            gnp[pl.ds(s * seg, seg), c] = dot(
                gpre[pl.ds(s * seg, seg), :], up[c, :], 1, 1
            ).astype(BF)

        loop(4, back)

    def rows_of(buf, s):
        return lambda p: buf.at[pl.ds(pl.multiple_of(s * seg + p * 128, 128), 128)]

    def gnf_start(s):
        reduce_start(T_GNF0 + s, rows_of(gnp, s), d_b.at[s, 1], d_b.at[s, 0])

    def gnf_mid(s):
        reduce_mid(T_GNF0 + s, rows_of(gnp, s), d_b.at[s, 1], y_b.at[s])

    gather_finish(T_NF0, nf_slot(0))
    gather_forward(T_NF1, nf_slot(1))
    ffn(0)
    gnf_start(0)
    gather_forward(T_GO1, go_slot(1))
    gnf_mid(0)
    gather_finish(T_NF1, nf_slot(1))
    gather_finish(T_GO1, go_slot(1))
    ffn(1)
    gnf_start(1)
    gnf_mid(1)

    w_cross_pass(CONV)
    w_drain(UP)
    nf2 = nf

    def up_grads(i):
        c = ds(i * 256, 256)
        up[c, :] = (
            dot(nf2[0, :, c], gpre[pl.ds(0, seg), :], 0, 0)
            + dot(nf2[1, :, c], gpre[pl.ds(seg, seg), :], 0, 0)
        ).astype(BF)

    loop(4, up_grads)
    gx_start(UP)
    gz_start(CONV)

    for s in range(2):
        c = reduce_end(T_GNF0 + s, rows_of(gnp, s), d_b.at[s, 0], y_b.at[s])
        u, inv = layer_norm(middle[s])
        g = go[s, tslot, :].astype(F32) + norm_back(c, u, inv)
        gm[s] = g
        gm_low[s] = g.astype(BF)
        reduce_drain(T_GNF0 + s, rows_of(gnp, s), d_b.at[s, 1])
    for s in range(2):
        swap_drain(T_ATT0 + s, att_src(s))

    def attended_grads(i):
        part = dot(gm_low[...].reshape(256, 1024), wo[ds(i * 256, 256), :], 1, 1)
        att_own[:, ds(i * 128, 128), :] = part.astype(BF).reshape(2, 128, col)

    loop(4, attended_grads)
    ga_src = lambda p: att_own.at[:, ds(p * 128, 128)]
    ga_dst = lambda p: ga.at[:, ds(p * 128, 128)]
    swap_start(T_GA, ga_src, ga_dst)
    ga[:, tslot, :] = att_own[:, tslot, :]
    for s in range(2):
        gather_drain(T_NF0 + s, nf_slot(s))

    def output_grads(i):
        c = ds(i * 256, 256)
        part = dot(att_rows[:, :, c].reshape(256, 256), gm_low[...].reshape(256, 1024), 0, 0)
        nf[lax.div(i, 2), ds(lax.rem(i, 2) * 256, 256), :] = part.astype(BF)

    loop(4, output_grads)
    op_part = lambda p: nf.at[:, :, ds(p * col, col)]
    reduce_start(T_OP, op_part, d_o.at[1], d_o.at[0])

    def out_parts(i):
        s = lax.div(i, 4)
        rows = ds(s * seg, seg)
        c = ds(lax.rem(i, 4) * 256, 256)
        gpre[rows, c] = dot(act[rows, :], down[:, c]).astype(BF)

    loop(8, out_parts)
    for s in range(2):
        reduce_start(T_OUT0 + s, rows_of(gpre, s), d_a.at[s, 1], d_a.at[s, 0])
    w_drain(DOWN)

    def down_grads(i):
        c = ds(i * 256, 256)
        down[c, :] = (
            dot(act[pl.ds(0, seg), c], go[0], 0, 0) + dot(act[pl.ds(seg, seg), c], go[1], 0, 0)
        ).astype(BF)

    loop(4, down_grads)
    gx_start(DOWN)
    gz_relay(CONV)
    reduce_mid(T_OP, op_part, d_o.at[1], y_o)
    swap_finish(T_GA, ga_dst)

    def attend_back(s, h):
        if True:
            lanes = pl.ds(h * 128, 128)
            vl = pl.ds(col + h * 128, 128)

            def values(i):
                c = ds(i * 512, 512)
                t_v[c, :] = dot(probs[s, h, :, c], ga[s, :, lanes], 0, 0).astype(BF)

            loop(3, values)

            def scores(i):
                rows = ds(i * 128, 128)
                p = probs[s, h, rows, :].astype(F32)
                gp = dot(ga[s, rows, lanes], kv[s, :, vl], 1, 1)
                inner = jnp.sum(p * gp, axis=-1, keepdims=True)
                gs = (p * (gp - inner)).astype(BF)
                probs[s, h, rows, :] = gs
                place = pl.ds(pl.multiple_of(1024 + i * 128, 128), 128)
                t = dot(gs, kv[s, :, lanes])
                t = t * cosines[place, :] - pltpu.roll(t, 64, 1) * sines[place, :]
                t_q[rows, :] = (t * HEAD_DIM ** (-0.5)).astype(BF)

            loop(4, scores)

            def keys(i):
                c = ds(i * 512, 512)
                t = dot(probs[s, h, :, c], qs[s, :, lanes], 0, 0)
                t = t * cosines[c, :] - pltpu.roll(t, 64, 1) * sines[c, :]
                kv[s, c, lanes] = t.astype(BF)
                kv[s, c, vl] = t_v[c, :]

            loop(3, keys)
            qs[s, :, lanes] = t_q[...]

    attend_back(0, 0)
    for s in range(2):
        reduce_mid(T_OUT0 + s, rows_of(gpre, s), d_a.at[s, 1], y_a.at[s])
    gz_start(UP)
    attend_back(0, 1)
    g_final(CONV, None)
    attend_back(1, 0)
    gz_relay(UP)
    attend_back(1, 1)
    gz_start(DOWN)

    reduce_drain(T_OP, op_part, d_o.at[1])
    l_o[...] = reduce_end(T_OP, op_part, d_o.at[0], y_o).astype(BF).reshape(1024, col)
    gx_start(WO)

    def kv_grads(i):
        c = ds(i * 256, 256)
        total = jnp.zeros((256, 2 * col), F32)
        for p in range(3):
            for s in range(2):
                total += dot(unit[p, s, :, c], kv[s, pl.ds(p * seg, seg), :], 0, 0)
        act[c, pl.ds(col, 2 * col)] = total.astype(BF)
        act[c, pl.ds(0, col)] = (
            dot(unit[2, 0, :, c], qs[0], 0, 0) + dot(unit[2, 1, :, c], qs[1], 0, 0)
        ).astype(BF)

    loop(4, kv_grads)
    gx_start(QKV)
    g_final(UP, gain_f)
    gz_relay(DOWN)

    def hidden_grads(i):
        s = lax.div(i, 4)
        c = ds(lax.rem(i, 4) * 256, 256)
        part = dot(kv[s, pl.ds(1024, seg), :], wqkv[c, pl.ds(col, 2 * col)], 1, 1) + dot(
            qs[s], wqkv[c, pl.ds(0, col)], 1, 1
        )
        gnp[ds(s * seg, seg), c] = part.astype(BF)

    loop(8, hidden_grads)
    for s in range(2):
        reduce_start(T_GN0 + s, rows_of(gnp, s), d_b.at[s, 1], d_b.at[s, 0])
    ld_h = load(hidden, gm_low, 13)
    g_pass(CONV)
    for s in range(2):
        reduce_mid(T_GN0 + s, rows_of(gnp, s), d_b.at[s, 1], y_b.at[s])
    gz_start(WO)
    gz_relay(WO)
    w_cross_finish(CONV)
    gather_drain(T_GO, go_slot(0))
    gather_drain(T_GO1, go_slot(1))
    ld_w = [
        load(conv_all.at[pl.ds(i * seg, seg)], go.at[i], 14 + i) for i in range(2)
    ]
    for s in range(2):
        out = reduce_end(T_OUT0 + s, rows_of(gpre, s), d_a.at[s, 0], y_a.at[s])
        reduce_drain(T_OUT0 + s, rows_of(gpre, s), d_a.at[s, 1])
        y_a[s] = (middle[s] + out).astype(BF)
    st_out = load(y_a, layer_out, 16)
    for d in ld_w:
        d.wait()
    swap_drain(T_GA, ga_src)
    w_tap = lambda i, k: go[i, :, pl.ds(k * col, col)]

    def fresh(s, carry):
        taps = []
        for k in range(4):
            rows = memraw.at[s, 1 - k % 2]
            taps.append(
                dot(rows[:, pl.ds(0, seg)], w_tap(0, k)) + dot(rows[:, pl.ds(seg, seg)], w_tap(1, k))
            )
        at = lax.broadcasted_iota(jnp.int32, taps[0].shape, 0)
        total = taps[1] + taps[2]
        total += jnp.where(at == 0, 0.0, pltpu.roll(taps[0], 1, 0))
        total += jnp.where(at == 255, 0.0, pltpu.roll(taps[3], 255, 0))
        att_own[s, pl.ds(0, 256), :] = total.astype(BF)
        return carry

    lax.fori_loop(0, 2, fresh, 0)
    fr_src = lambda p: att_own.at[:, ds(p * 64, 64)]
    fr_dst = lambda p: fresh_out.at[:, :, ds(p * col, col)]
    swap_start(T_FR, fr_src, fr_dst)
    st_fr = load(fr_src(r), fr_dst(r), 17)
    gz_start(QKV)
    g_pass(UP)
    g_final(DOWN, None)
    gz_relay(QKV)

    for s in range(2):
        c = reduce_end(T_GN0 + s, rows_of(gnp, s), d_b.at[s, 0], y_b.at[s])
        if s == 0:
            ld_h.wait()
        u, inv = layer_norm(gm_low[s].astype(F32))
        gm[s] = gm[s] + norm_back(c, u, inv)
    st_gi = load(gm, grad_input, 18)
    g_final(WO, None)
    g_pass(DOWN)
    g_final(QKV, gain_a)
    g_pass(WO)
    g_pass(QKV)

    for p in range(3):
        tm_copy(ctx_src[p], ctx_slot[p](r), T_CTX0 + p, 0, r1).wait_send()
        tm_copy(ctx_src[p], ctx_slot[p](r), T_CTX0 + p, 1, r2).wait_send()
    swap_drain(T_GF, gf_src)
    gather_drain(T_WO, wo_slot)
    for s in range(2):
        reduce_drain(T_GN0 + s, rows_of(gnp, s), d_b.at[s, 1])
    swap_finish(T_FR, fr_dst)
    swap_drain(T_FR, fr_src)
    for d in (st_out, st_fr, st_gi):
        d.wait()
    w_drain(QKV)
    w_drain(WO)
    w_cross_drain(CONV)
    for g in range(5):
        g_drain(g)


def widen(steps, pieces, *refs):
    ins, weights, gains, outs, kept = refs[:8], refs[8:12], refs[12], refs[13:25], refs[25]
    for src, dst in zip(ins[:3], outs):
        dst[...] = src[...]
    qkv, o, up, down, conv = ins[3:]
    outs[8][...] = down[...].astype(F32)
    if len(up.shape) == 2:
        outs[7][...] = up[...].astype(F32)
    else:
        for p in range(PARTS):
            size = up.shape[2] // pieces
            for i in range(pieces):
                there = pl.ds((i * PARTS + p) * size, size)
                outs[7][:, there] = up[p, :, pl.ds(i * size, size)].astype(F32)
    for p in range(PARTS):
        here = pl.ds(p * 256, 256)
        for i in range(3):
            outs[3 + i][:, here] = qkv[p, :, pl.ds(i * 256, 256)].astype(F32)
        outs[6][:, here] = o[p].astype(F32)
        for k in range(4):
            outs[9][k, :, here] = conv[p, :, pl.ds(k * 256, 256)].astype(F32)
    step = pl.program_id(0)
    block = weights[0].shape[0]
    rows = pl.ds(pl.multiple_of(step * block, block), block)
    total = jnp.zeros((block, 1), F32)
    for w, g in zip(weights[:3], outs[3:6]):
        total += jnp.sum(w[...].astype(F32) * g[...], axis=-1, keepdims=True)
    kept[rows, 0:1] = total
    kept[rows, 1:2] = jnp.sum(weights[3][...].astype(F32) * outs[7][...], axis=-1, keepdims=True)

    @pl.when(step == steps - 1)
    def _():
        own = kept.shape[0]
        eye = lax.broadcasted_iota(jnp.int32, (own, own), 0) == lax.broadcasted_iota(
            jnp.int32, (own, own), 1
        )
        for i in range(2):
            line = jnp.sum(jnp.where(eye, kept[:, i : i + 1], 0.0), axis=0, keepdims=True)
            outs[10 + i][...] = line / gains[i : i + 1, :]


def per_device(
    hidden,
    memory,
    compressed,
    reset_flag,
    boundary,
    query_weight,
    key_weight,
    value_weight,
    output_weight,
    up_weight,
    down_weight,
    conv_weight,
    attn_gain,
    ffn_gain,
    grad_out,
    grad_fresh,
):
    groups = lax.axis_size("stream")
    rank = lax.axis_index("tm")
    streams, seg_rows, width = hidden.shape
    own = query_weight.shape[0]
    seg = seg_rows * PARTS
    cols = width // PARTS
    n_z = groups // 2
    ff_rows = down_weight.shape[0] // PARTS
    pieces = groups if ff_rows % 128 == 0 else 1
    up_in = up_weight
    if pieces == 1:
        up_in = lax.dynamic_index_in_dim(
            up_weight.reshape(own, groups, PARTS, ff_rows), rank, 2, keepdims=False
        ).reshape(own, groups * ff_rows)
    gains = jnp.stack([attn_gain, ffn_gain]).astype(F32)
    spots = np.arange(seg)
    places = np.concatenate([spots, seg + spots[::2], seg + spots[1::2], 2 * seg + spots])
    half = HEAD_DIM // 2
    frequency = 10000.0 ** (-np.arange(half) * 2.0 / HEAD_DIM)
    angles = places[:, None] * frequency[None, :]
    cosine = np.cos(angles).astype(np.float32)
    sine = np.sin(angles).astype(np.float32)
    cosines = np.concatenate([cosine, cosine], axis=1)
    sines = np.concatenate([-sine, sine], axis=1)

    hbm = pl.BlockSpec(memory_space=pl.ANY)
    big = (seg * streams, width)
    out_shape = (
        jax.ShapeDtypeStruct(hidden.shape, BF),
        jax.ShapeDtypeStruct(grad_fresh.shape, BF),
        jax.ShapeDtypeStruct(hidden.shape, F32),
        jax.ShapeDtypeStruct((PARTS, own, 3 * cols), BF),
        jax.ShapeDtypeStruct((PARTS, own, cols), BF),
        jax.ShapeDtypeStruct((PARTS, own, width), BF),
        jax.ShapeDtypeStruct((PARTS * own, width), BF),
        jax.ShapeDtypeStruct((PARTS, own, width), BF),
        jax.ShapeDtypeStruct((width, width), BF),
    )

    def v(shape, dtype=BF):
        return pltpu.VMEM(shape, dtype)

    seg2 = (streams, seg, cols)
    rows2 = (streams, seg_rows, width)
    wide = (3 * cols, cols, width, width, width)
    sem = pltpu.SemaphoreType.DMA
    scratch = (
        [
            v((3, streams, seg, width)),
            v((streams, 2, seg // 2, width)),
            v((width, 3 * cols)),
            v((width, width)),
            v(big),
            v(big),
            v(seg2),
            v((streams, 3 * seg, 2 * cols)),
            v((streams, 2, seg, 3 * seg)),
            v(seg2),
            v(rows2),
            v(rows2, F32),
            v((streams, seg, width)),
            v((streams, seg, width)),
            v((streams, seg // 2, cols)),
            v(big),
            v(big),
            v(seg2),
            v(rows2, F32),
            v(rows2),
            v(big),
            v((streams, 2, seg_rows, width)),
            v(rows2),
            v((streams, 2, seg_rows, width)),
            v(rows2),
            v((2, streams, seg, cols)),
            v(seg2),
            v((width, cols)),
            v(big),
        ]
        + [v((n_z * own, c)) for c in wide]
        + [v(((n_z - 1) * own, c)) for c in wide]
        + [v((own, c)) for c in wide]
        + [
            v((3 * seg, HEAD_DIM)),
            v((seg, HEAD_DIM)),
            v((own, 2), F32),
            v((streams, seg, 2), F32),
            v((streams, seg), F32),
            v(boundary.shape, jnp.int32),
            v(gains.shape, F32),
            v(cosines.shape, F32),
            v(sines.shape, F32),
            sem((20 + pieces,)),
            sem((T_COUNT, 3)),
            sem((T_COUNT, 3)),
            sem((5, 2 * n_z + 1)),
            sem((5, 2 * n_z + 1)),
            sem((5, n_z)),
            sem((5, n_z)),
            sem((5, n_z)),
            sem((5, n_z)),
            sem((5, 3)),
            sem((5, 3)),
            sem((5,)),
        ]
    )
    results = pl.pallas_call(
        functools.partial(kernel, n_z, own, pieces),
        out_shape=out_shape,
        in_specs=[hbm] * 16 + [pl.BlockSpec(memory_space=pltpu.SMEM)],
        out_specs=tuple([hbm] * len(out_shape)),
        scratch_shapes=scratch,
        compiler_params=pltpu.CompilerParams(
            collective_id=0, has_side_effects=True, vmem_limit_bytes=64000 * 1024
        ),
        name="layer",
    )(
        hidden,
        memory,
        compressed,
        query_weight,
        key_weight,
        value_weight,
        output_weight,
        up_in,
        down_weight,
        conv_weight,
        grad_out,
        grad_fresh,
        boundary,
        gains,
        cosines,
        sines,
        reset_flag,
    )
    g_up = results[5]
    if pieces == 1:
        g_up = (
            g_up.reshape(PARTS, own, groups, ff_rows)
            .transpose(1, 2, 0, 3)
            .reshape(up_weight.shape)
        )
    steps = max(1, own // 64)
    moved = [*results[:5], g_up, *results[6:8]]
    square = jax.ShapeDtypeStruct((own, width), F32)
    grads = (square,) * 4 + tuple(
        jax.ShapeDtypeStruct(w.shape, F32) for w in (up_weight, down_weight, conv_weight)
    )
    shapes = tuple(jax.ShapeDtypeStruct(t.shape, t.dtype) for t in results[:3]) + grads
    weights = (query_weight, key_weight, value_weight, up_weight)

    def cut(t):
        shape = list(t.shape)
        dim = len(shape) - 2
        shape[dim] //= steps
        return pl.BlockSpec(tuple(shape), lambda i: (0,) * dim + (i, 0))

    line = jax.ShapeDtypeStruct((1, own), F32)
    whole = lambda t: pl.BlockSpec(t.shape, lambda i: (0, 0))
    done = pl.pallas_call(
        functools.partial(widen, steps, pieces),
        grid=(steps,),
        out_shape=shapes + (line, line),
        in_specs=[cut(t) for t in moved] + [cut(t) for t in weights] + [whole(gains)],
        out_specs=tuple([cut(t) for t in shapes] + [whole(line)] * 2),
        scratch_shapes=[pltpu.VMEM((own, 2), F32)],
        compiler_params=pltpu.CompilerParams(vmem_limit_bytes=64000 * 1024),
        name="widen",
    )(*moved, *weights, gains)
    return tuple(done[:10]) + (done[10].reshape(own), done[11].reshape(own))


def solution(mesh):
    act = P("stream", "tm", None)
    row = P("stream", None)
    in_specs = (act, act, act, P("stream"), row) + (row,) * 6 + (
        P(None, "stream", None),
        P("stream"),
        P("stream"),
        act,
        act,
    )
    out_specs = (act, act, act) + (row,) * 6 + (
        P(None, "stream", None),
        P("stream"),
        P("stream"),
    )
    return jax.shard_map(
        per_device, mesh=mesh, in_specs=in_specs, out_specs=out_specs, check_vma=False
    )
```

```python
import functools

import jax
import jax.numpy as jnp
import numpy as np
from jax import lax
from jax.experimental import pallas as pl
from jax.experimental.pallas import tpu as pltpu
from jax.sharding import PartitionSpec as P

HEAD_DIM = 128
PARTS = 4
BF = jnp.bfloat16
F32 = jnp.float32
MESH = pl.DeviceIdType.MESH

QKV, WO, UP, DOWN, CONV = range(5)
(T_CTX0, T_CTX1, T_CTX2, T_GO, T_GF, T_WO, T_ATT0, T_ATT1, T_NF0, T_NF1, T_GNF0, T_GNF1) = range(12)
(T_OUT0, T_OUT1, T_GA, T_OP, T_GN0, T_GN1, T_FR, T_GO1) = range(12, 20)
T_COUNT = 20


def dot(a, b, ca=1, cb=0):
    return lax.dot_general(a, b, (((ca,), (cb,)), ((), ())), preferred_element_type=F32)


def loop(n, body):
    def step(i, carry):
        body(i)
        return carry

    lax.fori_loop(0, n, step, 0)


def ds(start, size):
    return pl.ds(pl.multiple_of(start, size), size)


def mean(x):
    return jnp.sum(x, axis=-1, keepdims=True) * (1.0 / x.shape[-1])


def layer_norm(rows):
    center = rows - mean(rows)
    inv = lax.rsqrt(mean(center * center) + 1e-05)
    return center * inv, inv


def norm_back(c, unit, inv):
    return inv * (c - mean(c) - unit * mean(c * unit))


def kernel(
    n_z,
    own,
    pieces,
    hidden,
    memory,
    compressed,
    query_weight,
    key_weight,
    value_weight,
    output_weight,
    up_weight,
    down_weight,
    conv_weight,
    grad_out,
    grad_fresh,
    boundary_in,
    gains_in,
    cosines_in,
    sines_in,
    reset_flag,
    layer_out,
    fresh_out,
    grad_input,
    out_qkv,
    out_o,
    out_up,
    out_down,
    out_conv,
    conv_all,
    unit,
    memraw,
    wqkv,
    wo,
    up,
    down,
    qs,
    kv,
    probs,
    att_own,
    att_rows,
    middle,
    nf,
    go,
    gf,
    act,
    gpre,
    ga,
    gm,
    gm_low,
    gnp,
    d_a,
    y_a,
    d_b,
    y_b,
    d_o,
    y_o,
    l_o,
    l_conv,
    x_qkv,
    x_o,
    x_up,
    x_down,
    x_conv,
    z_qkv,
    z_o,
    z_up,
    z_down,
    z_conv,
    r_qkv,
    r_o,
    r_up,
    r_down,
    r_conv,
    t_v,
    t_q,
    gain_cols,
    row_info,
    doc_k,
    boundary,
    gains,
    cosines,
    sines,
    loc,
    tm_s,
    tm_r,
    ag_s,
    ag_r,
    rx_s,
    rx_r,
    rz_s,
    rz_r,
    fin_s,
    fin_r,
    fin_l,
):
    st = lax.axis_index("stream")
    r = lax.axis_index("tm")
    z = lax.div(st, 2)
    x = lax.rem(st, 2)
    core = lax.rem(r, 2)
    r1 = r + 1 - 2 * core
    r2 = lax.rem(r + 2, 4)
    r3 = lax.rem(r1 + 2, 4)
    xn = z * 2 + 1 - x
    seg = 512
    col = 256

    def zpeer(dz):
        return lax.rem(z + dz, n_z)

    def zfrom(dz):
        return lax.rem(z + n_z - dz, n_z)

    def load(src, dst, i):
        d = pltpu.make_async_copy(src, dst, loc.at[i])
        d.start()
        return d

    own_rows = ds(st * own, own)
    rcol = ds(r * col, col)
    ld_g = load(gains_in, gains, 16)
    ld_b = load(boundary_in, boundary, 17)
    ld_q = load(query_weight.at[:, rcol], wqkv.at[own_rows, pl.ds(0, col)], 0)
    ld_k = load(key_weight.at[:, rcol], wqkv.at[own_rows, pl.ds(col, col)], 1)
    ld_v = load(value_weight.at[:, rcol], wqkv.at[own_rows, pl.ds(2 * col, col)], 2)
    ld_o = load(output_weight.at[:, rcol], wo.at[own_rows, rcol], 3)
    if pieces > 1:
        size = 1024 // pieces
        ld_up = [
            load(
                up_weight.at[:, ds((i * PARTS + r) * size, size)],
                up.at[own_rows, pl.ds(i * size, size)],
                18 + i,
            )
            for i in range(pieces)
        ]
    else:
        ld_up = [load(up_weight, up.at[own_rows], 4)]
    ld_dn = load(down_weight.at[ds(r * own, own)], down.at[own_rows], 5)
    ld_cv = [
        load(conv_weight.at[k, :, rcol], conv_all.at[own_rows, pl.ds(k * col, col)], 6 + k)
        for k in range(4)
    ]
    tslot = ds(r * 128, 128)
    ld_m = load(memory, att_rows, 11)
    ld_c = {
        0: load(compressed, unit.at[0, :, tslot], 10),
        2: load(hidden, unit.at[2, :, tslot], 12),
    }
    ld_h = load(hidden, gm_low, 13)
    ld_t = [load(cosines_in, cosines, 18 + pieces), load(sines_in, sines, 19 + pieces)]
    ld_go = load(grad_out, go.at[:, tslot], 14)
    ld_gf = load(grad_fresh.at[:, :, rcol], gf.at[:, ds(r * 64, 64)], 15)

    barrier = pltpu.get_barrier_semaphore()
    for peer in (r1, r2, r3):
        pl.semaphore_signal(barrier, 1, device_id=(st, peer), device_id_type=MESH)
    pl.semaphore_signal(barrier, 1, device_id=(xn, r), device_id_type=MESH)

    def greet(i):
        pl.semaphore_signal(
            barrier, 1, device_id=(zpeer(i + 1) * 2 + x, r), device_id_type=MESH
        )

    loop(n_z - 1, greet)

    ld_g.wait()
    eye = lax.broadcasted_iota(jnp.int32, (own, own), 0) == lax.broadcasted_iota(
        jnp.int32, (own, own), 1
    )
    gain_cols[...] = dot(eye.astype(F32).astype(BF), gains[...].astype(BF), 1, 1)
    gain_a = gain_cols[:, 0:1]
    gain_f = gain_cols[:, 1:2]
    for d in (ld_q, ld_k, ld_v):
        d.wait()
    wqkv[own_rows] = (wqkv[own_rows].astype(F32) * gain_a).astype(BF)
    ld_m.wait()
    row = lax.broadcasted_iota(jnp.int32, (128, 128), 0)
    source = 2 * lax.rem(row, 64) + lax.div(row, 64)
    pick = (lax.broadcasted_iota(jnp.int32, (128, 128), 1) == source).astype(F32).astype(BF)
    for s in range(2):
        split = dot(pick, att_rows[s]).astype(BF)
        memraw[s, 0, ds(r * 64, 64), :] = split[:64]
        memraw[s, 1, ds(r * 64, 64), :] = split[64:]
    for d in ld_up:
        d.wait()
    up[own_rows] = (up[own_rows].astype(F32) * gain_f).astype(BF)
    for d in (ld_o, ld_dn):
        d.wait()
    pl.semaphore_wait(barrier, 4 + n_z - 1)

    def tm_copy(src, dst, op, i, peer):
        return pltpu.make_async_remote_copy(
            src, dst, tm_s.at[op, i], tm_r.at[op, i], device_id=(st, peer), device_id_type=MESH
        )

    def gather_start(op, src, slot):
        tm_copy(src, slot(r), op, 1, r2).start()
        tm_copy(src, slot(r), op, 0, r1).start()

    def gather_forward(op, slot):
        tm_copy(slot(r2), slot(r2), op, 1, r2).wait_recv()
        tm_copy(slot(r2), slot(r2), op, 2, r1).start()

    def gather_finish(op, slot):
        tm_copy(slot(r1), slot(r1), op, 0, r1).wait_recv()
        tm_copy(slot(r3), slot(r3), op, 2, r1).wait_recv()

    def gather_drain(op, slot):
        tm_copy(slot(r), slot(r), op, 0, r1).wait_send()
        tm_copy(slot(r), slot(r), op, 1, r2).wait_send()
        tm_copy(slot(r2), slot(r2), op, 2, r1).wait_send()

    peers = ((0, r1), (1, r2), (2, r3))

    def swap_start(op, src, dst):
        for i, p in peers[::-1]:
            tm_copy(src(p), dst(r), op, i, p).start()

    def swap_finish(op, dst):
        for i, p in peers:
            tm_copy(dst(p), dst(p), op, i, p).wait_recv()

    def swap_drain(op, src):
        for i, p in peers:
            tm_copy(src(p), src(p), op, i, p).wait_send()

    def reduce_start(op, part, far, near):
        tm_copy(part(r3), far, op, 0, r1).start()
        tm_copy(part(r1), near, op, 1, r1).start()

    def reduce_mid(op, part, far, land):
        tm_copy(far, far, op, 0, r1).wait_recv()
        far[...] = (far[...].astype(F32) + part(r2)[...].astype(F32)).astype(BF)
        tm_copy(far, land, op, 2, r2).start()

    def reduce_end(op, part, near, land):
        tm_copy(near, near, op, 1, r1).wait_recv()
        tm_copy(land, land, op, 2, r2).wait_recv()
        return part(r)[...].astype(F32) + near[...].astype(F32) + land[...].astype(F32)

    def reduce_drain(op, part, far):
        tm_copy(part(r3), far, op, 0, r1).wait_send()
        tm_copy(part(r1), far, op, 1, r1).wait_send()
        tm_copy(far, far, op, 2, r2).wait_send()

    held = {
        QKV: wqkv,
        WO: wo.at[:, rcol],
        UP: up,
        DOWN: down,
        CONV: conv_all,
    }

    def wslot(g, s):
        return held[g].at[ds(s * own, own)]

    def w_copy(g, s, i, dev, j=None):
        return pltpu.make_async_remote_copy(
            wslot(g, s),
            wslot(g, s),
            ag_s.at[g, i],
            ag_r.at[g, i if j is None else j],
            device_id=(dev, r),
            device_id_type=MESH,
        )

    relay = n_z == 4
    inner = (z == 1) | (z == 2)

    def direct(dz):
        zz = zpeer(dz)
        return (z + 3 != zz) & (zz + 3 != z)

    def w_send_x(g):
        w_copy(g, st, 0, xn).start()

    def w_send_z(g):
        if relay:
            for dz in (1, 3, 2):

                @pl.when(direct(dz))
                def _():
                    w_copy(g, st, dz, zpeer(dz) * 2 + x).start()
        else:
            loop(n_z - 1, lambda i: w_copy(g, st, i + 1, zpeer(i + 1) * 2 + x).start())

    def w_pass(g, dz):
        s = zfrom(dz) * 2 + x
        w_copy(g, s, dz, st).wait_recv()
        w_copy(g, s, n_z + dz - 1, xn).start()

    def w_relay(g):
        s = zfrom(2) * 2 + x
        return w_copy(g, s, 2 * n_z - 1, 3 * (z - 1) * 2 + x, 2 * z - 1)

    last = jnp.where(z == 0, 1, 3)

    def w_forward(g):
        if relay:
            s = zfrom(2) * 2 + x
            w_copy(g, s, 2, st).wait_recv()

            @pl.when(inner)
            def _():
                w_relay(g).start()

            w_copy(g, s, n_z + 1, xn).start()
            w_pass(g, 4 - last)
        else:
            loop(n_z - 1, lambda i: w_pass(g, i + 1))

    def w_forward_last(g):
        if relay:
            w_pass(g, last)

    def w_cross(g):
        w_copy(g, xn, 0, xn).wait_recv()
        if relay:
            for dz in (2, 1, 3):

                @pl.when(direct(dz))
                def _():
                    w_copy(g, xn, n_z + dz - 1, zpeer(dz) * 2 + x).start()
        else:
            loop(n_z - 1, lambda i: w_copy(g, xn, n_z + i, zpeer(i + 1) * 2 + x).start())

    def w_relay_cross(g):
        s = zfrom(2) * 2 + 1 - x
        return w_copy(g, s, 2 * n_z, 3 * (z - 1) * 2 + x, n_z + 2 * z - 2)

    def w_cross_pass(g):
        if relay:
            w_copy(g, zfrom(2) * 2 + x, 2, st).wait_recv()
            w_copy(g, zfrom(2) * 2 + 1 - x, n_z + 1, st).wait_recv()

            @pl.when(inner)
            def _():
                w_relay(g).start()
                w_relay_cross(g).start()

    def w_cross_finish(g):
        rest = (1, 3) if relay else range(1, n_z)
        for dz in rest:
            w_copy(g, zfrom(dz) * 2 + x, dz, st).wait_recv()
            w_copy(g, zfrom(dz) * 2 + 1 - x, n_z + dz - 1, st).wait_recv()

    def w_cross_drain(g):
        w_copy(g, st, 0, xn).wait_send()
        for dz in range(1, n_z):
            if relay:

                @pl.when(direct(dz))
                def _():
                    w_copy(g, st, dz, xn).wait_send()
                    w_copy(g, st, n_z + dz - 1, xn).wait_send()
            else:
                w_copy(g, st, dz, xn).wait_send()
                w_copy(g, st, n_z + dz - 1, xn).wait_send()
        if relay:

            @pl.when(inner)
            def _():
                w_relay(g).wait_send()
                w_relay_cross(g).wait_send()

    def w_finish(g):
        w_copy(g, xn, 0, xn).wait_recv()
        loop(n_z - 1, lambda i: w_copy(g, zfrom(i + 1) * 2 + 1 - x, n_z + i, xn).wait_recv())

    def w_drain(g):
        w_copy(g, st, 0, xn).wait_send()
        loop(n_z - 1, lambda i: w_copy(g, st, n_z + i, xn).wait_send())
        if relay:
            for dz in (1, 2, 3):

                @pl.when(direct(dz))
                def _():
                    w_copy(g, st, dz, xn).wait_send()

            @pl.when(inner)
            def _():
                w_relay(g).wait_send()
        else:
            loop(n_z - 1, lambda i: w_copy(g, st, i + 1, xn).wait_send())

    x_buf = {QKV: x_qkv, WO: x_o, UP: x_up, DOWN: x_down, CONV: x_conv}
    r_buf = {QKV: r_qkv, WO: r_o, UP: r_up, DOWN: r_down, CONV: r_conv}
    z_buf = {QKV: z_qkv, WO: z_o, UP: z_up, DOWN: z_down, CONV: z_conv}
    grads = {QKV: act.at[:, pl.ds(0, 3 * col)], WO: l_o, UP: up, DOWN: down, CONV: l_conv}

    def gx_copy(g, zz):
        return pltpu.make_async_remote_copy(
            grads[g].at[ds((zz * 2 + 1 - x) * own, own)],
            x_buf[g].at[ds(zz * own, own)],
            rx_s.at[g, zz],
            rx_r.at[g, zz],
            device_id=(xn, r),
            device_id_type=MESH,
        )

    def gx_start(g):
        if relay:
            for dz in (1, 3, 2, 0):
                gx_copy(g, zpeer(dz)).start()
        else:
            loop(n_z, lambda i: gx_copy(g, zpeer(i + 1)).start())

    def gz_copy(g, dz, zz):
        return pltpu.make_async_remote_copy(
            x_buf[g].at[ds(zz * own, own)],
            z_buf[g].at[ds((dz - 1) * own, own)],
            rz_s.at[g, dz],
            rz_r.at[g, dz],
            device_id=(zz * 2 + x, r),
            device_id_type=MESH,
        )

    def gz_fold(g, zz):
        gx_copy(g, zz).wait_recv()
        rows = ds(zz * own, own)
        x_buf[g][rows] = (
            x_buf[g][rows].astype(F32) + grads[g][ds((zz * 2 + x) * own, own)].astype(F32)
        ).astype(BF)

    def gz_far(g, dz, zz):
        return pltpu.make_async_remote_copy(
            x_buf[g].at[ds(zz * own, own)],
            r_buf[g],
            rz_s.at[g, dz],
            rz_r.at[g, 0],
            device_id=(jnp.where(z == 0, 1, 2) * 2 + x, r),
            device_id_type=MESH,
        )

    def gz_start(g):
        if not relay:

            def one(i):
                zz = zpeer(i + 1)
                gz_fold(g, zz)
                gz_copy(g, i + 1, zz).start()

            loop(n_z - 1, one)
            return
        for dz in (1, 3):
            zz = zpeer(dz)
            gz_fold(g, zz)

            @pl.when(direct(dz))
            def _():
                gz_copy(g, dz, zz).start()

            @pl.when(jnp.logical_not(direct(dz)))
            def _():
                gz_far(g, dz, zz).start()

        @pl.when(jnp.logical_not(inner))
        def _():
            gz_fold(g, zpeer(2))
            gz_copy(g, 2, zpeer(2)).start()

    def gz_relay(g):
        if relay:

            @pl.when(inner)
            def _():
                zz = zpeer(2)
                gz_fold(g, zz)
                gz_far(g, 2, zz).wait_recv()
                rows = ds(zz * own, own)
                x_buf[g][rows] = (x_buf[g][rows].astype(F32) + r_buf[g][...].astype(F32)).astype(BF)
                gz_copy(g, 2, zz).start()

    outs = {
        QKV: (((0, 3 * col), lambda p: out_qkv.at[p]),),
        WO: (((0, col), lambda p: out_o.at[p]),),
        UP: (((0, 1024), lambda p: out_up.at[p]),),
        DOWN: (((0, 1024), lambda p: out_down.at[ds(p * own, own)]),),
        CONV: (((0, 1024), lambda p: out_conv.at[p]),),
    }
    fin_base = {g: g for g in range(5)}

    def fin_copy(g, j, i, p, slot_rank):
        (lane, size), slot = outs[g][j]
        n = fin_base[g] + j
        return pltpu.make_async_remote_copy(
            x_buf[g].at[ds(z * own, own), pl.ds(lane, size)],
            slot(slot_rank),
            fin_s.at[n, i],
            fin_r.at[n, i],
            device_id=(st, p),
            device_id_type=MESH,
        )

    def g_keep(g, j):
        (lane, size), slot = outs[g][j]
        return pltpu.make_async_copy(
            x_buf[g].at[ds(z * own, own), pl.ds(lane, size)], slot(r), fin_l.at[fin_base[g] + j]
        )

    def g_final(g, gain):
        gx_copy(g, z).wait_recv()
        rows = ds(z * own, own)
        total = x_buf[g][rows].astype(F32) + grads[g][ds((z * 2 + x) * own, own)].astype(F32)
        for dz in range(1, n_z):
            if relay:

                @pl.when(direct(n_z - dz))
                def _():
                    gz_copy(g, dz, zpeer(dz)).wait_recv()
            else:
                gz_copy(g, dz, zpeer(dz)).wait_recv()
            total = total + z_buf[g][pl.ds((dz - 1) * own, own)].astype(F32)
        if gain is not None:
            total = total * gain
        x_buf[g][rows] = total.astype(BF)
        for j in range(len(outs[g])):
            fin_copy(g, j, 1, r2, r).start()
            fin_copy(g, j, 0, r1, r).start()
            g_keep(g, j).start()

    def fin_pass(g, j):
        slot = outs[g][j][1](r2)
        n = fin_base[g] + j
        return pltpu.make_async_remote_copy(
            slot, slot, fin_s.at[n, 2], fin_r.at[n, 2], device_id=(st, r1), device_id_type=MESH
        )

    def g_pass(g):
        for j in range(len(outs[g])):
            fin_copy(g, j, 1, r2, r2).wait_recv()
            fin_pass(g, j).start()

    def g_drain(g):
        loop(n_z, lambda i: gx_copy(g, i).wait_send())
        loop(n_z - 1, lambda i: gz_copy(g, i + 1, zpeer(i + 1)).wait_send())
        for j in range(len(outs[g])):
            fin_copy(g, j, 0, r1, r1).wait()
            fin_copy(g, j, 1, r2, r).wait_send()
            fin_pass(g, j).wait()
            g_keep(g, j).wait()

    ctx_slot = (
        lambda p: unit.at[0, :, ds(p * 128, 128)],
        lambda p: memraw.at[:, :, ds(p * 64, 64)],
        lambda p: unit.at[2, :, ds(p * 128, 128)],
    )
    gather_start(T_CTX0, compressed, ctx_slot[0])
    w_send_x(QKV)
    w_send_z(QKV)
    gather_start(T_CTX1, ctx_slot[1](r), ctx_slot[1])
    gather_start(T_CTX2, hidden, ctx_slot[2])
    ctx_src = (compressed, ctx_slot[1](r), hidden)
    gf_src = lambda p: grad_fresh.at[:, :, ds(p * col, col)]
    gf_dst = lambda p: gf.at[:, ds(p * 64, 64)]
    swap_start(T_GF, gf_src, gf_dst)
    w_send_x(WO)
    w_send_z(WO)
    w_send_z(UP)
    w_send_z(DOWN)
    if relay:
        for end, dz in ((0, 1), (3, 3)):

            @pl.when(z == end)
            def _():
                for g in range(5):
                    z_buf[g][pl.ds((dz - 1) * own, own)] = jnp.zeros((own, z_buf[g].shape[1]), BF)

    before = lax.broadcasted_iota(jnp.int32, (seg, seg), 1) <= lax.broadcasted_iota(
        jnp.int32, (seg, seg), 0
    )
    before = before.astype(F32).astype(BF)
    ld_b.wait()
    starts = boundary[...].astype(F32).astype(BF)
    docs = dot(before, starts, 1, 1)
    doc_k[...] = dot(starts, before, 1, 1)
    for s in range(2):
        row_info[s, :, 0:1] = docs[:, s : s + 1]
        away = docs[:, s : s + 1] + reset_flag[s].astype(F32)
        row_info[s, :, 1:2] = jnp.where(away == 0.0, 0.0, -1e30)

    def norm_block(p, rank):
        def one(s):
            if p == 1:
                for half in range(2):
                    raw = memraw[s, half, ds(rank * 64, 64), :]
                    unit[p, s, ds(half * 256 + rank * 64, 64), :] = layer_norm(raw.astype(F32))[
                        0
                    ].astype(BF)
            else:
                rows = ds(rank * 128, 128)
                unit[p, s, rows, :] = layer_norm(unit[p, s, rows, :].astype(F32))[0].astype(BF)

        loop(2, one)

    def context(p, meanwhile=None):
        op, slot = T_CTX0 + p, ctx_slot[p]
        if p in ld_c:
            ld_c[p].wait()
        norm_block(p, r)
        gather_forward(op, slot)
        if meanwhile is not None:
            meanwhile()
        tm_copy(slot(r1), slot(r1), op, 0, r1).wait_recv()
        norm_block(p, r1)
        tm_copy(slot(r3), slot(r3), op, 2, r1).wait_recv()
        norm_block(p, r3)
        tm_copy(slot(r2), slot(r2), op, 2, r1).wait_send()
        norm_block(p, r2)

    def project(p):
        def one(i):
            s = lax.div(i, 2)
            at = lax.rem(i, 2) * 256
            rows = ds(at, 256)
            place = pl.ds(pl.multiple_of(p * seg + at, 256), 256)
            a = unit[p, s, rows, :]
            cs = cosines[place, :]
            sn = sines[place, :]

            def rot(t):
                return t * cs + pltpu.roll(t, 64, 1) * sn

            both = dot(a, wqkv[:, pl.ds(col, 2 * col)])
            for h in range(2):
                kv[s, place, pl.ds(h * 128, 128)] = rot(both[:, h * 128 : h * 128 + 128]).astype(BF)
            kv[s, place, pl.ds(col, col)] = both[:, col:].astype(BF)
            if p == 2:
                q = dot(a, wqkv[:, pl.ds(0, col)])
                for h in range(2):
                    qs[s, rows, pl.ds(h * 128, 128)] = (
                        rot(q[:, h * 128 : h * 128 + 128]) * HEAD_DIM ** (-0.5)
                    ).astype(BF)

        loop(4, one)

    context(0)
    w_forward(QKV)
    w_forward(WO)
    for d in ld_cv:
        d.wait()
    w_send_x(CONV)
    w_send_z(CONV)
    for d in ld_t:
        d.wait()
    context(1)
    w_forward_last(QKV)
    w_forward_last(WO)
    w_send_x(UP)
    w_send_x(DOWN)
    w_finish(QKV)
    project(0)
    project(1)
    w_forward(UP)
    w_cross(CONV)
    wo_slot = lambda p: wo.at[:, ds(p * col, col)]
    go_slot = lambda s: lambda p: go.at[s, ds(p * 128, 128)]

    def gather_wo():
        w_finish(WO)
        gather_start(T_WO, wo_slot(r), wo_slot)

    context(2, gather_wo)
    w_forward_last(UP)
    project(2)

    ld_gf.wait()
    swap_finish(T_GF, gf_dst)

    def conv_grads(i):
        c = ds(i * 256, 256)
        even_acc = jnp.zeros((256, 512), F32)
        odd_acc = jnp.zeros((256, 512), F32)
        for s in range(2):
            g = gf[s].astype(F32)
            at = lax.broadcasted_iota(jnp.int32, g.shape, 0)
            ahead = jnp.where(at == 255, 0.0, pltpu.roll(g, 255, 0))
            behind = jnp.where(at == 0, 0.0, pltpu.roll(g, 1, 0))
            low = gf[s]
            odd_acc += dot(memraw[s, 1, :, c], jnp.concatenate([ahead.astype(BF), low], 1), 0, 0)
            even_acc += dot(memraw[s, 0, :, c], jnp.concatenate([low, behind.astype(BF)], 1), 0, 0)
        l_conv[c, pl.ds(0, col)] = odd_acc[:, :col].astype(BF)
        l_conv[c, pl.ds(col, col)] = even_acc[:, :col].astype(BF)
        l_conv[c, pl.ds(2 * col, col)] = odd_acc[:, col:].astype(BF)
        l_conv[c, pl.ds(3 * col, col)] = even_acc[:, col:].astype(BF)

    loop(4, conv_grads)

    def attend(s):
        def one(qt):
            rows = ds(qt * 128, 128)
            shape = (128, seg)
            below = lax.broadcasted_iota(jnp.int32, shape, 1) <= (
                lax.broadcasted_iota(jnp.int32, shape, 0) + qt * 128
            )
            info = row_info[s, rows, :]
            same = doc_k[pl.ds(s, 1), :] == info[:, 0:1]
            seen = below & same
            bias = info[:, 1:2]
            for h in range(2):
                lanes = pl.ds(h * 128, 128)
                q = qs[s, rows, lanes]
                far = dot(q, kv[s, pl.ds(0, 1024), lanes], 1, 1) + bias
                near = jnp.where(seen, dot(q, kv[s, pl.ds(1024, seg), lanes], 1, 1), -1e30)
                top = jnp.maximum(
                    jnp.max(far, axis=-1, keepdims=True), jnp.max(near, axis=-1, keepdims=True)
                )
                far = jnp.exp(far - top)
                near = jnp.exp(near - top)
                inv = 1.0 / (
                    jnp.sum(far, axis=-1, keepdims=True) + jnp.sum(near, axis=-1, keepdims=True)
                )
                far = (far * inv).astype(BF)
                near = (near * inv).astype(BF)
                probs[s, h, rows, pl.ds(0, 1024)] = far
                probs[s, h, rows, pl.ds(1024, seg)] = near
                vl = pl.ds(col + h * 128, 128)
                o = dot(far, kv[s, pl.ds(0, 1024), vl]) + dot(near, kv[s, pl.ds(1024, seg), vl])
                att_own[s, rows, lanes] = o.astype(BF)

        loop(4, one)

    att_src = lambda s: lambda p: att_own.at[s, ds(p * 128, 128)]
    att_dst = lambda s: lambda p: att_rows.at[s, :, ds(p * col, col)]

    def attend_send(s):
        swap_start(T_ATT0 + s, att_src(s), att_dst(s))
        att_rows[s, :, rcol] = att_own[s, tslot, :]

    gather_start(T_GO, grad_out.at[0], go_slot(0))
    attend(0)
    attend_send(0)
    w_forward(DOWN)
    gather_forward(T_WO, wo_slot)
    attend(1)
    attend_send(1)
    w_forward_last(DOWN)
    gx_start(CONV)
    gather_forward(T_GO, go_slot(0))

    swap_finish(T_ATT0, att_dst(0))
    swap_finish(T_ATT1, att_dst(1))
    gather_finish(T_WO, wo_slot)
    ld_h.wait()

    def project_out(i):
        c = ds(i * 256, 256)
        mid = dot(att_rows[...].reshape(256, 1024), wo[:, c]).reshape(2, 128, 256)
        middle[:, :, c] = gm_low[:, :, c].astype(F32) + mid

    loop(4, project_out)
    nf_slot = lambda s: lambda p: nf.at[s, ds(p * 128, 128)]
    for s in range(2):
        nf[s, tslot, :] = layer_norm(middle[s])[0].astype(BF)
        gather_start(T_NF0 + s, nf_slot(s)(r), nf_slot(s))
    gather_start(T_GO1, grad_out.at[1], go_slot(1))
    ld_go.wait()
    gather_forward(T_NF0, nf_slot(0))
    gather_finish(T_GO, go_slot(0))
    w_finish(UP)
    w_finish(DOWN)

    def ffn(s):
        def one(i):
            c = ds(i * 256, 256)
            pre = dot(nf[s], up[:, c])
            g_act = dot(go[s], down[c, :], 1, 1)
            phi = 0.5 + 0.5 * lax.erf(pre * 0.7071067811865476)
            act[pl.ds(s * seg, seg), c] = (pre * phi).astype(BF)
            slope = phi + pre * (jnp.exp(pre * pre * -0.5) * 0.3989422804014327)
            gpre[pl.ds(s * seg, seg), c] = (g_act * slope).astype(BF)

        loop(4, one)

        def back(i):
            c = ds(i * 256, 256)
            gnp[pl.ds(s * seg, seg), c] = dot(
                gpre[pl.ds(s * seg, seg), :], up[c, :], 1, 1
            ).astype(BF)

        loop(4, back)

    def rows_of(buf, s):
        return lambda p: buf.at[pl.ds(pl.multiple_of(s * seg + p * 128, 128), 128)]

    def gnf_start(s):
        reduce_start(T_GNF0 + s, rows_of(gnp, s), d_b.at[s, 1], d_b.at[s, 0])

    def gnf_mid(s):
        reduce_mid(T_GNF0 + s, rows_of(gnp, s), d_b.at[s, 1], y_b.at[s])

    gather_finish(T_NF0, nf_slot(0))
    gather_forward(T_NF1, nf_slot(1))
    ffn(0)
    gnf_start(0)
    gather_forward(T_GO1, go_slot(1))
    gnf_mid(0)
    gather_finish(T_NF1, nf_slot(1))
    gather_finish(T_GO1, go_slot(1))
    ffn(1)
    gnf_start(1)
    gnf_mid(1)

    w_cross_pass(CONV)
    w_drain(UP)
    nf2 = nf

    def up_grads(i):
        c = ds(i * 256, 256)
        up[c, :] = (
            dot(nf2[0, :, c], gpre[pl.ds(0, seg), :], 0, 0)
            + dot(nf2[1, :, c], gpre[pl.ds(seg, seg), :], 0, 0)
        ).astype(BF)

    loop(4, up_grads)
    gx_start(UP)
    gz_start(CONV)

    for s in range(2):
        c = reduce_end(T_GNF0 + s, rows_of(gnp, s), d_b.at[s, 0], y_b.at[s])
        u, inv = layer_norm(middle[s])
        g = go[s, tslot, :].astype(F32) + norm_back(c, u, inv)
        gm[s] = g
        gm_low[s] = g.astype(BF)
        reduce_drain(T_GNF0 + s, rows_of(gnp, s), d_b.at[s, 1])
    for s in range(2):
        swap_drain(T_ATT0 + s, att_src(s))

    def attended_grads(i):
        part = dot(gm_low[...].reshape(256, 1024), wo[ds(i * 256, 256), :], 1, 1)
        att_own[:, ds(i * 128, 128), :] = part.astype(BF).reshape(2, 128, col)

    loop(4, attended_grads)
    ga_src = lambda p: att_own.at[:, ds(p * 128, 128)]
    ga_dst = lambda p: ga.at[:, ds(p * 128, 128)]
    swap_start(T_GA, ga_src, ga_dst)
    ga[:, tslot, :] = att_own[:, tslot, :]
    for s in range(2):
        gather_drain(T_NF0 + s, nf_slot(s))

    def output_grads(i):
        c = ds(i * 256, 256)
        part = dot(att_rows[:, :, c].reshape(256, 256), gm_low[...].reshape(256, 1024), 0, 0)
        nf[lax.div(i, 2), ds(lax.rem(i, 2) * 256, 256), :] = part.astype(BF)

    loop(4, output_grads)
    op_part = lambda p: nf.at[:, :, ds(p * col, col)]
    reduce_start(T_OP, op_part, d_o.at[1], d_o.at[0])

    def out_parts(i):
        s = lax.div(i, 4)
        rows = ds(s * seg, seg)
        c = ds(lax.rem(i, 4) * 256, 256)
        gpre[rows, c] = dot(act[rows, :], down[:, c]).astype(BF)

    loop(8, out_parts)
    for s in range(2):
        reduce_start(T_OUT0 + s, rows_of(gpre, s), d_a.at[s, 1], d_a.at[s, 0])
    w_drain(DOWN)

    def down_grads(i):
        c = ds(i * 256, 256)
        down[c, :] = (
            dot(act[pl.ds(0, seg), c], go[0], 0, 0) + dot(act[pl.ds(seg, seg), c], go[1], 0, 0)
        ).astype(BF)

    loop(4, down_grads)
    gx_start(DOWN)
    gz_relay(CONV)
    reduce_mid(T_OP, op_part, d_o.at[1], y_o)
    swap_finish(T_GA, ga_dst)

    def attend_back(s, h):
        if True:
            lanes = pl.ds(h * 128, 128)
            vl = pl.ds(col + h * 128, 128)

            def values(i):
                c = ds(i * 512, 512)
                t_v[c, :] = dot(probs[s, h, :, c], ga[s, :, lanes], 0, 0).astype(BF)

            loop(3, values)

            def scores(i):
                rows = ds(i * 128, 128)
                p = probs[s, h, rows, :].astype(F32)
                gp = dot(ga[s, rows, lanes], kv[s, :, vl], 1, 1)
                inner = jnp.sum(p * gp, axis=-1, keepdims=True)
                gs = (p * (gp - inner)).astype(BF)
                probs[s, h, rows, :] = gs
                place = pl.ds(pl.multiple_of(1024 + i * 128, 128), 128)
                t = dot(gs, kv[s, :, lanes])
                t = t * cosines[place, :] - pltpu.roll(t, 64, 1) * sines[place, :]
                t_q[rows, :] = (t * HEAD_DIM ** (-0.5)).astype(BF)

            loop(4, scores)

            def keys(i):
                c = ds(i * 512, 512)
                t = dot(probs[s, h, :, c], qs[s, :, lanes], 0, 0)
                t = t * cosines[c, :] - pltpu.roll(t, 64, 1) * sines[c, :]
                kv[s, c, lanes] = t.astype(BF)
                kv[s, c, vl] = t_v[c, :]

            loop(3, keys)
            qs[s, :, lanes] = t_q[...]

    attend_back(0, 0)
    w_cross_finish(CONV)

    gather_drain(T_GO, go_slot(0))
    gather_drain(T_GO1, go_slot(1))
    ld_w = [
        load(conv_all.at[pl.ds(i * seg, seg)], go.at[i], 14 + i) for i in range(2)
    ]
    for d in ld_w:
        d.wait()
    swap_drain(T_GA, ga_src)
    w_tap = lambda i, k: go[i, :, pl.ds(k * col, col)]

    def fresh(s, carry):
        taps = []
        for k in range(4):
            rows = memraw.at[s, 1 - k % 2]
            taps.append(
                dot(rows[:, pl.ds(0, seg)], w_tap(0, k)) + dot(rows[:, pl.ds(seg, seg)], w_tap(1, k))
            )
        at = lax.broadcasted_iota(jnp.int32, taps[0].shape, 0)
        total = taps[1] + taps[2]
        total += jnp.where(at == 0, 0.0, pltpu.roll(taps[0], 1, 0))
        total += jnp.where(at == 255, 0.0, pltpu.roll(taps[3], 255, 0))
        att_own[s, pl.ds(0, 256), :] = total.astype(BF)
        return carry

    lax.fori_loop(0, 2, fresh, 0)
    fr_src = lambda p: att_own.at[:, ds(p * 64, 64)]
    fr_dst = lambda p: fresh_out.at[:, :, ds(p * col, col)]
    swap_start(T_FR, fr_src, fr_dst)
    st_fr = load(fr_src(r), fr_dst(r), 17)

    for s in range(2):
        reduce_mid(T_OUT0 + s, rows_of(gpre, s), d_a.at[s, 1], y_a.at[s])
    gz_start(UP)
    attend_back(0, 1)
    g_final(CONV, None)
    attend_back(1, 0)
    gz_relay(UP)
    attend_back(1, 1)
    gz_start(DOWN)

    reduce_drain(T_OP, op_part, d_o.at[1])
    l_o[...] = reduce_end(T_OP, op_part, d_o.at[0], y_o).astype(BF).reshape(1024, col)
    gx_start(WO)

    def kv_grads(i):
        c = ds(i * 256, 256)
        total = jnp.zeros((256, 2 * col), F32)
        for p in range(3):
            for s in range(2):
                total += dot(unit[p, s, :, c], kv[s, pl.ds(p * seg, seg), :], 0, 0)
        act[c, pl.ds(col, 2 * col)] = total.astype(BF)
        act[c, pl.ds(0, col)] = (
            dot(unit[2, 0, :, c], qs[0], 0, 0) + dot(unit[2, 1, :, c], qs[1], 0, 0)
        ).astype(BF)

    loop(4, kv_grads)
    gx_start(QKV)
    g_final(UP, gain_f)
    gz_relay(DOWN)

    def hidden_grads(i):
        s = lax.div(i, 4)
        c = ds(lax.rem(i, 4) * 256, 256)
        part = dot(kv[s, pl.ds(1024, seg), :], wqkv[c, pl.ds(col, 2 * col)], 1, 1) + dot(
            qs[s], wqkv[c, pl.ds(0, col)], 1, 1
        )
        gnp[ds(s * seg, seg), c] = part.astype(BF)

    loop(8, hidden_grads)
    for s in range(2):
        reduce_start(T_GN0 + s, rows_of(gnp, s), d_b.at[s, 1], d_b.at[s, 0])
    ld_h = load(hidden, gm_low, 13)
    g_pass(CONV)
    for s in range(2):
        reduce_mid(T_GN0 + s, rows_of(gnp, s), d_b.at[s, 1], y_b.at[s])
    gz_start(WO)
    gz_relay(WO)
    for s in range(2):
        out = reduce_end(T_OUT0 + s, rows_of(gpre, s), d_a.at[s, 0], y_a.at[s])
        reduce_drain(T_OUT0 + s, rows_of(gpre, s), d_a.at[s, 1])
        y_a[s] = (middle[s] + out).astype(BF)
    st_out = load(y_a, layer_out, 16)
    gz_start(QKV)
    g_pass(UP)
    g_final(DOWN, None)
    gz_relay(QKV)

    for s in range(2):
        c = reduce_end(T_GN0 + s, rows_of(gnp, s), d_b.at[s, 0], y_b.at[s])
        if s == 0:
            ld_h.wait()
        u, inv = layer_norm(gm_low[s].astype(F32))
        gm[s] = gm[s] + norm_back(c, u, inv)
    st_gi = load(gm, grad_input, 18)
    g_final(WO, None)
    g_pass(DOWN)
    g_final(QKV, gain_a)
    g_pass(WO)
    g_pass(QKV)

    for p in range(3):
        tm_copy(ctx_src[p], ctx_slot[p](r), T_CTX0 + p, 0, r1).wait_send()
        tm_copy(ctx_src[p], ctx_slot[p](r), T_CTX0 + p, 1, r2).wait_send()
    swap_drain(T_GF, gf_src)
    gather_drain(T_WO, wo_slot)
    for s in range(2):
        reduce_drain(T_GN0 + s, rows_of(gnp, s), d_b.at[s, 1])
    swap_finish(T_FR, fr_dst)
    swap_drain(T_FR, fr_src)
    for d in (st_out, st_fr, st_gi):
        d.wait()
    w_drain(QKV)
    w_drain(WO)
    w_cross_drain(CONV)
    for g in range(5):
        g_drain(g)


def widen(steps, pieces, *refs):
    ins, weights, gains, outs, kept = refs[:8], refs[8:12], refs[12], refs[13:25], refs[25]
    for src, dst in zip(ins[:3], outs):
        dst[...] = src[...]
    qkv, o, up, down, conv = ins[3:]
    outs[8][...] = down[...].astype(F32)
    if len(up.shape) == 2:
        outs[7][...] = up[...].astype(F32)
    else:
        for p in range(PARTS):
            size = up.shape[2] // pieces
            for i in range(pieces):
                there = pl.ds((i * PARTS + p) * size, size)
                outs[7][:, there] = up[p, :, pl.ds(i * size, size)].astype(F32)
    for p in range(PARTS):
        here = pl.ds(p * 256, 256)
        for i in range(3):
            outs[3 + i][:, here] = qkv[p, :, pl.ds(i * 256, 256)].astype(F32)
        outs[6][:, here] = o[p].astype(F32)
        for k in range(4):
            outs[9][k, :, here] = conv[p, :, pl.ds(k * 256, 256)].astype(F32)
    step = pl.program_id(0)
    block = weights[0].shape[0]
    rows = pl.ds(pl.multiple_of(step * block, block), block)
    total = jnp.zeros((block, 1), F32)
    for w, g in zip(weights[:3], outs[3:6]):
        total += jnp.sum(w[...].astype(F32) * g[...], axis=-1, keepdims=True)
    kept[rows, 0:1] = total
    kept[rows, 1:2] = jnp.sum(weights[3][...].astype(F32) * outs[7][...], axis=-1, keepdims=True)

    @pl.when(step == steps - 1)
    def _():
        own = kept.shape[0]
        eye = lax.broadcasted_iota(jnp.int32, (own, own), 0) == lax.broadcasted_iota(
            jnp.int32, (own, own), 1
        )
        for i in range(2):
            line = jnp.sum(jnp.where(eye, kept[:, i : i + 1], 0.0), axis=0, keepdims=True)
            outs[10 + i][...] = line / gains[i : i + 1, :]


def per_device(
    hidden,
    memory,
    compressed,
    reset_flag,
    boundary,
    query_weight,
    key_weight,
    value_weight,
    output_weight,
    up_weight,
    down_weight,
    conv_weight,
    attn_gain,
    ffn_gain,
    grad_out,
    grad_fresh,
):
    groups = lax.axis_size("stream")
    rank = lax.axis_index("tm")
    streams, seg_rows, width = hidden.shape
    own = query_weight.shape[0]
    seg = seg_rows * PARTS
    cols = width // PARTS
    n_z = groups // 2
    ff_rows = down_weight.shape[0] // PARTS
    pieces = groups if ff_rows % 128 == 0 else 1
    up_in = up_weight
    if pieces == 1:
        up_in = lax.dynamic_index_in_dim(
            up_weight.reshape(own, groups, PARTS, ff_rows), rank, 2, keepdims=False
        ).reshape(own, groups * ff_rows)
    gains = jnp.stack([attn_gain, ffn_gain]).astype(F32)
    spots = np.arange(seg)
    places = np.concatenate([spots, seg + spots[::2], seg + spots[1::2], 2 * seg + spots])
    half = HEAD_DIM // 2
    frequency = 10000.0 ** (-np.arange(half) * 2.0 / HEAD_DIM)
    angles = places[:, None] * frequency[None, :]
    cosine = np.cos(angles).astype(np.float32)
    sine = np.sin(angles).astype(np.float32)
    cosines = np.concatenate([cosine, cosine], axis=1)
    sines = np.concatenate([-sine, sine], axis=1)

    hbm = pl.BlockSpec(memory_space=pl.ANY)
    big = (seg * streams, width)
    out_shape = (
        jax.ShapeDtypeStruct(hidden.shape, BF),
        jax.ShapeDtypeStruct(grad_fresh.shape, BF),
        jax.ShapeDtypeStruct(hidden.shape, F32),
        jax.ShapeDtypeStruct((PARTS, own, 3 * cols), BF),
        jax.ShapeDtypeStruct((PARTS, own, cols), BF),
        jax.ShapeDtypeStruct((PARTS, own, width), BF),
        jax.ShapeDtypeStruct((PARTS * own, width), BF),
        jax.ShapeDtypeStruct((PARTS, own, width), BF),
        jax.ShapeDtypeStruct((width, width), BF),
    )

    def v(shape, dtype=BF):
        return pltpu.VMEM(shape, dtype)

    seg2 = (streams, seg, cols)
    rows2 = (streams, seg_rows, width)
    wide = (3 * cols, cols, width, width, width)
    sem = pltpu.SemaphoreType.DMA
    scratch = (
        [
            v((3, streams, seg, width)),
            v((streams, 2, seg // 2, width)),
            v((width, 3 * cols)),
            v((width, width)),
            v(big),
            v(big),
            v(seg2),
            v((streams, 3 * seg, 2 * cols)),
            v((streams, 2, seg, 3 * seg)),
            v(seg2),
            v(rows2),
            v(rows2, F32),
            v((streams, seg, width)),
            v((streams, seg, width)),
            v((streams, seg // 2, cols)),
            v(big),
            v(big),
            v(seg2),
            v(rows2, F32),
            v(rows2),
            v(big),
            v((streams, 2, seg_rows, width)),
            v(rows2),
            v((streams, 2, seg_rows, width)),
            v(rows2),
            v((2, streams, seg, cols)),
            v(seg2),
            v((width, cols)),
            v(big),
        ]
        + [v((n_z * own, c)) for c in wide]
        + [v(((n_z - 1) * own, c)) for c in wide]
        + [v((own, c)) for c in wide]
        + [
            v((3 * seg, HEAD_DIM)),
            v((seg, HEAD_DIM)),
            v((own, 2), F32),
            v((streams, seg, 2), F32),
            v((streams, seg), F32),
            v(boundary.shape, jnp.int32),
            v(gains.shape, F32),
            v(cosines.shape, F32),
            v(sines.shape, F32),
            sem((20 + pieces,)),
            sem((T_COUNT, 3)),
            sem((T_COUNT, 3)),
            sem((5, 2 * n_z + 1)),
            sem((5, 2 * n_z + 1)),
            sem((5, n_z)),
            sem((5, n_z)),
            sem((5, n_z)),
            sem((5, n_z)),
            sem((5, 3)),
            sem((5, 3)),
            sem((5,)),
        ]
    )
    results = pl.pallas_call(
        functools.partial(kernel, n_z, own, pieces),
        out_shape=out_shape,
        in_specs=[hbm] * 16 + [pl.BlockSpec(memory_space=pltpu.SMEM)],
        out_specs=tuple([hbm] * len(out_shape)),
        scratch_shapes=scratch,
        compiler_params=pltpu.CompilerParams(
            collective_id=0, has_side_effects=True, vmem_limit_bytes=64000 * 1024
        ),
        name="layer",
    )(
        hidden,
        memory,
        compressed,
        query_weight,
        key_weight,
        value_weight,
        output_weight,
        up_in,
        down_weight,
        conv_weight,
        grad_out,
        grad_fresh,
        boundary,
        gains,
        cosines,
        sines,
        reset_flag,
    )
    g_up = results[5]
    if pieces == 1:
        g_up = (
            g_up.reshape(PARTS, own, groups, ff_rows)
            .transpose(1, 2, 0, 3)
            .reshape(up_weight.shape)
        )
    steps = max(1, own // 64)
    moved = [*results[:5], g_up, *results[6:8]]
    square = jax.ShapeDtypeStruct((own, width), F32)
    grads = (square,) * 4 + tuple(
        jax.ShapeDtypeStruct(w.shape, F32) for w in (up_weight, down_weight, conv_weight)
    )
    shapes = tuple(jax.ShapeDtypeStruct(t.shape, t.dtype) for t in results[:3]) + grads
    weights = (query_weight, key_weight, value_weight, up_weight)

    def cut(t):
        shape = list(t.shape)
        dim = len(shape) - 2
        shape[dim] //= steps
        return pl.BlockSpec(tuple(shape), lambda i: (0,) * dim + (i, 0))

    line = jax.ShapeDtypeStruct((1, own), F32)
    whole = lambda t: pl.BlockSpec(t.shape, lambda i: (0, 0))
    done = pl.pallas_call(
        functools.partial(widen, steps, pieces),
        grid=(steps,),
        out_shape=shapes + (line, line),
        in_specs=[cut(t) for t in moved] + [cut(t) for t in weights] + [whole(gains)],
        out_specs=tuple([cut(t) for t in shapes] + [whole(line)] * 2),
        scratch_shapes=[pltpu.VMEM((own, 2), F32)],
        compiler_params=pltpu.CompilerParams(vmem_limit_bytes=64000 * 1024),
        name="widen",
    )(*moved, *weights, gains)
    return tuple(done[:10]) + (done[10].reshape(own), done[11].reshape(own))


def solution(mesh):
    act = P("stream", "tm", None)
    row = P("stream", None)
    in_specs = (act, act, act, P("stream"), row) + (row,) * 6 + (
        P(None, "stream", None),
        P("stream"),
        P("stream"),
        act,
        act,
    )
    out_specs = (act, act, act) + (row,) * 6 + (
        P(None, "stream", None),
        P("stream"),
        P("stream"),
    )
    return jax.shard_map(
        per_device, mesh=mesh, in_specs=in_specs, out_specs=out_specs, check_vma=False
    )
```
